256 devices in a mesh: gx: 16 (over y, x), gy: 16 (over z, core).
Axes of the slice: x: 4, y: 4, z: 8, core: 2. Of those that a mesh axis runs over, the one named last changes fastest.
Arguments:
- points: float32 [64, 128, 3, 256], P('gx', 'gy'), may hold values from 0 to 128, as said below
- right_sides: float32 [64, 128, 4, 256], P('gx', 'gy'), may hold values from -6 to 6
- leaf_counts: int32 [64, 128], P('gx', 'gy'), may hold values from 128 to 256, as said below
- near_mask: int32 [64, 128, 9], P('gx', 'gy'), may hold values from 0 to 1, as said below
- leaf_basis: float32 [64, 128, 64, 256], P('gx', 'gy'), may hold values from -0.375 to 0.375
- leaf_transfer: float32 [64, 128, 64, 64], P('gx', 'gy'), may hold values from -0.75 to 0.75
- upper_transfer: float32 [2, 64, 64], replicated, may hold values from -0.75 to 0.75
- proxy_nodes: float32 [3, 64], replicated, may hold values from -1 to 1
Outputs:
- solution: float32 [64, 128, 4, 256], P('gx', 'gy')
- residual: float32 [64, 128, 4, 256], P('gx', 'gy')
The draws below stay inside these ranges and needn't reach their ends.
Inputs may be any that keep to these rules, and one draw needn't show every extreme that they name: Coordinates of the points of leaf (a, b): the first lies in [a, a + 1), the second in [b, b + 1), the third in [0, 1). `leaf_counts`: the first leaf of every tile of 4 x 8 leaves is full. `near_mask`: entry 3 i + j is 1 where leaf (a + i - 1, b + j - 1) lies in the near field of leaf (a, b); the entry of the leaf itself is 1, entries of leaves outside the grid are 0, and the relation is symmetric.
All inputs are finite; a program needn't handle non-finite values.
Results may differ from the reference program's by a relative error of at most 0.0003.
Values sent between devices are 32-bit elements; how exact they have to be, the bound alone decides.
No kernel may reach another device: no remote copies, remote signals or barrier semaphores. Data moves between devices by JAX's collectives and lax.ppermute only.
A program may use at most 128 MiB of HBM per device.

```python
import jax
import jax.numpy as jnp
from jax import lax

P_SIZE = 256
K = 64
R = 4
ITERS = 2
TX = 4
TY = 8
NLX = 64
NLY = 128
N_GX = 16
N_GY = 16


def draw_points(key, part):
    key = jax.random.fold_in(key, 11)
    jitter = jax.random.uniform(key, (NLX, NLY, 3, P_SIZE), jnp.float32)
    first_base = jnp.broadcast_to(jnp.arange(NLX, dtype=jnp.float32)[:, None], (NLX, NLY))
    second_base = jnp.broadcast_to(jnp.arange(NLY, dtype=jnp.float32)[None, :], (NLX, NLY))
    third_base = jnp.zeros((NLX, NLY), jnp.float32)
    base_corner = jnp.stack([first_base, second_base, third_base], axis=2)
    return base_corner[:, :, :, None] + jitter


def draw_leaf_counts(key, part):
    key = jax.random.fold_in(key, 12)
    counts_drawn = jax.random.randint(key, (NLX, NLY), P_SIZE // 2, P_SIZE + 1)
    first_leaf = (jnp.arange(NLX) % TX == 0)[:, None] & (jnp.arange(NLY) % TY == 0)[None, :]
    return jnp.where(first_leaf, P_SIZE, counts_drawn).astype(jnp.int32)


def draw_near_mask(key, part):
    key = jax.random.fold_in(key, 13)
    edge_bits = jax.random.randint(key, (4, NLX, NLY), 0, 2)
    row_grid = jnp.arange(NLX)[:, None]
    col_grid = jnp.arange(NLY)[None, :]
    planes = [jnp.zeros((NLX, NLY), jnp.int32) for offset_code in range(9)]
    planes[4] = jnp.ones((NLX, NLY), jnp.int32)
    for half_code, (step_row, step_col) in enumerate(((1, 0), (0, 1), (1, 1), (1, -1))):
        inside_ahead = (row_grid + step_row >= 0) & (row_grid + step_row < NLX) & (col_grid + step_col >= 0) & (col_grid + step_col < NLY)
        forward = jnp.where(inside_ahead, edge_bits[half_code], 0)
        planes[(step_row + 1) * 3 + (step_col + 1)] = forward
        inside_behind = (row_grid - step_row >= 0) & (row_grid - step_row < NLX) & (col_grid - step_col >= 0) & (col_grid - step_col < NLY)
        backward = jnp.roll(forward, (step_row, step_col), axis=(0, 1))
        planes[(1 - step_row) * 3 + (1 - step_col)] = jnp.where(inside_behind, backward, 0)
    return jnp.stack(planes, axis=2).astype(jnp.int32)


def block_levels(rng, shape, shards, smallest, largest):
    def one(dim, parts):
        draws = jax.random.uniform(jax.random.fold_in(jax.random.fold_in(rng, 6), dim), (parts,), jnp.float32, smallest / len(shards), largest / len(shards))
        return jnp.repeat(jnp.exp(draws), shape[dim] // parts).reshape((-1,) + (1,) * (len(shape) - dim - 1))

    level = one(*shards[0])
    for cut in shards[1:]:
        level = level * one(*cut)
    return level


def scatter_about(rng, dims, scale, reach, cuts=(), held_as=jnp.bfloat16):
    drawn = scale * jax.random.normal(rng, dims, jnp.float32)
    if cuts:
        drawn = drawn * block_levels(rng, dims, cuts, -0.22, 0.18)
    return jnp.clip(drawn, -reach, reach).astype(held_as)


def setup_inputs(seed: int = 0) -> dict:
    splits = jax.random.split(jax.random.key(seed), 9)
    points = draw_points(jax.random.fold_in(splits[8], 71), 0)
    right_sides = scatter_about(splits[1], (NLX, NLY, R, P_SIZE), 1.0, 6.0, ((0, 16), (1, 16)), jnp.float32)
    leaf_counts = draw_leaf_counts(jax.random.fold_in(splits[8], 71), 0)
    near_mask = draw_near_mask(jax.random.fold_in(splits[8], 71), 0)
    leaf_basis = scatter_about(splits[4], (NLX, NLY, K, P_SIZE), P_SIZE ** -0.5, 0.375, ((0, 16), (1, 16)), jnp.float32)
    leaf_transfer = scatter_about(splits[5], (NLX, NLY, K, K), K ** -0.5, 0.75, ((0, 16), (1, 16)), jnp.float32)
    upper_transfer = scatter_about(splits[6], (2, K, K), K ** -0.5, 0.75, (), jnp.float32)
    proxy_nodes = jnp.clip(jax.random.uniform(splits[7], (3, K), jnp.float32, -1.0, 1.0), -1.0, 1.0)
    return dict(points=points, right_sides=right_sides, leaf_counts=leaf_counts, near_mask=near_mask, leaf_basis=leaf_basis, leaf_transfer=leaf_transfer, upper_transfer=upper_transfer, proxy_nodes=proxy_nodes)


PRECISE = lax.Precision.HIGHEST
NEAR_LENGTH = 0.5
FAR_LENGTH = 16.0
NOISE_LEVEL = 1.0
COUPLING_SCALE = 1.0 / 128.0

def matern(squared, length_value):
    scaled = jnp.sqrt(3.0 * squared) / length_value
    return (1.0 + scaled) * jnp.exp(-scaled)

def kernel_block(target, source):
    squared = (target[..., 0, :, None] - source[..., 0, None, :]) ** 2
    squared = squared + (target[..., 1, :, None] - source[..., 1, None, :]) ** 2
    squared = squared + (target[..., 2, :, None] - source[..., 2, None, :]) ** 2
    return matern(squared, NEAR_LENGTH)

def cluster_nodes(cluster_index, span_width, anchors, tile_rows, tile_cols, count_cols):
    first_device = cluster_index * span_width
    if span_width <= count_cols:
        extent_rows = 1
        extent_cols = span_width
    else:
        extent_rows = span_width // count_cols
        extent_cols = count_cols
    start_row = (first_device // count_cols).astype(jnp.float32)
    start_col = (first_device % count_cols).astype(jnp.float32)
    centre_first = tile_rows * (start_row + 0.5 * extent_rows)
    centre_second = tile_cols * (start_col + 0.5 * extent_cols)
    spots_first = centre_first[..., None] + 0.5 * tile_rows * extent_rows * anchors[0]
    spots_second = centre_second[..., None] + 0.5 * tile_cols * extent_cols * anchors[1]
    spots_third = 0.5 + 0.5 * anchors[2] + 0.0 * spots_first
    return (spots_first, spots_second, spots_third)

def coupling_matrix(target_spots, source_spots):
    squared = (target_spots[0][..., :, None] - source_spots[0][..., None, :]) ** 2
    squared = squared + (target_spots[1][..., :, None] - source_spots[1][..., None, :]) ** 2
    squared = squared + (target_spots[2][..., :, None] - source_spots[2][..., None, :]) ** 2
    return COUPLING_SCALE * matern(squared, FAR_LENGTH)

def tree_far_terms(device_coef, upper_transfer, anchors, tile_rows, tile_cols, count_cols):
    total_devices = device_coef.shape[0]
    levels_count = total_devices.bit_length() - 1
    current = device_coef
    far_terms = []
    for level_index in range(levels_count - 1):
        span_width = 2 ** level_index
        clusters = total_devices // span_width
        cluster_index = jnp.arange(clusters, dtype=jnp.int32)
        partner_index = cluster_index + 2 - 4 * (cluster_index // 2 % 2)
        partner_coef = jnp.take(current, partner_index, axis=0)
        coupling = coupling_matrix(cluster_nodes(cluster_index, span_width, anchors, tile_rows, tile_cols, count_cols), cluster_nodes(partner_index, span_width, anchors, tile_rows, tile_cols, count_cols))
        far_terms.append(jnp.einsum('nrb,nab->nra', partner_coef, coupling, precision=PRECISE))
        if level_index + 2 < levels_count:
            paired = current.reshape(clusters // 2, 2, current.shape[1], current.shape[2])
            current = jnp.einsum('nrk,jk->nrj', paired[:, 0], upper_transfer[0], precision=PRECISE) + jnp.einsum('nrk,jk->nrj', paired[:, 1], upper_transfer[1], precision=PRECISE)
    return far_terms

def solve_small(matrix, right_block):
    order_size = matrix.shape[0]
    row_list = [matrix[position] for position in range(order_size)]
    rhs_list = [right_block[position] for position in range(order_size)]
    for column in range(order_size):
        pivot = row_list[column][column]
        for lower_row in range(column + 1, order_size):
            factor = row_list[lower_row][column] / pivot
            row_list[lower_row] = row_list[lower_row] - factor * row_list[column]
            rhs_list[lower_row] = rhs_list[lower_row] - factor * rhs_list[column]
    result = [rhs_list[0]] * order_size
    for column in reversed(range(order_size)):
        partial_sum = rhs_list[column]
        for later_row in range(column + 1, order_size):
            partial_sum = partial_sum - row_list[column][later_row] * result[later_row]
        result[column] = partial_sum / row_list[column][column]
    return jnp.stack(result)

def near_field(vector, points, near_mask):
    padded_points = jnp.pad(points, ((1, 1), (1, 1), (0, 0), (0, 0)))
    padded_vector = jnp.pad(vector, ((1, 1), (1, 1), (0, 0), (0, 0)))
    cols_all = points.shape[1]

    def one_row(row_index):
        target = lax.dynamic_index_in_dim(points, row_index, 0, keepdims=False)
        mask_row = lax.dynamic_index_in_dim(near_mask, row_index, 0, keepdims=False).astype(jnp.float32)
        accumulated = jnp.zeros((cols_all, vector.shape[2], vector.shape[3]), jnp.float32)
        for offset_code in range(9):
            shift_row = offset_code // 3
            shift_col = offset_code % 3
            source = lax.dynamic_index_in_dim(padded_points, row_index + shift_row, 0, keepdims=False)[shift_col:shift_col + cols_all]
            values = lax.dynamic_index_in_dim(padded_vector, row_index + shift_row, 0, keepdims=False)[shift_col:shift_col + cols_all]
            kernel_tile = kernel_block(target, source)
            contribution = jnp.einsum('bpq,brq->brp', kernel_tile, values, precision=PRECISE)
            accumulated = accumulated + mask_row[:, offset_code][:, None, None] * contribution
        return accumulated
    return lax.map(one_row, jnp.arange(points.shape[0], dtype=jnp.int32))

def far_field(vector, leaf_basis, leaf_transfer, upper_transfer, proxy_nodes):
    leaf_coef_up = jnp.einsum('abrp,abkp->abrk', vector, leaf_basis, precision=PRECISE)
    grouped = leaf_coef_up.reshape(N_GX, TX, N_GY, TY, R, K)
    transfer = leaf_transfer.reshape(N_GX, TX, N_GY, TY, K, K)
    device_coef = jnp.einsum('xaybrk,xaybjk->xyrj', grouped, transfer, precision=PRECISE).reshape(N_GX * N_GY, R, K)
    far_terms = tree_far_terms(device_coef, upper_transfer, proxy_nodes, TX, TY, N_GY)
    downward = far_terms[-1]
    for level_index in reversed(range(len(far_terms) - 1)):
        lower_half = jnp.einsum('nrj,jk->nrk', downward, upper_transfer[0], precision=PRECISE)
        higher = jnp.einsum('nrj,jk->nrk', downward, upper_transfer[1], precision=PRECISE)
        downward = far_terms[level_index] + jnp.stack([lower_half, higher], axis=1).reshape(-1, R, K)
    downward = downward.reshape(N_GX, N_GY, R, K)
    leaf_coef_down = jnp.einsum('xyrj,xaybjk->xaybrk', downward, transfer, precision=PRECISE).reshape(NLX, NLY, R, K)
    return jnp.einsum('abrk,abkp->abrp', leaf_coef_down, leaf_basis, precision=PRECISE)

def reference(points, right_sides, leaf_counts, near_mask, leaf_basis, leaf_transfer, upper_transfer, proxy_nodes):
    valid_mask = (jnp.arange(P_SIZE, dtype=jnp.int32)[None, None, :] < leaf_counts[:, :, None]).astype(jnp.float32)[:, :, None, :]
    near_scale = 1.0 / P_SIZE ** 0.5

    def apply_operator(vector):
        local_part = NOISE_LEVEL * vector + near_scale * near_field(vector, points, near_mask)
        return valid_mask * (local_part + far_field(vector, leaf_basis, leaf_transfer, upper_transfer, proxy_nodes))

    def gram_of(left, right_block):
        return jnp.einsum('abrp,absp->rs', left, right_block, precision=PRECISE)
    solution = jnp.zeros_like(right_sides)
    residual = valid_mask * right_sides
    direction = residual
    gram_now = gram_of(residual, residual)
    for step_index in range(ITERS):
        applied = apply_operator(direction)
        curvature = gram_of(direction, applied)
        step_weights = solve_small(curvature, gram_now)
        solution = solution + jnp.einsum('absp,sr->abrp', direction, step_weights, precision=PRECISE)
        residual = residual - jnp.einsum('absp,sr->abrp', applied, step_weights, precision=PRECISE)
        if step_index + 1 < ITERS:
            gram_next = gram_of(residual, residual)
            mix_weights = solve_small(gram_now, gram_next)
            direction = residual + jnp.einsum('absp,sr->abrp', direction, mix_weights, precision=PRECISE)
            gram_now = gram_next
    return (solution, residual)
```

```python
import functools

import jax
import jax.numpy as jnp
import numpy as np
from jax import lax
from jax.experimental import pallas as pl
from jax.experimental.pallas import tpu as pltpu
from jax.sharding import PartitionSpec as P

F32 = jnp.float32
BF = jnp.bfloat16
NEAR_LENGTH = 0.5
FAR_LENGTH = 16.0
NEAR_RATE = 3.0**0.5 / NEAR_LENGTH
FAR_RATE = 3.0**0.5 / FAR_LENGTH
LOG2E = 1.4426950408889634
COUPLING_SCALE = 1.0 / 128.0
UNROLL = 8
CHUNK = 64
VMEM_LIMIT = 48 * 2**20
VM = pl.BlockSpec(memory_space=pltpu.VMEM)
SM = pl.BlockSpec(memory_space=pltpu.SMEM)


def rounded(x):
    return x.astype(BF).astype(F32)


def split2(x):
    high = x.astype(BF)
    return high, (x - high.astype(F32)).astype(BF)


def rows16(x):
    first = rounded(x)
    second = rounded(x - first)
    third = rounded(x - first - second)
    return jnp.concatenate([first, second, third, jnp.zeros_like(x)], axis=0).astype(BF)


def join16(y):
    return y[0:4] + y[4:8] + y[8:12]


def dot(a, b):
    return jnp.dot(a, b, preferred_element_type=F32)


def dot_nt(a, b):
    return lax.dot_general(a, b, (((1,), (1,)), ((), ())), preferred_element_type=F32)


def dot3(a, b):
    a_high, a_low = split2(a)
    b_high, b_low = split2(b)
    return dot(a_high, b_high) + (dot(a_low, b_high) + dot(a_high, b_low))


def feature_tables():
    target = np.zeros((32, 24), np.float32)
    source = np.zeros((32, 24), np.float32)
    factor = np.ones((9, 32), np.float32)
    one = 19
    for c in range(3):
        target[2 * c, c] = target[2 * c + 1, c] = -2
        source[2 * c, c] = source[2 * c + 1, 8 + c] = 1
        target[6 + 2 * c, 8 + c] = target[7 + 2 * c, 8 + c] = -2
        source[6 + 2 * c, c] = source[7 + 2 * c, 8 + c] = 1
    for k in range(3):
        target[12 + k, one] = source[12 + k, 16 + k] = 1
        target[15 + k, 16 + k] = source[15 + k, one] = 1
    for c in range(2):
        target[18 + 2 * c, c] = target[19 + 2 * c, 8 + c] = 1
        source[18 + 2 * c, one] = source[19 + 2 * c, one] = 1
        target[22 + 2 * c, one] = target[23 + 2 * c, one] = 1
        source[22 + 2 * c, c] = source[23 + 2 * c, 8 + c] = 1
    target[26, one] = source[26, one] = 1
    for code in range(9):
        off = (code // 3 - 1, code % 3 - 1)
        for c in range(2):
            factor[code, 18 + 2 * c : 20 + 2 * c] = -2 * off[c]
            factor[code, 22 + 2 * c : 24 + 2 * c] = 2 * off[c]
        factor[code, 26] = off[0] ** 2 + off[1] ** 2
    return target, source, factor


def geometry_kernel(x_ref, target_ref, source_ref, s_ref, t_ref):
    row = lax.broadcasted_iota(jnp.int32, (8, x_ref.shape[2]), 0)

    def body(e, carry):
        x = jnp.where(row < 3, x_ref[e], 0.0)
        first = rounded(x)
        second = rounded(x - first)
        held = first + second
        norm = jnp.sum(held * held, axis=0, keepdims=True)
        n1 = rounded(norm)
        n2 = rounded(norm - n1)
        n3 = rounded(norm - n1 - n2)
        last = jnp.where(row == 0, n1, jnp.where(row == 1, n2, jnp.where(row == 2, n3, jnp.where(row == 3, 1.0, 0.0))))
        f = jnp.concatenate([first, second, last], axis=0).astype(BF)
        t_ref[e] = dot(target_ref[...], f).astype(BF)
        s_ref[e] = lax.dot_general(
            f, source_ref[...], (((0,), (1,)), ((), ())), preferred_element_type=F32
        ).astype(BF)
        return carry

    lax.fori_loop(0, x_ref.shape[0], body, 0, unroll=4)


def geometry(x, target_table, source_table):
    leaves, _, size = x.shape
    return pl.pallas_call(
        geometry_kernel,
        out_shape=[
            jax.ShapeDtypeStruct((leaves, size, 32), BF),
            jax.ShapeDtypeStruct((leaves, 32, size), BF),
        ],
        in_specs=[VM] * 3,
        out_specs=[VM] * 2,
        compiler_params=pltpu.CompilerParams(vmem_limit_bytes=VMEM_LIMIT),
        name="geometry",
    )(x, jnp.asarray(target_table, BF), jnp.asarray(source_table, BF))


def near_kernel(nx, ny, mask_ref, v_ref, s_ref, t_ref, factor_ref, o_ref, v16, acc, todo):
    wide = ny + 2
    leaves = (nx + 2) * wide
    size = v_ref.shape[2]

    def split_leaf(e, carry):
        v16[e] = rows16(v_ref[e])
        return carry

    lax.fori_loop(0, leaves, split_leaf, 0, unroll=4)
    v16[leaves] = jnp.zeros((16, size), BF)
    acc[...] = jnp.zeros_like(acc)

    def note(i, count):
        todo[count] = i
        return count + jnp.where(mask_ref[i] != 0, 1, 0)

    count = lax.fori_loop(0, nx * ny * 9, note, 0, unroll=8)
    for j in range(UNROLL):
        todo[count + j] = -1

    def one_pair(i):
        entry = todo[i]
        pair = jnp.maximum(entry, 0)
        a = pair // 9
        code = pair - a * 9
        row = a // ny
        col = a - row * ny
        code_row = code // 3
        code_col = code - code_row * 3
        source = (row + code_row) * wide + col + code_col
        t = t_ref[(row + 1) * wide + col + 1] * factor_ref[code]
        s = s_ref[source]
        v = v16[jnp.where(entry < 0, leaves, source)]
        total = jnp.zeros((16, size), F32)
        for k in range(size // CHUNK):
            part = slice(k * CHUNK, (k + 1) * CHUNK)
            squared = jnp.maximum(dot(s[part], t), 1e-30)
            distance = squared * lax.rsqrt(squared)
            value = (1.0 + NEAR_RATE * distance) * jnp.exp2((-NEAR_RATE * LOG2E) * distance)
            high, low = split2(value)
            total += dot(v[:, part], high) + dot(v[:, part], low)
        return a, total

    def group(g, carry):
        for a, total in [one_pair(g * UNROLL + j) for j in range(UNROLL)]:
            acc[a] += total
        return carry

    lax.fori_loop(0, (count + UNROLL - 1) // UNROLL, group, 0)

    def finish(a, carry):
        o_ref[a] = join16(acc[a]) * (1.0 / size**0.5)
        return carry

    lax.fori_loop(0, nx * ny, finish, 0, unroll=4)


def near_field(nx, ny, mask, v, s, t, factor):
    leaves, _, size = v.shape
    return pl.pallas_call(
        functools.partial(near_kernel, nx, ny),
        out_shape=jax.ShapeDtypeStruct((nx * ny, 4, size), F32),
        in_specs=[SM, VM, VM, VM, VM],
        out_specs=VM,
        scratch_shapes=[
            pltpu.VMEM((leaves + 1, 16, size), BF),
            pltpu.VMEM((nx * ny, 16, size), F32),
            pltpu.SMEM((nx * ny * 9 + UNROLL,), jnp.int32),
        ],
        compiler_params=pltpu.CompilerParams(vmem_limit_bytes=VMEM_LIMIT),
        name="near",
    )(mask, v, s, t, factor)


def upward_kernel(r_ref, basis_ref, transfer_ref, high_ref, low_ref, c_ref):
    leaves = r_ref.shape[0]

    def body(a, total):
        b_high, b_low = split2(basis_ref[a])
        t_high, t_low = split2(transfer_ref[a])
        joint = dot(t_high, b_high) + (dot(t_low, b_high) + dot(t_high, b_low))
        high, low = split2(joint)
        high_ref[a] = high
        low_ref[a] = low
        v = rows16(r_ref[a])
        return total + (dot_nt(v, high) + dot_nt(v, low))

    total = lax.fori_loop(0, leaves, body, jnp.zeros((16, 64), F32), unroll=4)
    c_ref[...] = jnp.concatenate([join16(total), jnp.zeros((4, 64), F32)], axis=0)


def upward(r, basis, transfer):
    leaves, _, size = r.shape
    terms = basis.shape[1]
    joint = jax.ShapeDtypeStruct((leaves, terms, size), BF)
    return pl.pallas_call(
        upward_kernel,
        out_shape=[joint, joint, jax.ShapeDtypeStruct((8, terms), F32)],
        in_specs=[VM] * 3,
        out_specs=[VM] * 3,
        compiler_params=pltpu.CompilerParams(vmem_limit_bytes=VMEM_LIMIT),
        name="upward",
    )(r, basis, transfer)


def coupling_kernel(levels, cols, tile, place_ref, upper_ref, row_ref, col_ref, b_ref, g_ref):
    place = place_ref[0]
    down = None
    for level in range(levels):
        span = 2**level
        extent = (1, span) if span <= cols else (span // cols, cols)
        half = (0.5 * tile[0] * extent[0], 0.5 * tile[1] * extent[1], 0.5)
        apart = (0.0, 2.0 * span * tile[1]) if 2 * span < cols else (2.0 * span / cols * tile[0], 0.0)

        def matrix(sign):
            squared = jnp.zeros((64, 64), F32)
            for c in range(3):
                step = half[c] * (col_ref[:, c : c + 1] - row_ref[c : c + 1, :])
                if c < 2:
                    step = step + sign * apart[c]
                squared = squared + step * step
            squared = jnp.maximum(squared, 1e-30)
            scaled = FAR_RATE * (squared * lax.rsqrt(squared))
            return COUPLING_SCALE * ((1.0 + scaled) * jnp.exp(-scaled))

        b_ref[level] = matrix(-1.0)
        upper = (place // (2 * span)) % 2
        own = matrix(jnp.where(upper == 1, -1.0, 1.0))
        g_ref[level] = own if down is None else dot3(own, down)
        if level + 1 < levels:
            bit = (place // span) % 2
            step_down = upper_ref[bit]
            down = step_down if down is None else dot3(step_down, down)


def couplings(levels, cols, tile, place, upper, nodes):
    out = jax.ShapeDtypeStruct((levels, 64, 64), F32)
    return pl.pallas_call(
        functools.partial(coupling_kernel, levels, cols, tile),
        out_shape=[out, out],
        in_specs=[SM, VM, VM, VM],
        out_specs=[VM, VM],
        name="couplings",
    )(place, upper, nodes, nodes.T)


def tree(levels, place, c, upper_t, g_ref, b_ref, scratch, energy):
    own = jnp.zeros((8, 64), F32)
    pair_sums = [jnp.zeros((8, 64), F32) for _ in range(4)]
    for level in range(levels):
        count = c.shape[0]
        scratch[0:count] = c
        partner = (place // 2**level) ^ 2
        own = own + dot3(scratch[partner], g_ref[level])
        paired = c.reshape(count // 2, 2, 8, 64)
        if energy:
            quads = c.reshape(count // 4, 4, 8, 64)
            low = quads[:, 0:2].reshape(count // 2 * 8, 64)
            high = quads[:, 2:4].reshape(count // 2, 8, 64)
            carried = dot3(low, b_ref[level]).reshape(count // 2, 8, 64)
            for s in range(4):
                pair_sums[s] = pair_sums[s] + jnp.sum(carried * high[:, s : s + 1, :], axis=0)
        if level + 1 < levels:
            c = (
                dot3(paired[:, 0].reshape(count // 2 * 8, 64), upper_t[0])
                + dot3(paired[:, 1].reshape(count // 2 * 8, 64), upper_t[1])
            ).reshape(count // 2, 8, 64)
    return own[0:4], pair_sums


def middle_kernel(
    levels, place_ref, count_ref, c_ref, upper_ref, g_ref, high_ref, low_ref, r_ref, n_ref, e_ref, out_ref, scratch
):
    leaves, _, size = r_ref.shape
    own, _ = tree(levels, place_ref[0], c_ref[...], upper_ref, g_ref, None, scratch, False)
    y = rows16(own)
    lane = lax.broadcasted_iota(jnp.int32, (4, size), 1)

    def body(a, carry):
        c_total, m_total = carry
        high = high_ref[a]
        low = low_ref[a]
        far = join16(dot(y, high) + dot(y, low))
        e = jnp.where(lane < count_ref[a], n_ref[a] + far, 0.0)
        e_ref[a] = e
        e16 = rows16(e)
        both = jnp.concatenate([rows16(r_ref[a]), e16], axis=0)
        return c_total + (dot_nt(e16, high) + dot_nt(e16, low)), m_total + dot_nt(both, both)

    c_total, m_total = lax.fori_loop(
        0, leaves, body, (jnp.zeros((16, 64), F32), jnp.zeros((32, 32), F32)), unroll=4
    )

    def block(i, j):
        part = m_total[16 * i : 16 * i + 16, 16 * j : 16 * j + 16]
        part = join16(part)
        return part[:, 0:4] + part[:, 4:8] + part[:, 8:12]

    moments = jnp.concatenate([block(0, 0), block(0, 1), block(1, 1), jnp.zeros((4, 52), F32)], axis=1)
    out_ref[...] = jnp.concatenate([join16(c_total), moments], axis=0)


def middle(levels, place, counts, c, upper_t, g, high, low, r, n):
    return pl.pallas_call(
        functools.partial(middle_kernel, levels),
        out_shape=[jax.ShapeDtypeStruct(r.shape, F32), jax.ShapeDtypeStruct((8, 64), F32)],
        in_specs=[SM, SM] + [VM] * 7,
        out_specs=[VM] * 2,
        scratch_shapes=[pltpu.VMEM(c.shape, F32)],
        compiler_params=pltpu.CompilerParams(vmem_limit_bytes=VMEM_LIMIT),
        name="middle",
    )(place, counts, c, upper_t, g, high, low, r, n)


def energy_kernel(e_ref, n_ref, c_ref, out_ref):
    leaves = e_ref.shape[0]
    sums = []
    for s in range(4):
        total = jnp.zeros(e_ref.shape[1:], F32)
        for a in range(leaves):
            total = total + e_ref[a] * n_ref[a, s : s + 1, :]
        sums.append(jnp.sum(total, axis=1, keepdims=True))
    block = jnp.concatenate([jnp.zeros((4, 12), F32)] + sums + [jnp.zeros((4, 48), F32)], axis=1)
    out_ref[...] = c_ref[...] + jnp.concatenate([jnp.zeros((4, 64), F32), block], axis=0)


def energy(e, n, c):
    return pl.pallas_call(
        energy_kernel,
        out_shape=jax.ShapeDtypeStruct((8, 64), F32),
        in_specs=[VM] * 3,
        out_specs=VM,
        name="energy",
    )(e, n, c)


def mat_mul(a, b):
    return [[sum(a[i][k] * b[k][j] for k in range(4)) for j in range(4)] for i in range(4)]


def mat_add(a, b):
    return [[a[i][j] + b[i][j] for j in range(4)] for i in range(4)]


def mat_sub(a, b):
    return [[a[i][j] - b[i][j] for j in range(4)] for i in range(4)]


def mat_t(a):
    return [[a[j][i] for j in range(4)] for i in range(4)]


def mat_solve(a, b):
    a = [list(row) for row in a]
    b = [list(row) for row in b]
    width = len(b[0])
    inverse = []
    for col in range(4):
        inverse.append(1.0 / a[col][col])
        for row in range(col + 1, 4):
            factor = a[row][col] * inverse[col]
            for k in range(col + 1, 4):
                a[row][k] = a[row][k] - factor * a[col][k]
            for k in range(width):
                b[row][k] = b[row][k] - factor * b[col][k]
    result = [None] * 4
    for col in reversed(range(4)):
        row = list(b[col])
        for later in range(col + 1, 4):
            row = [row[k] - a[col][later] * result[later][k] for k in range(width)]
        result[col] = [value * inverse[col] for value in row]
    return result


def weights(gram, cross, square, cubic):
    curvature = mat_add(gram, cross)
    both = mat_solve(curvature, [gram[i] + cross[i] for i in range(4)])
    step = [row[0:4] for row in both]
    rest = [row[4:8] for row in both]
    mixed = mat_mul(mat_t(rest), mat_mul(cross, step))
    gram_next = mat_sub(
        mat_add(mat_mul(mat_t(rest), mat_mul(gram, rest)), mat_mul(mat_t(step), mat_mul(square, step))),
        mat_add(mixed, mat_t(mixed)),
    )
    mix = mat_solve(gram, gram_next)
    lead = mat_add(rest, mix)
    second = mat_sub(lead, step)
    with_r = mat_sub(mat_add(mat_mul(gram, lead), mat_mul(cross, second)), mat_mul(square, step))
    with_e = mat_sub(mat_add(mat_mul(mat_t(cross), lead), mat_mul(square, second)), mat_mul(cubic, step))
    curvature_next = mat_sub(mat_mul(mat_t(lead), with_r), mat_mul(mat_t(step), with_e))
    step_next = mat_solve(curvature_next, gram_next)
    lead_step = mat_mul(lead, step_next)
    step_step = mat_mul(step, step_next)
    second_step = mat_sub(lead_step, step_step)
    solution = (mat_add(step, lead_step), [[-v for v in row] for row in step_step], None)
    residual = (mat_sub(rest, lead_step), [[-(step[i][j] + second_step[i][j]) for j in range(4)] for i in range(4)], step_step)
    return solution, residual


def final_kernel(
    levels, place_ref, count_ref, c_ref, upper_ref, g_ref, b_ref, high_ref, low_ref, r_ref, e_ref, n_ref,
    x_ref, out_ref, scratch,
):
    leaves, _, size = r_ref.shape
    c = c_ref[...]
    own, pair_sums = tree(levels, place_ref[0], c, upper_ref, g_ref, b_ref, scratch, True)
    y = rows16(own)
    moments = jnp.sum(c, axis=0)[4:8]

    def splat(x):
        return jnp.broadcast_to(x, (1, 128))

    def matrix(at):
        return [[splat(moments[i : i + 1, at + j : at + j + 1]) for j in range(4)] for i in range(4)]

    half = [[splat(jnp.sum(pair_sums[j], axis=1, keepdims=True)[i : i + 1]) for j in range(4)] for i in range(4)]
    cubic = mat_add(matrix(12), mat_add(half, mat_t(half)))
    solution, residual = weights(matrix(0), matrix(4), matrix(8), cubic)
    row = lax.broadcasted_iota(jnp.int32, (8, 128), 0)
    col = lax.broadcasted_iota(jnp.int32, (8, 128), 1)
    table = jnp.zeros((8, 128), F32)
    for first, parts in ((0, solution), (4, residual)):
        for k, part in enumerate(parts):
            if part is None:
                continue
            for i in range(4):
                line = jnp.zeros((8, 128), F32)
                for j in range(4):
                    line = jnp.where(row == first + j, part[i][j], line)
                table = jnp.where(col == 4 * k + i, line + table, table)
    table = table[:, 0:16]
    lane = lax.broadcasted_iota(jnp.int32, (4, size), 1)

    def body(a, carry):
        far = join16(dot(y, high_ref[a]) + dot(y, low_ref[a]))
        f = jnp.where(lane < count_ref[a], n_ref[a] + far, 0.0)
        stacked = jnp.concatenate([r_ref[a], e_ref[a], f, jnp.zeros_like(f)], axis=0)
        both = jnp.dot(table, stacked, precision=lax.Precision.HIGHEST, preferred_element_type=F32)
        x_ref[a] = both[0:4]
        out_ref[a] = both[4:8]
        return carry

    lax.fori_loop(0, leaves, body, 0, unroll=4)


def final(levels, place, counts, c, upper_t, g, b, high, low, r, e, n):
    out = jax.ShapeDtypeStruct(r.shape, F32)
    return pl.pallas_call(
        functools.partial(final_kernel, levels),
        out_shape=[out, out],
        in_specs=[SM, SM] + [VM] * 9,
        out_specs=[VM] * 2,
        scratch_shapes=[pltpu.VMEM(c.shape, F32)],
        compiler_params=pltpu.CompilerParams(vmem_limit_bytes=VMEM_LIMIT),
        name="final",
    )(place, counts, c, upper_t, g, b, high, low, r, e, n)


def with_halo(x):
    for axis, dim in (("gx", 0), ("gy", 1)):
        count, length = lax.axis_size(axis), x.shape[dim]
        up = [(i, i + 1) for i in range(count - 1)]
        down = [(j, i) for i, j in up]
        before = lax.ppermute(lax.slice_in_dim(x, length - 1, length, axis=dim), axis, up)
        after = lax.ppermute(lax.slice_in_dim(x, 0, 1, axis=dim), axis, down)
        x = jnp.concatenate([before, x, after], axis=dim)
    return x


def from_all(x):
    for axis in ("gy", "gx"):
        count = lax.axis_size(axis)
        x = lax.all_to_all(jnp.broadcast_to(x[None], (count,) + x.shape), axis, 0, 0, tiled=True)
    return x.reshape((-1,) + x.shape[2:])


def on_device(points, right_sides, leaf_counts, near_mask, leaf_basis, leaf_transfer, upper_transfer, proxy_nodes):
    nx, ny, _, size = points.shape
    leaves = nx * ny
    cols = lax.axis_size("gy")
    devices = lax.axis_size("gx") * cols
    levels = devices.bit_length() - 2
    gx, gy = lax.axis_index("gx"), lax.axis_index("gy")
    place = (gx * cols + gy).astype(jnp.int32).reshape(1)
    target_table, source_table, factor = feature_tables()
    factor = jnp.asarray(np.broadcast_to(factor[:, :, None], (9, 32, size)), BF)

    valid = jnp.arange(size, dtype=jnp.int32) < leaf_counts[:, :, None, None]
    r = jnp.where(valid, right_sides, 0.0)
    corner = jnp.stack(
        [
            jnp.broadcast_to((gx * nx + jnp.arange(nx))[:, None], (nx, ny)).astype(F32) + 0.5,
            jnp.broadcast_to((gy * ny + jnp.arange(ny))[None, :], (nx, ny)).astype(F32) + 0.5,
            jnp.full((nx, ny), 0.5, F32),
        ],
        axis=2,
    )
    packed = jnp.concatenate([points - corner[..., None], jnp.zeros((nx, ny, 1, size), F32), r], axis=2)
    extended = with_halo(packed)
    leaves_out = (nx + 2) * (ny + 2)
    s, t = geometry(extended.reshape(leaves_out, 8, size), target_table, source_table)
    flat_r = r.reshape(leaves, 4, size)
    counts = leaf_counts.reshape(leaves)
    mask = near_mask.reshape(leaves * 9)
    high, low, c = upward(
        flat_r, leaf_basis.reshape((leaves,) + leaf_basis.shape[2:]), leaf_transfer.reshape((leaves,) + leaf_transfer.shape[2:])
    )
    upper_t = jnp.swapaxes(upper_transfer, 1, 2)
    b, g = couplings(levels, cols, (nx, ny), place, upper_transfer, proxy_nodes)
    everyone = from_all(c)
    n = near_field(nx, ny, mask, extended[:, :, 4:8].reshape(leaves_out, 4, size), s, t, factor)
    e, c = middle(levels, place, counts, everyone, upper_t, g, high, low, flat_r, n)
    extended_e = with_halo(e.reshape(nx, ny, 4, size)).reshape(leaves_out, 4, size)
    n = near_field(nx, ny, mask, extended_e, s, t, factor)
    everyone = from_all(energy(e, n, c))
    x, out = final(levels, place, counts, everyone, upper_t, g, b, high, low, flat_r, e, n)
    shape = (nx, ny, 4, size)
    return x.reshape(shape), out.reshape(shape)


def solution(mesh):
    return jax.shard_map(
        on_device,
        mesh=mesh,
        in_specs=(
            P("gx", "gy", None, None),
            P("gx", "gy", None, None),
            P("gx", "gy"),
            P("gx", "gy", None),
            P("gx", "gy", None, None),
            P("gx", "gy", None, None),
            P(),
            P(),
        ),
        out_specs=(P("gx", "gy", None, None), P("gx", "gy", None, None)),
        check_vma=False,
    )
```

```python
import functools

import jax
import jax.numpy as jnp
import numpy as np
from jax import lax
from jax.experimental import pallas as pl
from jax.experimental.pallas import tpu as pltpu
from jax.sharding import PartitionSpec as P

F32 = jnp.float32
BF = jnp.bfloat16
NEAR_LENGTH = 0.5
FAR_LENGTH = 16.0
NEAR_RATE = 3.0**0.5 / NEAR_LENGTH
FAR_RATE = 3.0**0.5 / FAR_LENGTH
LOG2E = 1.4426950408889634
COUPLING_SCALE = 1.0 / 128.0
GROUP = 8
CHUNK = 64
BUILD_SLOTS = 2
READ_SLOTS = 4
VMEM_LIMIT = 20 * 2**20
VM = pl.BlockSpec(memory_space=pltpu.VMEM)
ANY = pl.BlockSpec(memory_space=pl.ANY)
SM = pl.BlockSpec(memory_space=pltpu.SMEM)


def rounded(x):
    return x.astype(BF).astype(F32)


def split2(x):
    high = x.astype(BF)
    return high, (x - high.astype(F32)).astype(BF)


def rows16(x):
    first = rounded(x)
    second = rounded(x - first)
    third = rounded(x - first - second)
    return jnp.concatenate([first, second, third, jnp.zeros_like(x)], axis=0).astype(BF)


def join16(y):
    return y[0:4] + y[4:8] + y[8:12]


def dot(a, b):
    return jnp.dot(a, b, preferred_element_type=F32)


def dot_nt(a, b):
    return lax.dot_general(a, b, (((1,), (1,)), ((), ())), preferred_element_type=F32)


def split3(x):
    first = x.astype(BF)
    rest = x - first.astype(F32)
    second = rest.astype(BF)
    return first, second, (rest - second.astype(F32)).astype(BF)


def exact_dot(a, b):
    return jnp.dot(a, b, precision=lax.Precision.HIGHEST, preferred_element_type=F32)


def feature_tables():
    target = np.zeros((32, 24), np.float32)
    source = np.zeros((32, 24), np.float32)
    factor = np.ones((9, 32), np.float32)
    one = 19
    for c in range(3):
        target[2 * c, c] = target[2 * c + 1, c] = -2
        source[2 * c, c] = source[2 * c + 1, 8 + c] = 1
        target[6 + 2 * c, 8 + c] = target[7 + 2 * c, 8 + c] = -2
        source[6 + 2 * c, c] = source[7 + 2 * c, 8 + c] = 1
    for k in range(3):
        target[12 + k, one] = source[12 + k, 16 + k] = 1
        target[15 + k, 16 + k] = source[15 + k, one] = 1
    for c in range(2):
        target[18 + 2 * c, c] = target[19 + 2 * c, 8 + c] = 1
        source[18 + 2 * c, one] = source[19 + 2 * c, one] = 1
        target[22 + 2 * c, one] = target[23 + 2 * c, one] = 1
        source[22 + 2 * c, c] = source[23 + 2 * c, 8 + c] = 1
    target[26, one] = source[26, one] = 1
    for code in range(9):
        off = (code // 3 - 1, code % 3 - 1)
        for c in range(2):
            factor[code, 18 + 2 * c : 20 + 2 * c] = -2 * off[c]
            factor[code, 22 + 2 * c : 24 + 2 * c] = 2 * off[c]
        factor[code, 26] = off[0] ** 2 + off[1] ** 2
    return target, source, factor


def params():
    return pltpu.CompilerParams(vmem_limit_bytes=VMEM_LIMIT)


def around(nx, ny):
    wide = ny + 2
    return (
        (nx * ny, lambda i: (i // ny + 1) * wide + i % ny + 1),
        (ny, lambda i: i + 1),
        (ny, lambda i: (nx + 1) * wide + i + 1),
        (nx + 2, lambda i: i * wide),
        (nx + 2, lambda i: i * wide + wide - 1),
    )


def each_leaf(nx, ny, refs, body, unroll=4):
    for ref, (count, place) in zip(refs, around(nx, ny)):

        def step(i, carry, ref=ref, place=place):
            body(place(i), ref, i)
            return carry

        lax.fori_loop(0, count, step, 0, unroll=unroll if count % unroll == 0 else 2)


def pack_kernel(nx, ny, count_ref, points_ref, sides_ref, packed_ref, top_ref, bottom_ref, r_ref, valid_ref):
    size = points_ref.shape[2]
    row = lax.broadcasted_iota(jnp.int32, (3, size), 0)
    lane = lax.broadcasted_iota(jnp.int32, (1, size), 1)

    def body(a, carry):
        first = (lax.axis_index("gx") * nx + a // ny).astype(F32) + 0.5
        second = (lax.axis_index("gy") * ny + a % ny).astype(F32) + 0.5
        packed_ref[a, 0:3] = points_ref[a] - jnp.where(row == 0, first, jnp.where(row == 1, second, 0.5))
        count = count_ref[a // ny, a % ny]
        packed_ref[a, 3:4] = jnp.full((1, size), count.astype(F32))
        valid = jnp.where(lane < count, 1.0, 0.0)
        r = jnp.where(valid > 0.0, sides_ref[a], 0.0)
        packed_ref[a, 4:8] = r
        part = pl.ds(pl.multiple_of(a * size, size), size)
        r_ref[:, part] = r
        valid_ref[:, part] = valid
        return carry

    lax.fori_loop(0, nx * ny, body, 0, unroll=4)
    top_ref[...] = packed_ref[0:ny]
    bottom_ref[...] = packed_ref[(nx - 1) * ny : nx * ny]


def pack(nx, ny, counts, points, sides):
    leaves, _, size = points.shape
    return pl.pallas_call(
        functools.partial(pack_kernel, nx, ny),
        out_shape=[
            jax.ShapeDtypeStruct((leaves, 8, size), F32),
            jax.ShapeDtypeStruct((ny, 8, size), F32),
            jax.ShapeDtypeStruct((ny, 8, size), F32),
            jax.ShapeDtypeStruct((4, leaves * size), F32),
            jax.ShapeDtypeStruct((1, leaves * size), F32),
        ],
        in_specs=[SM, VM, VM],
        out_specs=[VM] * 5,
        compiler_params=params(),
        name="pack",
    )(counts, points, sides)


def sides_kernel(nx, ny, own_ref, up_ref, down_ref, left_ref, right_ref):
    for col, ref in ((0, left_ref), (ny - 1, right_ref)):
        ref[0] = up_ref[col]
        ref[nx + 1] = down_ref[col]
        for i in range(nx):
            ref[i + 1] = own_ref[i * ny + col]


def side_columns(nx, ny, own, up, down):
    out = jax.ShapeDtypeStruct((nx + 2,) + own.shape[1:], F32)
    return pl.pallas_call(
        functools.partial(sides_kernel, nx, ny),
        out_shape=[out, out],
        in_specs=[VM] * 3,
        out_specs=[VM] * 2,
        compiler_params=params(),
        name="side_columns",
    )(own, up, down)


def geometry_kernel(nx, ny, own_ref, up_ref, down_ref, left_ref, right_ref, target_ref, source_ref, s_ref, t_ref):
    row = lax.broadcasted_iota(jnp.int32, (8, own_ref.shape[2]), 0)

    def body(e, ref, i):
        x = jnp.where(row < 3, ref[i], 0.0)
        first = rounded(x)
        second = rounded(x - first)
        held = first + second
        norm = jnp.sum(held * held, axis=0, keepdims=True)
        n1 = rounded(norm)
        n2 = rounded(norm - n1)
        n3 = rounded(norm - n1 - n2)
        last = jnp.where(row == 0, n1, jnp.where(row == 1, n2, jnp.where(row == 2, n3, jnp.where(row == 3, 1.0, 0.0))))
        f = jnp.concatenate([first, second, last], axis=0).astype(BF)
        t_ref[e] = dot(target_ref[...], f).astype(BF)
        s_ref[e] = lax.dot_general(
            f, source_ref[...], (((0,), (1,)), ((), ())), preferred_element_type=F32
        ).astype(BF)

    each_leaf(nx, ny, (own_ref, up_ref, down_ref, left_ref, right_ref), body, 8)


def geometry(nx, ny, parts, target_table, source_table):
    leaves, size = (nx + 2) * (ny + 2), parts[0].shape[2]
    return pl.pallas_call(
        functools.partial(geometry_kernel, nx, ny),
        out_shape=[
            jax.ShapeDtypeStruct((leaves, size, 32), BF),
            jax.ShapeDtypeStruct((leaves, 32, size), BF),
        ],
        in_specs=[VM] * 7,
        out_specs=[VM] * 2,
        compiler_params=params(),
        name="geometry",
    )(*parts, jnp.asarray(target_table, BF), jnp.asarray(source_table, BF))


def build_kernel(
    nx, ny, mask_ref, own_ref, up_ref, down_ref, left_ref, right_ref, s_ref, t_ref, factor_ref, c_ref, g_ref, b_ref,
    o_ref, list_ref, cache_ref, out_ref, v16, acc, spare, count_ref, buffer, sems,
):
    wide = ny + 2
    leaves = (nx + 2) * wide
    size = own_ref.shape[2]
    short = size - CHUNK

    def split_leaf(e, ref, i):
        v16[e] = rows16(ref[i, 4:8])
        count_ref[e] = ref[i, 3, 0].astype(jnp.int32)

    each_leaf(nx, ny, (own_ref, up_ref, down_ref, left_ref, right_ref), split_leaf)
    v16[leaves] = jnp.zeros((16, size), BF)
    acc[...] = jnp.zeros_like(acc)
    for slot in range(BUILD_SLOTS):
        for j in range(GROUP):
            buffer[slot, j, :, short:size] = jnp.zeros((2, CHUNK, size), BF)
    dummy = leaves * 1024

    def note(a, carry):
        full, less = carry
        corner = (a // ny) * wide + a % ny
        for code in range(9):
            source = corner + code // 3 * wide + code % 3
            entry = (source * 16 + code) * 64 + a
            on = jnp.where(mask_ref[a // ny, a % ny, code] != 0, 1, 0)
            long = jnp.where(count_ref[source] > short, on, 0)
            list_ref[full] = entry
            spare[less] = entry
            full = full + long
            less = less + (on - long)
        return full, less

    full, less = lax.fori_loop(0, nx * ny, note, (0, 0), unroll=2)
    for j in range(GROUP):
        list_ref[full + j] = dummy
        spare[less + j] = dummy
    full_groups = (full + GROUP - 1) // GROUP
    less_groups = (less + GROUP - 1) // GROUP
    groups = full_groups + less_groups

    def move(k, carry):
        list_ref[full_groups * GROUP + k] = spare[k]
        return carry

    lax.fori_loop(0, less_groups * GROUP, move, 0)
    list_ref[list_ref.shape[0] - 1] = groups

    def copy_out(g):
        slot = g % BUILD_SLOTS
        return pltpu.make_async_copy(buffer.at[slot], cache_ref.at[g], sems.at[slot])

    def run(first, last, rows):
        def group(g, carry):
            slot = g % BUILD_SLOTS

            @pl.when(g >= BUILD_SLOTS)
            def _():
                copy_out(g - BUILD_SLOTS).wait()

            done = []
            for j in range(GROUP):
                entry = list_ref[g * GROUP + j]
                a = entry & 63
                code = (entry >> 6) & 15
                source = entry >> 10
                t = t_ref[(a // ny + 1) * wide + a % ny + 1] * factor_ref[code]
                s = s_ref[jnp.minimum(source, leaves - 1)]
                v = v16[source]
                total = jnp.zeros((16, size), F32)
                for k in range(rows // CHUNK):
                    part = slice(k * CHUNK, (k + 1) * CHUNK)
                    squared = jnp.maximum(dot(s[part], t), 1e-30)
                    distance = squared * lax.rsqrt(squared)
                    value = (1.0 + NEAR_RATE * distance) * jnp.exp2((-NEAR_RATE * LOG2E) * distance)
                    high, low = split2(value)
                    buffer[slot, j, 0, part] = high
                    buffer[slot, j, 1, part] = low
                    total += dot(v[:, part], high) + dot(v[:, part], low)
                done.append((a, total))
            for a, total in done:
                acc[a] += total
            copy_out(g).start()
            return carry

        lax.fori_loop(first, last, group, 0)

    run(0, full_groups, size)
    run(full_groups, groups, short)
    for back in range(BUILD_SLOTS):
        copy_out(groups - 1 - back).wait()

    def finish(a, carry):
        o_ref[:, pl.ds(pl.multiple_of(a * size, size), size)] = join16(acc[a]) * (1.0 / size**0.5)
        return carry

    lax.fori_loop(0, nx * ny, finish, 0, unroll=4)
    for i in range(out_ref.shape[0]):
        out_ref[i] = c_ref[...]


def near_build(nx, ny, mask, parts, s, t, factor, c, g, b, copies):
    size = parts[0].shape[2]
    leaves = (nx + 2) * (ny + 2)
    most = nx * ny * 9 + 2 * GROUP
    return pl.pallas_call(
        functools.partial(build_kernel, nx, ny),
        out_shape=[
            jax.ShapeDtypeStruct((4, nx * ny * size), F32),
            jax.ShapeDtypeStruct((most + 8,), jnp.int32),
            jax.ShapeDtypeStruct((most // GROUP, GROUP, 2, size, size), BF),
            jax.ShapeDtypeStruct((copies, 8, 128), F32),
        ],
        in_specs=[SM] + [VM] * 9 + [ANY] * 2,
        out_specs=[VM, SM, ANY, VM],
        scratch_shapes=[
            pltpu.VMEM((leaves + 1, 16, size), BF),
            pltpu.VMEM((nx * ny, 16, size), F32),
            pltpu.SMEM((most,), jnp.int32),
            pltpu.SMEM((leaves,), jnp.int32),
            pltpu.VMEM((BUILD_SLOTS, GROUP, 2, size, size), BF),
            pltpu.SemaphoreType.DMA((BUILD_SLOTS,)),
        ],
        compiler_params=params(),
        name="near_build",
    )(mask, *parts, s, t, factor, c, g, b)


def reuse_kernel(
    nx, ny, list_ref, own_ref, up_ref, down_ref, left_ref, right_ref, c_ref, cache_ref,
    o_ref, out_ref, v16, acc, buffer, sems,
):
    wide = ny + 2
    leaves = (nx + 2) * wide
    size = own_ref.shape[2]
    groups = list_ref[list_ref.shape[0] - 1]

    def copy_in(g):
        slot = g % READ_SLOTS
        return pltpu.make_async_copy(cache_ref.at[g], buffer.at[slot], sems.at[slot])

    for g in range(READ_SLOTS - 1):
        copy_in(g).start()

    def split_leaf(e, ref, i):
        v16[e] = rows16(ref[i])

    each_leaf(nx, ny, (own_ref, up_ref, down_ref, left_ref, right_ref), split_leaf)
    v16[leaves] = jnp.zeros((16, size), BF)
    acc[...] = jnp.zeros_like(acc)

    def group(g, carry):
        slot = g % READ_SLOTS
        copy_in(g).wait()

        @pl.when(g + READ_SLOTS - 1 < groups)
        def _():
            copy_in(g + READ_SLOTS - 1).start()

        done = []
        for j in range(GROUP):
            entry = list_ref[g * GROUP + j]
            v = v16[entry >> 10]
            done.append((entry & 63, dot(v, buffer[slot, j, 0]) + dot(v, buffer[slot, j, 1])))
        for a, total in done:
            acc[a] += total
        return carry

    lax.fori_loop(0, groups, group, 0)

    def finish(a, sums):
        near = join16(acc[a]) * (1.0 / size**0.5)
        o_ref[:, pl.ds(pl.multiple_of(a * size, size), size)] = near
        v = own_ref[a]
        return tuple(sums[s] + v * near[s : s + 1] for s in range(4))

    sums = lax.fori_loop(0, nx * ny, finish, tuple(jnp.zeros((4, size), F32) for _ in range(4)), unroll=4)
    columns = [jnp.sum(x, axis=1, keepdims=True) for x in sums]
    block = jnp.concatenate([jnp.zeros((4, 12), F32)] + columns + [jnp.zeros((4, 112), F32)], axis=1)
    total = c_ref[...] + jnp.concatenate([jnp.zeros((4, 128), F32), block], axis=0)
    for i in range(out_ref.shape[0]):
        out_ref[i] = total


def near_reuse(nx, ny, todo, parts, c, cache, copies):
    size = parts[0].shape[2]
    leaves = (nx + 2) * (ny + 2)
    return pl.pallas_call(
        functools.partial(reuse_kernel, nx, ny),
        out_shape=[jax.ShapeDtypeStruct((4, nx * ny * size), F32), jax.ShapeDtypeStruct((copies, 8, 128), F32)],
        in_specs=[SM] + [VM] * 6 + [ANY],
        out_specs=[VM] * 2,
        scratch_shapes=[
            pltpu.VMEM((leaves + 1, 16, size), BF),
            pltpu.VMEM((nx * ny, 16, size), F32),
            pltpu.VMEM((READ_SLOTS,) + cache.shape[1:], BF),
            pltpu.SemaphoreType.DMA((READ_SLOTS,)),
        ],
        compiler_params=params(),
        name="near_reuse",
    )(todo, *parts, c, cache)


def upward_kernel(r_ref, basis_ref, transfer_ref, joint_ref, c_ref):
    leaves, terms, size = basis_ref.shape

    def body(a, total):
        part = pl.ds(pl.multiple_of(a * size, size), size)
        joint = exact_dot(transfer_ref[a], basis_ref[a])
        terms3 = split3(joint)
        v = rows16(r_ref[:, part])
        for k, term in enumerate(terms3):
            joint_ref[k, :, part] = term
            total = total + dot_nt(v, term)
        return total

    total = join16(lax.fori_loop(0, leaves, body, jnp.zeros((16, terms), F32), unroll=8))
    total = jnp.concatenate([total, jnp.zeros((4, 128 - terms), F32)], axis=1)
    total = jnp.concatenate([total, jnp.zeros((4, 128), F32)], axis=0)
    c_ref[...] = total


def upward(r, basis, transfer):
    leaves, terms, size = basis.shape
    return pl.pallas_call(
        upward_kernel,
        out_shape=[
            jax.ShapeDtypeStruct((3, terms, leaves * size), BF),
            jax.ShapeDtypeStruct((8, 128), F32),
        ],
        in_specs=[VM] * 3,
        out_specs=[VM] * 2,
        compiler_params=params(),
        name="upward",
    )(r, basis, transfer)


def own_place(cols):
    return lax.axis_index("gx") * cols + lax.axis_index("gy")


def coupling_kernel(levels, cols, tile, upper_ref, row_ref, b_ref, g_ref, turned_ref):
    place = own_place(cols)
    col_values = jnp.concatenate([row_ref[...], jnp.zeros((5, 64), F32)], axis=0).T
    for k in range(2):
        turned_ref[k] = upper_ref[k].T
    down = None
    for level in range(levels):
        span = 2**level
        extent = (1, span) if span <= cols else (span // cols, cols)
        half = (0.5 * tile[0] * extent[0], 0.5 * tile[1] * extent[1], 0.5)
        apart = (0.0, 2.0 * span * tile[1]) if 2 * span < cols else (2.0 * span / cols * tile[0], 0.0)

        def matrix(sign):
            squared = jnp.zeros((64, 64), F32)
            for c in range(3):
                step = half[c] * (col_values[:, c : c + 1] - row_ref[c : c + 1, :])
                if c < 2:
                    step = step + sign * apart[c]
                squared = squared + step * step
            squared = jnp.maximum(squared, 1e-30)
            scaled = FAR_RATE * (squared * lax.rsqrt(squared))
            return COUPLING_SCALE * ((1.0 + scaled) * jnp.exp(-scaled))

        b_ref[level] = matrix(-1.0)
        upper = (place // (2 * span)) % 2
        own = matrix(jnp.where(upper == 1, -1.0, 1.0))
        g_ref[level] = own if down is None else exact_dot(own, down)
        if level + 1 < levels:
            bit = (place // span) % 2
            step_down = upper_ref[bit]
            down = step_down if down is None else exact_dot(step_down, down)


def couplings(levels, cols, tile, upper, nodes):
    out = jax.ShapeDtypeStruct((levels, 64, 64), F32)
    return pl.pallas_call(
        functools.partial(coupling_kernel, levels, cols, tile),
        out_shape=[out, out, jax.ShapeDtypeStruct(upper.shape, F32)],
        in_specs=[VM] * 2,
        out_specs=[VM] * 3,
        compiler_params=params(),
        name="couplings",
    )(upper, nodes)


def pair_energy(c, b, sums):
    count = c.shape[0]
    quads = c.reshape(count // 4, 4, 8, 64)
    low = quads[:, 0:2].reshape(count // 2 * 8, 64)
    high = quads[:, 2:4].reshape(count // 2, 8, 64)
    carried = exact_dot(low, b).reshape(count // 2, 8, 64)
    return [sums[s] + jnp.sum(carried * high[:, s : s + 1, :], axis=0) for s in range(4)]


def lift(c, upper_t):
    count = c.shape[0]
    paired = c.reshape(count // 2, 2, 8, 64)
    even = paired[:, 0].reshape(count // 2 * 8, 64)
    odd = paired[:, 1].reshape(count // 2 * 8, 64)
    return (exact_dot(even, upper_t[0]) + exact_dot(odd, upper_t[1])).reshape(count // 2, 8, 64)


def no_sums():
    return [jnp.zeros((8, 64), F32) for _ in range(4)]


def columns_of(sums):
    return jnp.concatenate([jnp.sum(x, axis=1, keepdims=True) for x in sums], axis=1)


def row_kernel(with_energy, c_ref, upper_ref, g_ref, b_ref, y_ref, out_ref, scratch):
    x = c_ref[...]
    c = x[:, :, 0:64]
    place = lax.axis_index("gy")
    y = jnp.zeros((8, 64), F32)
    sums = no_sums()
    level = 0
    while c.shape[0] > 2:
        scratch[0 : c.shape[0]] = c
        y = y + exact_dot(scratch[(place // 2**level) ^ 2], g_ref[level])
        if with_energy:
            sums = pair_energy(c, b_ref[level], sums)
        c = lift(c, upper_ref)
        level += 1
    y_ref[...] = y
    lower = jnp.zeros((4, 128), F32)
    if with_energy:
        lower = jnp.sum(x, axis=0)[4:8]
        lower = jnp.concatenate([lower[:, 0:16], columns_of(sums)[0:4], jnp.zeros((4, 108), F32)], axis=1)
    total = jnp.concatenate([jnp.concatenate([c[0, 0:4], c[1, 0:4]], axis=1), lower], axis=0)
    for i in range(out_ref.shape[0]):
        out_ref[i] = total


def row_tree(with_energy, c, upper_t, g, b):
    return pl.pallas_call(
        functools.partial(row_kernel, with_energy),
        out_shape=[jax.ShapeDtypeStruct((8, 64), F32), jax.ShapeDtypeStruct(c.shape, F32)],
        in_specs=[VM] * 4,
        out_specs=[VM] * 2,
        scratch_shapes=[pltpu.VMEM((c.shape[0], 8, 64), F32)],
        compiler_params=params(),
        name="row_tree",
    )(c, upper_t, g, b)


def upper_levels(cols, levels, x, y, upper_ref, g_ref, b_ref, scratch, with_energy):
    place = own_place(cols)
    level = cols.bit_length() - 2
    c = jnp.stack([x[:, :, 0:64], x[:, :, 64:128]], axis=1).reshape(2 * x.shape[0], 8, 64)
    sums = no_sums()
    while level < levels:
        scratch[0 : c.shape[0]] = c
        y = y + exact_dot(scratch[(place // 2**level) ^ 2], g_ref[level])
        if with_energy:
            sums = pair_energy(c, b_ref[level], sums)
        if level + 1 < levels:
            c = lift(c, upper_ref)
        level += 1
    return y[0:4], sums


SPLITS = 8


def far_of(y, joint_ref, part):
    return join16(dot(y, joint_ref[0, :, part]) + (dot(y, joint_ref[1, :, part]) + dot(y, joint_ref[2, :, part])))


def middle_kernel(
    cols, levels, x_ref, y_ref, upper_ref, g_ref, joint_ref, r_ref, n_ref, valid_ref,
    e_ref, leaf_ref, top_ref, bottom_ref, out_ref, scratch, both,
):
    leaves, _, size = leaf_ref.shape
    own, _ = upper_levels(cols, levels, x_ref[...], y_ref[...], upper_ref, g_ref, None, scratch, False)
    y = rows16(own)
    width = leaves * size // SPLITS
    for k in range(SPLITS):
        part = slice(k * width, (k + 1) * width)
        far = far_of(y, joint_ref, part)
        e = valid_ref[:, part] * (n_ref[:, part] + far)
        e_ref[:, part] = e
        both[0:16, part] = rows16(r_ref[:, part])
        both[16:32, part] = rows16(e)
        for i in range(leaves // SPLITS):
            leaf_ref[k * (leaves // SPLITS) + i] = e[:, i * size : (i + 1) * size]
    edge = top_ref.shape[0]
    top_ref[...] = leaf_ref[0:edge]
    bottom_ref[...] = leaf_ref[leaves - edge : leaves]
    e16 = both[16:32, :]
    c = join16(dot_nt(e16, joint_ref[0]) + (dot_nt(e16, joint_ref[1]) + dot_nt(e16, joint_ref[2])))
    square = dot_nt(both[...], both[...])

    def block(i, j):
        part = join16(square[16 * i : 16 * i + 16, 16 * j : 16 * j + 16])
        return part[:, 0:4] + part[:, 4:8] + part[:, 8:12]

    moments = jnp.concatenate([block(0, 0), block(0, 1), block(1, 1), jnp.zeros((4, 116), F32)], axis=1)
    out_ref[...] = jnp.concatenate([jnp.concatenate([c, jnp.zeros((4, 64), F32)], axis=1), moments], axis=0)


def middle(cols, levels, leaves, edge, x, y, upper_t, g, joint, r, n, valid):
    size = r.shape[1] // leaves
    return pl.pallas_call(
        functools.partial(middle_kernel, cols, levels),
        out_shape=[
            jax.ShapeDtypeStruct(r.shape, F32),
            jax.ShapeDtypeStruct((leaves, 4, size), F32),
            jax.ShapeDtypeStruct((edge, 4, size), F32),
            jax.ShapeDtypeStruct((edge, 4, size), F32),
            jax.ShapeDtypeStruct((8, 128), F32),
        ],
        in_specs=[VM] * 8,
        out_specs=[VM] * 5,
        scratch_shapes=[pltpu.VMEM((2 * x.shape[0], 8, 64), F32), pltpu.VMEM((32, r.shape[1]), BF)],
        compiler_params=params(),
        name="middle",
    )(x, y, upper_t, g, joint, r, n, valid)


def mat_mul(a, b):
    return [[sum(a[i][k] * b[k][j] for k in range(4)) for j in range(4)] for i in range(4)]


def mat_add(a, b):
    return [[a[i][j] + b[i][j] for j in range(4)] for i in range(4)]


def mat_sub(a, b):
    return [[a[i][j] - b[i][j] for j in range(4)] for i in range(4)]


def mat_t(a):
    return [[a[j][i] for j in range(4)] for i in range(4)]


def mat_solve(a, b):
    a = [list(row) for row in a]
    b = [list(row) for row in b]
    width = len(b[0])
    inverse = []
    for col in range(4):
        inverse.append(1.0 / a[col][col])
        for row in range(col + 1, 4):
            factor = a[row][col] * inverse[col]
            for k in range(col + 1, 4):
                a[row][k] = a[row][k] - factor * a[col][k]
            for k in range(width):
                b[row][k] = b[row][k] - factor * b[col][k]
    result = [None] * 4
    for col in reversed(range(4)):
        row = list(b[col])
        for later in range(col + 1, 4):
            row = [row[k] - a[col][later] * result[later][k] for k in range(width)]
        result[col] = [value * inverse[col] for value in row]
    return result


def weights(gram, cross, square, cubic):
    curvature = mat_add(gram, cross)
    both = mat_solve(curvature, [gram[i] + cross[i] for i in range(4)])
    step = [row[0:4] for row in both]
    rest = [row[4:8] for row in both]
    mixed = mat_mul(mat_t(rest), mat_mul(cross, step))
    gram_next = mat_sub(
        mat_add(mat_mul(mat_t(rest), mat_mul(gram, rest)), mat_mul(mat_t(step), mat_mul(square, step))),
        mat_add(mixed, mat_t(mixed)),
    )
    mix = mat_solve(gram, gram_next)
    lead = mat_add(rest, mix)
    second = mat_sub(lead, step)
    with_r = mat_sub(mat_add(mat_mul(gram, lead), mat_mul(cross, second)), mat_mul(square, step))
    with_e = mat_sub(mat_add(mat_mul(mat_t(cross), lead), mat_mul(square, second)), mat_mul(cubic, step))
    curvature_next = mat_sub(mat_mul(mat_t(lead), with_r), mat_mul(mat_t(step), with_e))
    step_next = mat_solve(curvature_next, gram_next)
    lead_step = mat_mul(lead, step_next)
    step_step = mat_mul(step, step_next)
    second_step = mat_sub(lead_step, step_step)
    solution = (mat_add(step, lead_step), [[-v for v in row] for row in step_step], None)
    residual = (mat_sub(rest, lead_step), [[-(step[i][j] + second_step[i][j]) for j in range(4)] for i in range(4)], step_step)
    return solution, residual


def final_kernel(
    cols, levels, c_ref, y_ref, upper_ref, g_ref, b_ref, joint_ref, r_ref, e_ref, n_ref, valid_ref,
    x_ref, out_ref, scratch,
):
    leaves, _, size = x_ref.shape
    c = c_ref[...]
    own, sums = upper_levels(cols, levels, c, y_ref[...], upper_ref, g_ref, b_ref, scratch, True)
    y = rows16(own)
    moments = jnp.sum(c, axis=0)[4:8]
    half = columns_of(sums)

    def matrix(x, at):
        return [[jnp.broadcast_to(x[i : i + 1, at + j : at + j + 1], (1, 128)) for j in range(4)] for i in range(4)]

    half = mat_add(matrix(moments, 16), matrix(half, 0))
    cubic = mat_add(matrix(moments, 12), mat_add(half, mat_t(half)))
    solution, residual = weights(matrix(moments, 0), matrix(moments, 4), matrix(moments, 8), cubic)
    row = lax.broadcasted_iota(jnp.int32, (8, 128), 0)
    col = lax.broadcasted_iota(jnp.int32, (8, 128), 1)
    table = jnp.zeros((8, 128), F32)
    for first, parts in ((0, solution), (4, residual)):
        for k, part in enumerate(parts):
            if part is None:
                continue
            for i in range(4):
                line = jnp.zeros((8, 128), F32)
                for j in range(4):
                    line = jnp.where(row == first + j, part[i][j], line)
                table = jnp.where(col == 4 * k + i, line + table, table)
    table = table[:, 0:16]
    width = leaves * size // SPLITS
    for k in range(SPLITS):
        part = slice(k * width, (k + 1) * width)
        far = far_of(y, joint_ref, part)
        f = valid_ref[:, part] * (n_ref[:, part] + far)
        stacked = jnp.concatenate([r_ref[:, part], e_ref[:, part], f, jnp.zeros_like(f)], axis=0)
        both = jnp.dot(table, stacked, precision=lax.Precision.HIGHEST, preferred_element_type=F32)
        for i in range(leaves // SPLITS):
            x_ref[k * (leaves // SPLITS) + i] = both[0:4, i * size : (i + 1) * size]
            out_ref[k * (leaves // SPLITS) + i] = both[4:8, i * size : (i + 1) * size]


def final(cols, levels, leaves, c, y, upper_t, g, b, joint, r, e, n, valid):
    out = jax.ShapeDtypeStruct((leaves, 4, r.shape[1] // leaves), F32)
    return pl.pallas_call(
        functools.partial(final_kernel, cols, levels),
        out_shape=[out, out],
        in_specs=[VM] * 10,
        out_specs=[VM] * 2,
        scratch_shapes=[pltpu.VMEM((2 * c.shape[0], 8, 64), F32)],
        compiler_params=params(),
        name="final",
    )(c, y, upper_t, g, b, joint, r, e, n, valid)


def swap(axis, first, last):
    count = lax.axis_size(axis)
    up = [(i, i + 1) for i in range(count - 1)]
    down = [(j, i) for i, j in up]
    return lax.ppermute(last, axis, up), lax.ppermute(first, axis, down)


def edges(nx, ny, own, top, bottom):
    up, down = swap("gx", top, bottom)
    left, right = swap("gy", *side_columns(nx, ny, own, up, down))
    return own, up, down, left, right


def exchange(x, axis):
    return lax.all_to_all(x, axis, 0, 0, tiled=True)


def on_device(points, right_sides, leaf_counts, near_mask, leaf_basis, leaf_transfer, upper_transfer, proxy_nodes):
    nx, ny, _, size = points.shape
    leaves = nx * ny
    rows, cols = lax.axis_size("gx"), lax.axis_size("gy")
    levels = (rows * cols).bit_length() - 2
    target_table, source_table, factor = feature_tables()
    factor = jnp.asarray(np.broadcast_to(factor[:, :, None], (9, 32, size)), BF)

    def flat(x):
        return x.reshape((leaves,) + x.shape[2:])

    packed, top, bottom, r, valid = pack(nx, ny, leaf_counts, flat(points), flat(right_sides))
    parts = edges(nx, ny, packed, top, bottom)
    joint, c = upward(r, flat(leaf_basis), flat(leaf_transfer))
    b, g, upper_t = couplings(levels, cols, (nx, ny), upper_transfer, proxy_nodes)
    s, t = geometry(nx, ny, parts, target_table, source_table)
    n, todo, cache, c = near_build(nx, ny, near_mask, parts, s, t, factor, c, g, b, cols)
    y, c = row_tree(False, exchange(c, "gy"), upper_t, g, b)
    e, e_leaves, top, bottom, c = middle(
        cols, levels, leaves, ny, exchange(c, "gx"), y, upper_t, g, joint, r, n, valid
    )
    n, c = near_reuse(nx, ny, todo, edges(nx, ny, e_leaves, top, bottom), c, cache, cols)
    y, c = row_tree(True, exchange(c, "gy"), upper_t, g, b)
    x, out = final(cols, levels, leaves, exchange(c, "gx"), y, upper_t, g, b, joint, r, e, n, valid)
    shape = (nx, ny, 4, size)
    return x.reshape(shape), out.reshape(shape)


def solution(mesh):
    return jax.shard_map(
        on_device,
        mesh=mesh,
        in_specs=(
            P("gx", "gy", None, None),
            P("gx", "gy", None, None),
            P("gx", "gy"),
            P("gx", "gy", None),
            P("gx", "gy", None, None),
            P("gx", "gy", None, None),
            P(),
            P(),
        ),
        out_specs=(P("gx", "gy", None, None), P("gx", "gy", None, None)),
        check_vma=False,
    )
```

```python
import functools

import jax
import jax.numpy as jnp
import numpy as np
from jax import lax
from jax.experimental import pallas as pl
from jax.experimental.pallas import tpu as pltpu
from jax.sharding import PartitionSpec as P

F32 = jnp.float32
BF = jnp.bfloat16
NEAR_LENGTH = 0.5
FAR_LENGTH = 16.0
NEAR_RATE = 3.0**0.5 / NEAR_LENGTH
FAR_RATE = 3.0**0.5 / FAR_LENGTH
LOG2E = 1.4426950408889634
COUPLING_SCALE = 1.0 / 128.0
GROUP = 8
CHUNK = 64
BUILD_SLOTS = 2
READ_SLOTS = 6
VMEM_LIMIT = 20 * 2**20
VM = pl.BlockSpec(memory_space=pltpu.VMEM)
ANY = pl.BlockSpec(memory_space=pl.ANY)
SM = pl.BlockSpec(memory_space=pltpu.SMEM)


def rounded(x):
    return x.astype(BF).astype(F32)


def split2(x):
    high = x.astype(BF)
    return high, (x - high.astype(F32)).astype(BF)


def rows16(x):
    first = rounded(x)
    second = rounded(x - first)
    third = rounded(x - first - second)
    return jnp.concatenate([first, second, third, jnp.zeros_like(x)], axis=0).astype(BF)


def join16(y):
    return y[0:4] + y[4:8] + y[8:12]


def dot(a, b):
    return jnp.dot(a, b, preferred_element_type=F32)


def dot_nt(a, b):
    return lax.dot_general(a, b, (((1,), (1,)), ((), ())), preferred_element_type=F32)


def split3(x):
    first = x.astype(BF)
    rest = x - first.astype(F32)
    second = rest.astype(BF)
    return first, second, (rest - second.astype(F32)).astype(BF)


def exact_dot(a, b):
    return jnp.dot(a, b, precision=lax.Precision.HIGHEST, preferred_element_type=F32)


def feature_tables():
    target = np.zeros((32, 24), np.float32)
    source = np.zeros((32, 24), np.float32)
    factor = np.ones((9, 32), np.float32)
    one = 19
    for c in range(3):
        target[2 * c, c] = target[2 * c + 1, c] = -2
        source[2 * c, c] = source[2 * c + 1, 8 + c] = 1
        target[6 + 2 * c, 8 + c] = target[7 + 2 * c, 8 + c] = -2
        source[6 + 2 * c, c] = source[7 + 2 * c, 8 + c] = 1
    for k in range(3):
        target[12 + k, one] = source[12 + k, 16 + k] = 1
        target[15 + k, 16 + k] = source[15 + k, one] = 1
    for c in range(2):
        target[18 + 2 * c, c] = target[19 + 2 * c, 8 + c] = 1
        source[18 + 2 * c, one] = source[19 + 2 * c, one] = 1
        target[22 + 2 * c, one] = target[23 + 2 * c, one] = 1
        source[22 + 2 * c, c] = source[23 + 2 * c, 8 + c] = 1
    target[26, one] = source[26, one] = 1
    for code in range(9):
        off = (code // 3 - 1, code % 3 - 1)
        for c in range(2):
            factor[code, 18 + 2 * c : 20 + 2 * c] = -2 * off[c]
            factor[code, 22 + 2 * c : 24 + 2 * c] = 2 * off[c]
        factor[code, 26] = off[0] ** 2 + off[1] ** 2
    return target, source, factor


def params():
    return pltpu.CompilerParams(vmem_limit_bytes=VMEM_LIMIT)


def around(nx, ny):
    wide = ny + 2
    return (
        (nx * ny, lambda i: (i // ny + 1) * wide + i % ny + 1),
        (ny, lambda i: i + 1),
        (ny, lambda i: (nx + 1) * wide + i + 1),
        (nx + 2, lambda i: i * wide),
        (nx + 2, lambda i: i * wide + wide - 1),
    )


def each_leaf(nx, ny, refs, body, unroll=4):
    for ref, (count, place) in zip(refs, around(nx, ny)):

        def step(i, carry, ref=ref, place=place):
            body(place(i), ref, i)
            return carry

        lax.fori_loop(0, count, step, 0, unroll=unroll if count % unroll == 0 else 2)


def pack_kernel(nx, ny, count_ref, points_ref, sides_ref, packed_ref, top_ref, bottom_ref, r_ref, valid_ref):
    size = points_ref.shape[3]
    lane = lax.broadcasted_iota(jnp.int32, (1, size), 1)

    def body(a, carry):
        first = (lax.axis_index("gx") * nx + a // ny).astype(F32) + 0.5
        second = (lax.axis_index("gy") * ny + a % ny).astype(F32) + 0.5
        for c, centre in enumerate((first, second, 0.5)):
            packed_ref[a, c : c + 1] = points_ref[a // ny, c, pl.ds(a % ny, 1)] - centre
        count = count_ref[a // ny, a % ny]
        packed_ref[a, 3:4] = jnp.full((1, size), count.astype(F32))
        valid = jnp.where(lane < count, 1.0, 0.0)
        r = jnp.where(valid > 0.0, sides_ref[a], 0.0)
        packed_ref[a, 4:8] = r
        part = pl.ds(pl.multiple_of(a * size, size), size)
        r_ref[:, part] = r
        valid_ref[:, part] = valid
        return carry

    lax.fori_loop(0, nx * ny, body, 0, unroll=4)
    top_ref[...] = packed_ref[0:ny]
    bottom_ref[...] = packed_ref[(nx - 1) * ny : nx * ny]


def pack(nx, ny, counts, points, sides):
    leaves, _, size = sides.shape
    return pl.pallas_call(
        functools.partial(pack_kernel, nx, ny),
        out_shape=[
            jax.ShapeDtypeStruct((leaves, 8, size), F32),
            jax.ShapeDtypeStruct((ny, 8, size), F32),
            jax.ShapeDtypeStruct((ny, 8, size), F32),
            jax.ShapeDtypeStruct((4, leaves * size), F32),
            jax.ShapeDtypeStruct((1, leaves * size), F32),
        ],
        in_specs=[SM, VM, VM],
        out_specs=[VM] * 5,
        compiler_params=params(),
        name="pack",
    )(counts, points, sides)


def sides_kernel(nx, ny, own_ref, up_ref, down_ref, after_ref, left_ref, right_ref):
    for col, ref in ((0, left_ref), (ny - 1, right_ref)):
        ref[0] = up_ref[col]
        ref[nx + 1] = down_ref[col]
        for i in range(nx):
            ref[i + 1] = own_ref[i * ny + col]


def side_columns(nx, ny, own, up, down, after):
    out = jax.ShapeDtypeStruct((nx + 2,) + own.shape[1:], F32)
    return pl.pallas_call(
        functools.partial(sides_kernel, nx, ny),
        out_shape=[out, out],
        in_specs=[VM] * 3 + [ANY],
        out_specs=[VM] * 2,
        compiler_params=params(),
        name="side_columns",
    )(own, up, down, after)


def geometry_kernel(
    nx, ny, mask_ref, own_ref, up_ref, down_ref, left_ref, right_ref, target_ref, source_ref, c_ref, after_ref,
    s_ref, t_ref, v_ref, long_ref, short_ref, groups_ref, out_ref, count_ref,
):
    wide = ny + 2
    leaves = (nx + 2) * wide
    size = own_ref.shape[2]
    row = lax.broadcasted_iota(jnp.int32, (8, size), 0)
    refs = (own_ref, up_ref, down_ref, left_ref, right_ref)

    def read_count(e, ref, i):
        count_ref[e] = ref[i, 3, 0].astype(jnp.int32)

    each_leaf(nx, ny, refs, read_count)

    def features(e, ref, i):
        packed = ref[i]
        x = jnp.where(row < 3, packed, 0.0)
        first = rounded(x)
        second = rounded(x - first)
        held = first + second
        norm = jnp.sum(held * held, axis=0, keepdims=True)
        n1 = rounded(norm)
        n2 = rounded(norm - n1)
        n3 = rounded(norm - n1 - n2)
        last = jnp.where(row == 0, n1, jnp.where(row == 1, n2, jnp.where(row == 2, n3, jnp.where(row == 3, 1.0, 0.0))))
        f = jnp.concatenate([first, second, last], axis=0).astype(BF)
        t_ref[e] = dot(target_ref[...], f).astype(BF)
        s_ref[e] = lax.dot_general(
            f, source_ref[...], (((0,), (1,)), ((), ())), preferred_element_type=F32
        ).astype(BF)
        v_ref[e] = rows16(packed[4:8])

    def note(a, carry):
        features((a // ny + 1) * wide + a % ny + 1, own_ref, a)
        long_count, short_count = carry
        corner = (a // ny) * wide + a % ny
        for code in range(9):
            source = corner + code // 3 * wide + code % 3
            entry = (source * 16 + code) * 64 + a
            on = jnp.where(mask_ref[a // ny, a % ny, code] != 0, 1, 0)
            is_long = jnp.where(count_ref[source] > size - CHUNK, on, 0)
            long_ref[long_count] = entry
            short_ref[short_count] = entry
            long_count = long_count + is_long
            short_count = short_count + (on - is_long)
        return long_count, short_count

    long_count, short_count = lax.fori_loop(0, nx * ny, note, (0, 0), unroll=4)
    for j in range(GROUP):
        long_ref[long_count + j] = leaves * 1024
        short_ref[short_count + j] = leaves * 1024
    groups_ref[0] = (long_count + GROUP - 1) // GROUP
    groups_ref[1] = (short_count + GROUP - 1) // GROUP
    for ref, (count, place) in list(zip(refs, around(nx, ny)))[1:]:

        def step(i, carry, ref=ref, place=place):
            features(place(i), ref, i)
            return carry

        lax.fori_loop(0, count, step, 0, unroll=True)
    v_ref[leaves] = jnp.zeros((16, size), BF)
    for i in range(out_ref.shape[0]):
        out_ref[i] = c_ref[...]


def geometry(nx, ny, mask, parts, target_table, source_table, c, after, copies):
    leaves, size = (nx + 2) * (ny + 2), parts[0].shape[2]
    most = nx * ny * 9 + GROUP
    return pl.pallas_call(
        functools.partial(geometry_kernel, nx, ny),
        out_shape=[
            jax.ShapeDtypeStruct((leaves, size, 32), BF),
            jax.ShapeDtypeStruct((leaves, 32, size), BF),
            jax.ShapeDtypeStruct((leaves + 1, 16, size), BF),
            jax.ShapeDtypeStruct((most,), jnp.int32),
            jax.ShapeDtypeStruct((most,), jnp.int32),
            jax.ShapeDtypeStruct((2,), jnp.int32),
            jax.ShapeDtypeStruct((copies, 8, 128), F32),
        ],
        in_specs=[SM] + [VM] * 8 + [ANY],
        out_specs=[VM] * 3 + [SM] * 3 + [VM],
        scratch_shapes=[pltpu.SMEM((leaves,), jnp.int32)],
        compiler_params=params(),
        name="geometry",
    )(mask, *parts, jnp.asarray(target_table, BF), jnp.asarray(source_table, BF), c, after)


def block_copy(buffer, cache_ref, sems, slots, rows, inward):
    def copy(g):
        slot = g % slots
        here, there = buffer.at[slot], cache_ref.at[g]
        if rows < cache_ref.shape[3]:
            here, there = here.at[:, :, 0:rows], there.at[:, :, 0:rows]
        if inward:
            return pltpu.make_async_copy(there, here, sems.at[slot])
        return pltpu.make_async_copy(here, there, sems.at[slot])

    return copy


def build_kernel(
    nx, ny, long_ref, short_ref, groups_ref, v_ref, s_ref, t_ref, factor_ref, after_ref,
    o_ref, cache_ref, acc, buffer, sems,
):
    wide = ny + 2
    leaves = (nx + 2) * wide
    size = o_ref.shape[1] // (nx * ny)
    short = size - CHUNK
    acc[...] = jnp.zeros_like(acc)
    long_groups = groups_ref[0]
    groups = long_groups + groups_ref[1]
    out_long = block_copy(buffer, cache_ref, sems, BUILD_SLOTS, size, False)
    out_short = block_copy(buffer, cache_ref, sems, BUILD_SLOTS, short, False)

    def wait(g):
        @pl.when(g < long_groups)
        def _():
            out_long(g).wait()

        @pl.when(g >= long_groups)
        def _():
            out_short(g).wait()

    def run(first, last, rows, list_ref, start):
        def group(g, carry):
            slot = g % BUILD_SLOTS

            @pl.when(g >= BUILD_SLOTS)
            def _():
                wait(g - BUILD_SLOTS)

            done = []
            for j in range(GROUP):
                entry = list_ref[(g - first) * GROUP + j]
                a = entry & 63
                code = (entry >> 6) & 15
                source = entry >> 10
                t = t_ref[(a // ny + 1) * wide + a % ny + 1] * factor_ref[code]
                s = s_ref[jnp.minimum(source, leaves - 1)]
                v = v_ref[source]
                total = jnp.zeros((16, size), F32)
                for k in range(rows // CHUNK):
                    part = slice(k * CHUNK, (k + 1) * CHUNK)
                    squared = jnp.maximum(dot(s[part], t), 1e-30)
                    distance = squared * lax.rsqrt(squared)
                    value = (1.0 + NEAR_RATE * distance) * jnp.exp2((-NEAR_RATE * LOG2E) * distance)
                    high, low = split2(value)
                    buffer[slot, j, 0, part] = high
                    buffer[slot, j, 1, part] = low
                    total += dot(v[:, part], high) + dot(v[:, part], low)
                done.append((a, total))
            for a, total in done:
                acc[a] += total
            start(g).start()
            return carry

        lax.fori_loop(first, last, group, 0)

    run(0, long_groups, size, long_ref, out_long)
    run(long_groups, groups, short, short_ref, out_short)
    for back in range(BUILD_SLOTS):
        wait(groups - 1 - back)

    def finish(a, carry):
        o_ref[:, pl.ds(pl.multiple_of(a * size, size), size)] = join16(acc[a]) * (1.0 / size**0.5)
        return carry

    lax.fori_loop(0, nx * ny, finish, 0, unroll=4)


def near_build(nx, ny, lists, v, s, t, factor, after):
    size = v.shape[2]
    most = lists[0].shape[0] // GROUP + 1
    return pl.pallas_call(
        functools.partial(build_kernel, nx, ny),
        out_shape=[
            jax.ShapeDtypeStruct((4, nx * ny * size), F32),
            jax.ShapeDtypeStruct((most, GROUP, 2, size, size), BF),
        ],
        in_specs=[SM] * 3 + [VM] * 4 + [ANY],
        out_specs=[VM, ANY],
        scratch_shapes=[
            pltpu.VMEM((nx * ny, 16, size), F32),
            pltpu.VMEM((BUILD_SLOTS, GROUP, 2, size, size), BF),
            pltpu.SemaphoreType.DMA((BUILD_SLOTS,)),
        ],
        compiler_params=params(),
        name="near_build",
    )(*lists, v, s, t, factor, after)


def reuse_kernel(
    nx, ny, long_ref, short_ref, groups_ref, own_ref, up_ref, down_ref, left_ref, right_ref, c_ref, cache_ref,
    o_ref, out_ref, v16, acc, buffer, sems,
):
    wide = ny + 2
    leaves = (nx + 2) * wide
    size = own_ref.shape[2]
    short = size - CHUNK
    long_groups = groups_ref[0]
    groups = long_groups + groups_ref[1]
    in_long = block_copy(buffer, cache_ref, sems, READ_SLOTS, size, True)
    in_short = block_copy(buffer, cache_ref, sems, READ_SLOTS, short, True)

    def fetch(g):
        @pl.when(g < long_groups)
        def _():
            in_long(g).start()

        @pl.when(jnp.logical_and(g >= long_groups, g < groups))
        def _():
            in_short(g).start()

    for g in range(READ_SLOTS - 1):
        fetch(g)

    def split_leaf(e, ref, i):
        v16[e] = rows16(ref[i])

    each_leaf(nx, ny, (own_ref, up_ref, down_ref, left_ref, right_ref), split_leaf)
    v16[leaves] = jnp.zeros((16, size), BF)
    acc[...] = jnp.zeros_like(acc)

    def run(first, last, rows, list_ref, copy):
        def group(g, carry):
            slot = g % READ_SLOTS
            copy(g).wait()
            fetch(g + READ_SLOTS - 1)
            done = []
            for j in range(GROUP):
                entry = list_ref[(g - first) * GROUP + j]
                v = v16[entry >> 10][:, 0:rows]
                done.append((entry & 63, dot(v, buffer[slot, j, 0, 0:rows]) + dot(v, buffer[slot, j, 1, 0:rows])))
            for a, total in done:
                acc[a] += total
            return carry

        lax.fori_loop(first, last, group, 0)

    run(0, long_groups, size, long_ref, in_long)
    run(long_groups, groups, short, short_ref, in_short)

    def finish(a, sums):
        near = join16(acc[a]) * (1.0 / size**0.5)
        o_ref[:, pl.ds(pl.multiple_of(a * size, size), size)] = near
        v = own_ref[a]
        return tuple(sums[s] + v * near[s : s + 1] for s in range(4))

    sums = lax.fori_loop(0, nx * ny, finish, tuple(jnp.zeros((4, size), F32) for _ in range(4)), unroll=4)
    columns = [jnp.sum(x, axis=1, keepdims=True) for x in sums]
    block = jnp.concatenate([jnp.zeros((4, 12), F32)] + columns + [jnp.zeros((4, 112), F32)], axis=1)
    total = c_ref[...] + jnp.concatenate([jnp.zeros((4, 128), F32), block], axis=0)
    for i in range(out_ref.shape[0]):
        out_ref[i] = total


def near_reuse(nx, ny, lists, parts, c, cache, copies):
    size = parts[0].shape[2]
    leaves = (nx + 2) * (ny + 2)
    return pl.pallas_call(
        functools.partial(reuse_kernel, nx, ny),
        out_shape=[jax.ShapeDtypeStruct((4, nx * ny * size), F32), jax.ShapeDtypeStruct((copies, 8, 128), F32)],
        in_specs=[SM] * 3 + [VM] * 6 + [ANY],
        out_specs=[VM] * 2,
        scratch_shapes=[
            pltpu.VMEM((leaves + 1, 16, size), BF),
            pltpu.VMEM((nx * ny, 16, size), F32),
            pltpu.VMEM((READ_SLOTS,) + cache.shape[1:], BF),
            pltpu.SemaphoreType.DMA((READ_SLOTS,)),
        ],
        compiler_params=params(),
        name="near_reuse",
    )(*lists, *parts, c, cache)


def upward_kernel(r_ref, basis_ref, transfer_ref, joint_ref, c_ref):
    leaves, terms, size = basis_ref.shape

    def body(a, total):
        part = pl.ds(pl.multiple_of(a * size, size), size)
        v = rows16(r_ref[:, part])
        for term, piece in enumerate(split3(exact_dot(transfer_ref[a], basis_ref[a]))):
            joint_ref[term, :, part] = piece
            total = total + dot_nt(v, piece)
        return total

    total = lax.fori_loop(0, leaves, body, jnp.zeros((16, terms), F32), unroll=8)
    total = jnp.concatenate([join16(total), jnp.zeros((4, 128 - terms), F32)], axis=1)
    c_ref[...] = jnp.concatenate([total, jnp.zeros((4, 128), F32)], axis=0)


def upward(r, basis, transfer):
    leaves, terms, size = basis.shape
    return pl.pallas_call(
        upward_kernel,
        out_shape=[
            jax.ShapeDtypeStruct((3, terms, leaves * size), BF),
            jax.ShapeDtypeStruct((8, 128), F32),
        ],
        in_specs=[VM] * 3,
        out_specs=[VM] * 2,
        compiler_params=params(),
        name="upward",
    )(r, basis, transfer)


def own_place(cols):
    return lax.axis_index("gx") * cols + lax.axis_index("gy")


def coupling_kernel(levels, cols, tile, upper_ref, row_ref, b_ref, g_ref, turned_ref):
    place = own_place(cols)
    col_values = jnp.concatenate([row_ref[...], jnp.zeros((5, 64), F32)], axis=0).T
    for k in range(2):
        turned_ref[k] = upper_ref[k].T
    down = None
    for level in range(levels):
        span = 2**level
        extent = (1, span) if span <= cols else (span // cols, cols)
        half = (0.5 * tile[0] * extent[0], 0.5 * tile[1] * extent[1], 0.5)
        apart = (0.0, 2.0 * span * tile[1]) if 2 * span < cols else (2.0 * span / cols * tile[0], 0.0)

        def matrix(sign):
            squared = jnp.zeros((64, 64), F32)
            for c in range(3):
                step = half[c] * (col_values[:, c : c + 1] - row_ref[c : c + 1, :])
                if c < 2:
                    step = step + sign * apart[c]
                squared = squared + step * step
            squared = jnp.maximum(squared, 1e-30)
            scaled = FAR_RATE * (squared * lax.rsqrt(squared))
            return COUPLING_SCALE * ((1.0 + scaled) * jnp.exp(-scaled))

        b_ref[level] = matrix(-1.0)
        upper = (place // (2 * span)) % 2
        own = matrix(jnp.where(upper == 1, -1.0, 1.0))
        g_ref[level] = own if down is None else exact_dot(own, down)
        if level + 1 < levels:
            bit = (place // span) % 2
            step_down = upper_ref[bit]
            down = step_down if down is None else exact_dot(step_down, down)


def couplings(levels, cols, tile, upper, nodes):
    out = jax.ShapeDtypeStruct((levels, 64, 64), F32)
    return pl.pallas_call(
        functools.partial(coupling_kernel, levels, cols, tile),
        out_shape=[out, out, jax.ShapeDtypeStruct(upper.shape, F32)],
        in_specs=[VM] * 2,
        out_specs=[VM] * 3,
        compiler_params=params(),
        name="couplings",
    )(upper, nodes)


def pair_energy(c, b, sums):
    count = c.shape[0]
    quads = c.reshape(count // 4, 4, 8, 64)
    low = quads[:, 0:2].reshape(count // 2 * 8, 64)
    high = quads[:, 2:4].reshape(count // 2, 8, 64)
    carried = exact_dot(low, b).reshape(count // 2, 8, 64)
    return [sums[s] + jnp.sum(carried * high[:, s : s + 1, :], axis=0) for s in range(4)]


def lift(c, upper_t):
    count = c.shape[0]
    paired = c.reshape(count // 2, 2, 8, 64)
    even = paired[:, 0].reshape(count // 2 * 8, 64)
    odd = paired[:, 1].reshape(count // 2 * 8, 64)
    return (exact_dot(even, upper_t[0]) + exact_dot(odd, upper_t[1])).reshape(count // 2, 8, 64)


def no_sums():
    return [jnp.zeros((8, 64), F32) for _ in range(4)]


def columns_of(sums):
    return jnp.concatenate([jnp.sum(x, axis=1, keepdims=True) for x in sums], axis=1)


def row_kernel(with_energy, c_ref, upper_ref, g_ref, b_ref, y_ref, out_ref, scratch):
    x = c_ref[...]
    c = x[:, :, 0:64]
    place = lax.axis_index("gy")
    y = jnp.zeros((8, 64), F32)
    sums = no_sums()
    level = 0
    while c.shape[0] > 2:
        scratch[0 : c.shape[0]] = c
        y = y + exact_dot(scratch[(place // 2**level) ^ 2], g_ref[level])
        if with_energy:
            sums = pair_energy(c, b_ref[level], sums)
        c = lift(c, upper_ref)
        level += 1
    y_ref[...] = y
    lower = jnp.zeros((4, 128), F32)
    if with_energy:
        lower = jnp.sum(x, axis=0)[4:8]
        lower = jnp.concatenate([lower[:, 0:16], columns_of(sums)[0:4], jnp.zeros((4, 108), F32)], axis=1)
    total = jnp.concatenate([jnp.concatenate([c[0, 0:4], c[1, 0:4]], axis=1), lower], axis=0)
    for i in range(out_ref.shape[0]):
        out_ref[i] = total


def row_tree(with_energy, c, upper_t, g, b):
    return pl.pallas_call(
        functools.partial(row_kernel, with_energy),
        out_shape=[jax.ShapeDtypeStruct((8, 64), F32), jax.ShapeDtypeStruct(c.shape, F32)],
        in_specs=[VM] * 4,
        out_specs=[VM] * 2,
        scratch_shapes=[pltpu.VMEM((c.shape[0], 8, 64), F32)],
        compiler_params=params(),
        name="row_tree",
    )(c, upper_t, g, b)


def upper_levels(cols, levels, x, y, upper_ref, g_ref, b_ref, scratch, with_energy):
    place = own_place(cols)
    level = cols.bit_length() - 2
    c = jnp.stack([x[:, :, 0:64], x[:, :, 64:128]], axis=1).reshape(2 * x.shape[0], 8, 64)
    sums = no_sums()
    while level < levels:
        scratch[0 : c.shape[0]] = c
        y = y + exact_dot(scratch[(place // 2**level) ^ 2], g_ref[level])
        if with_energy:
            sums = pair_energy(c, b_ref[level], sums)
        if level + 1 < levels:
            c = lift(c, upper_ref)
        level += 1
    return y[0:4], sums


SPLITS = 4


def far_of(y, joint_ref, part):
    return join16(dot(y, joint_ref[0, :, part]) + (dot(y, joint_ref[1, :, part]) + dot(y, joint_ref[2, :, part])))


def middle_kernel(
    cols, levels, x_ref, y_ref, upper_ref, g_ref, joint_ref, r_ref, n_ref, valid_ref,
    e_ref, leaf_ref, top_ref, bottom_ref, out_ref, scratch, both,
):
    leaves, _, size = leaf_ref.shape
    own, _ = upper_levels(cols, levels, x_ref[...], y_ref[...], upper_ref, g_ref, None, scratch, False)
    y = rows16(own)
    width = leaves * size // SPLITS
    for k in range(SPLITS):
        part = slice(k * width, (k + 1) * width)
        far = far_of(y, joint_ref, part)
        e = valid_ref[:, part] * (n_ref[:, part] + far)
        e_ref[:, part] = e
        both[0:16, part] = rows16(r_ref[:, part])
        both[16:32, part] = rows16(e)
        for i in range(leaves // SPLITS):
            leaf_ref[k * (leaves // SPLITS) + i] = e[:, i * size : (i + 1) * size]
    edge = top_ref.shape[0]
    top_ref[...] = leaf_ref[0:edge]
    bottom_ref[...] = leaf_ref[leaves - edge : leaves]
    e16 = both[16:32, :]
    c = join16(dot_nt(e16, joint_ref[0]) + (dot_nt(e16, joint_ref[1]) + dot_nt(e16, joint_ref[2])))
    square = dot_nt(both[...], both[...])

    def block(i, j):
        part = join16(square[16 * i : 16 * i + 16, 16 * j : 16 * j + 16])
        return part[:, 0:4] + part[:, 4:8] + part[:, 8:12]

    moments = jnp.concatenate([block(0, 0), block(0, 1), block(1, 1), jnp.zeros((4, 116), F32)], axis=1)
    out_ref[...] = jnp.concatenate([jnp.concatenate([c, jnp.zeros((4, 64), F32)], axis=1), moments], axis=0)


def middle(cols, levels, leaves, edge, x, y, upper_t, g, joint, r, n, valid):
    size = r.shape[1] // leaves
    return pl.pallas_call(
        functools.partial(middle_kernel, cols, levels),
        out_shape=[
            jax.ShapeDtypeStruct(r.shape, F32),
            jax.ShapeDtypeStruct((leaves, 4, size), F32),
            jax.ShapeDtypeStruct((edge, 4, size), F32),
            jax.ShapeDtypeStruct((edge, 4, size), F32),
            jax.ShapeDtypeStruct((8, 128), F32),
        ],
        in_specs=[VM] * 8,
        out_specs=[VM] * 5,
        scratch_shapes=[pltpu.VMEM((2 * x.shape[0], 8, 64), F32), pltpu.VMEM((32, r.shape[1]), BF)],
        compiler_params=params(),
        name="middle",
    )(x, y, upper_t, g, joint, r, n, valid)


def mat_mul(a, b):
    return [[sum(a[i][k] * b[k][j] for k in range(4)) for j in range(4)] for i in range(4)]


def mat_add(a, b):
    return [[a[i][j] + b[i][j] for j in range(4)] for i in range(4)]


def mat_sub(a, b):
    return [[a[i][j] - b[i][j] for j in range(4)] for i in range(4)]


def mat_t(a):
    return [[a[j][i] for j in range(4)] for i in range(4)]


def mat_solve(a, b):
    a = [list(row) for row in a]
    b = [list(row) for row in b]
    width = len(b[0])
    inverse = []
    for col in range(4):
        inverse.append(1.0 / a[col][col])
        for row in range(col + 1, 4):
            factor = a[row][col] * inverse[col]
            for k in range(col + 1, 4):
                a[row][k] = a[row][k] - factor * a[col][k]
            for k in range(width):
                b[row][k] = b[row][k] - factor * b[col][k]
    result = [None] * 4
    for col in reversed(range(4)):
        row = list(b[col])
        for later in range(col + 1, 4):
            row = [row[k] - a[col][later] * result[later][k] for k in range(width)]
        result[col] = [value * inverse[col] for value in row]
    return result


def weights(gram, cross, square, cubic):
    curvature = mat_add(gram, cross)
    both = mat_solve(curvature, [gram[i] + cross[i] for i in range(4)])
    step = [row[0:4] for row in both]
    rest = [row[4:8] for row in both]
    mixed = mat_mul(mat_t(rest), mat_mul(cross, step))
    gram_next = mat_sub(
        mat_add(mat_mul(mat_t(rest), mat_mul(gram, rest)), mat_mul(mat_t(step), mat_mul(square, step))),
        mat_add(mixed, mat_t(mixed)),
    )
    mix = mat_solve(gram, gram_next)
    lead = mat_add(rest, mix)
    second = mat_sub(lead, step)
    with_r = mat_sub(mat_add(mat_mul(gram, lead), mat_mul(cross, second)), mat_mul(square, step))
    with_e = mat_sub(mat_add(mat_mul(mat_t(cross), lead), mat_mul(square, second)), mat_mul(cubic, step))
    curvature_next = mat_sub(mat_mul(mat_t(lead), with_r), mat_mul(mat_t(step), with_e))
    step_next = mat_solve(curvature_next, gram_next)
    lead_step = mat_mul(lead, step_next)
    step_step = mat_mul(step, step_next)
    second_step = mat_sub(lead_step, step_step)
    solution = (mat_add(step, lead_step), [[-v for v in row] for row in step_step], None)
    residual = (mat_sub(rest, lead_step), [[-(step[i][j] + second_step[i][j]) for j in range(4)] for i in range(4)], step_step)
    return solution, residual


def final_kernel(
    cols, levels, c_ref, y_ref, upper_ref, g_ref, b_ref, joint_ref, r_ref, e_ref, n_ref, valid_ref,
    x_ref, out_ref, scratch,
):
    leaves, _, size = x_ref.shape
    c = c_ref[...]
    own, sums = upper_levels(cols, levels, c, y_ref[...], upper_ref, g_ref, b_ref, scratch, True)
    y = rows16(own)
    moments = jnp.sum(c, axis=0)[4:8]
    half = columns_of(sums)

    def matrix(x, at):
        return [[jnp.broadcast_to(x[i : i + 1, at + j : at + j + 1], (1, 128)) for j in range(4)] for i in range(4)]

    half = mat_add(matrix(moments, 16), matrix(half, 0))
    cubic = mat_add(matrix(moments, 12), mat_add(half, mat_t(half)))
    solution, residual = weights(matrix(moments, 0), matrix(moments, 4), matrix(moments, 8), cubic)
    row = lax.broadcasted_iota(jnp.int32, (8, 128), 0)
    col = lax.broadcasted_iota(jnp.int32, (8, 128), 1)
    table = jnp.zeros((8, 128), F32)
    for first, parts in ((0, solution), (4, residual)):
        for k, part in enumerate(parts):
            if part is None:
                continue
            for i in range(4):
                line = jnp.zeros((8, 128), F32)
                for j in range(4):
                    line = jnp.where(row == first + j, part[i][j], line)
                table = jnp.where(col == 4 * k + i, line + table, table)
    table = table[:, 0:16]
    width = leaves * size // SPLITS
    for k in range(SPLITS):
        part = slice(k * width, (k + 1) * width)
        far = far_of(y, joint_ref, part)
        f = valid_ref[:, part] * (n_ref[:, part] + far)
        stacked = jnp.concatenate([r_ref[:, part], e_ref[:, part], f, jnp.zeros_like(f)], axis=0)
        both = jnp.dot(table, stacked, precision=lax.Precision.HIGHEST, preferred_element_type=F32)
        for i in range(leaves // SPLITS):
            x_ref[k * (leaves // SPLITS) + i] = both[0:4, i * size : (i + 1) * size]
            out_ref[k * (leaves // SPLITS) + i] = both[4:8, i * size : (i + 1) * size]


def final(cols, levels, leaves, c, y, upper_t, g, b, joint, r, e, n, valid):
    out = jax.ShapeDtypeStruct((leaves, 4, r.shape[1] // leaves), F32)
    return pl.pallas_call(
        functools.partial(final_kernel, cols, levels),
        out_shape=[out, out],
        in_specs=[VM] * 10,
        out_specs=[VM] * 2,
        scratch_shapes=[pltpu.VMEM((2 * c.shape[0], 8, 64), F32)],
        compiler_params=params(),
        name="final",
    )(c, y, upper_t, g, b, joint, r, e, n, valid)


def swap(axis, first, last):
    count = lax.axis_size(axis)
    up = [(i, i + 1) for i in range(count - 1)]
    down = [(j, i) for i, j in up]
    return lax.ppermute(last, axis, up), lax.ppermute(first, axis, down)


def edges(nx, ny, own, top, bottom, after):
    up, down = swap("gx", top, bottom)
    left, right = swap("gy", *side_columns(nx, ny, own, up, down, after))
    return own, up, down, left, right


def exchange(x, axis):
    return lax.all_to_all(x, axis, 0, 0, tiled=True)


def on_device(points, right_sides, leaf_counts, near_mask, leaf_basis, leaf_transfer, upper_transfer, proxy_nodes):
    nx, ny, _, size = points.shape
    leaves = nx * ny
    rows, cols = lax.axis_size("gx"), lax.axis_size("gy")
    levels = (rows * cols).bit_length() - 2
    target_table, source_table, factor = feature_tables()
    factor = jnp.asarray(np.broadcast_to(factor[:, :, None], (9, 32, size)), BF)

    def flat(x):
        return x.reshape((leaves,) + x.shape[2:])

    packed, top, bottom, r, valid = pack(nx, ny, leaf_counts, jnp.swapaxes(points, 1, 2), flat(right_sides))
    joint, c = upward(r, flat(leaf_basis), flat(leaf_transfer))
    parts = edges(nx, ny, packed, top, bottom, c)
    b, g, upper_t = couplings(levels, cols, (nx, ny), upper_transfer, proxy_nodes)
    s, t, v, *lists, c = geometry(nx, ny, near_mask, parts, target_table, source_table, c, b, cols)
    y, c = row_tree(False, exchange(c, "gy"), upper_t, g, b)
    c = exchange(c, "gx")
    n, cache = near_build(nx, ny, lists, v, s, t, factor, c)
    e, e_leaves, top, bottom, c = middle(cols, levels, leaves, ny, c, y, upper_t, g, joint, r, n, valid)
    n, c = near_reuse(nx, ny, lists, edges(nx, ny, e_leaves, top, bottom, c), c, cache, cols)
    y, c = row_tree(True, exchange(c, "gy"), upper_t, g, b)
    x, out = final(cols, levels, leaves, exchange(c, "gx"), y, upper_t, g, b, joint, r, e, n, valid)
    shape = (nx, ny, 4, size)
    return x.reshape(shape), out.reshape(shape)


def solution(mesh):
    return jax.shard_map(
        on_device,
        mesh=mesh,
        in_specs=(
            P("gx", "gy", None, None),
            P("gx", "gy", None, None),
            P("gx", "gy"),
            P("gx", "gy", None),
            P("gx", "gy", None, None),
            P("gx", "gy", None, None),
            P(),
            P(),
        ),
        out_specs=(P("gx", "gy", None, None), P("gx", "gy", None, None)),
        check_vma=False,
    )
```

```python
import functools

import jax
import jax.numpy as jnp
import numpy as np
from jax import lax
from jax.experimental import pallas as pl
from jax.experimental.pallas import tpu as pltpu
from jax.sharding import PartitionSpec as P

F32 = jnp.float32
BF = jnp.bfloat16
NEAR_LENGTH = 0.5
FAR_LENGTH = 16.0
NEAR_RATE = 3.0**0.5 / NEAR_LENGTH
FAR_RATE = 3.0**0.5 / FAR_LENGTH
LOG2E = 1.4426950408889634
COUPLING_SCALE = 1.0 / 128.0
GROUP = 8
CHUNK = 64
BUILD_SLOTS = 2
READ_SLOTS = 6
VMEM_LIMIT = 20 * 2**20
VM = pl.BlockSpec(memory_space=pltpu.VMEM)
ANY = pl.BlockSpec(memory_space=pl.ANY)
SM = pl.BlockSpec(memory_space=pltpu.SMEM)


def rounded(x):
    return x.astype(BF).astype(F32)


def split2(x):
    high = x.astype(BF)
    return high, (x - high.astype(F32)).astype(BF)


def rows16(x):
    first = rounded(x)
    second = rounded(x - first)
    third = rounded(x - first - second)
    return jnp.concatenate([first, second, third, jnp.zeros_like(x)], axis=0).astype(BF)


def join16(y):
    return y[0:4] + y[4:8] + y[8:12]


def dot(a, b):
    return jnp.dot(a, b, preferred_element_type=F32)


def dot_nt(a, b):
    return lax.dot_general(a, b, (((1,), (1,)), ((), ())), preferred_element_type=F32)


def split3(x):
    first = x.astype(BF)
    rest = x - first.astype(F32)
    second = rest.astype(BF)
    return first, second, (rest - second.astype(F32)).astype(BF)


def exact_dot(a, b):
    return jnp.dot(a, b, precision=lax.Precision.HIGHEST, preferred_element_type=F32)


def feature_tables():
    target = np.zeros((32, 24), np.float32)
    source = np.zeros((32, 24), np.float32)
    factor = np.ones((9, 32), np.float32)
    one = 19
    for c in range(3):
        target[2 * c, c] = target[2 * c + 1, c] = -2
        source[2 * c, c] = source[2 * c + 1, 8 + c] = 1
        target[6 + 2 * c, 8 + c] = target[7 + 2 * c, 8 + c] = -2
        source[6 + 2 * c, c] = source[7 + 2 * c, 8 + c] = 1
    for k in range(3):
        target[12 + k, one] = source[12 + k, 16 + k] = 1
        target[15 + k, 16 + k] = source[15 + k, one] = 1
    for c in range(2):
        target[18 + 2 * c, c] = target[19 + 2 * c, 8 + c] = 1
        source[18 + 2 * c, one] = source[19 + 2 * c, one] = 1
        target[22 + 2 * c, one] = target[23 + 2 * c, one] = 1
        source[22 + 2 * c, c] = source[23 + 2 * c, 8 + c] = 1
    target[26, one] = source[26, one] = 1
    for code in range(9):
        off = (code // 3 - 1, code % 3 - 1)
        for c in range(2):
            factor[code, 18 + 2 * c : 20 + 2 * c] = -2 * off[c]
            factor[code, 22 + 2 * c : 24 + 2 * c] = 2 * off[c]
        factor[code, 26] = off[0] ** 2 + off[1] ** 2
    return target, source, factor


def params():
    return pltpu.CompilerParams(vmem_limit_bytes=VMEM_LIMIT)


def around(nx, ny):
    wide = ny + 2
    return (
        (nx * ny, lambda i: (i // ny + 1) * wide + i % ny + 1),
        (ny, lambda i: i + 1),
        (ny, lambda i: (nx + 1) * wide + i + 1),
        (nx + 2, lambda i: i * wide),
        (nx + 2, lambda i: i * wide + wide - 1),
    )


def each_leaf(nx, ny, refs, body, unroll=4):
    for ref, (count, place) in zip(refs, around(nx, ny)):

        def step(i, carry, ref=ref, place=place):
            body(place(i), ref, i)
            return carry

        lax.fori_loop(0, count, step, 0, unroll=unroll if count % unroll == 0 else 2)


def pack_kernel(nx, ny, count_ref, points_ref, sides_ref, packed_ref, top_ref, bottom_ref, r_ref, valid_ref):
    size = points_ref.shape[3]
    lane = lax.broadcasted_iota(jnp.int32, (1, size), 1)

    def body(a, carry):
        first = (lax.axis_index("gx") * nx + a // ny).astype(F32) + 0.5
        second = (lax.axis_index("gy") * ny + a % ny).astype(F32) + 0.5
        for c, centre in enumerate((first, second, 0.5)):
            packed_ref[a, c : c + 1] = points_ref[a // ny, c, pl.ds(a % ny, 1)] - centre
        count = count_ref[a // ny, a % ny]
        packed_ref[a, 3:4] = jnp.full((1, size), count.astype(F32))
        valid = jnp.where(lane < count, 1.0, 0.0)
        r = jnp.where(valid > 0.0, sides_ref[a], 0.0)
        packed_ref[a, 4:8] = r
        part = pl.ds(pl.multiple_of(a * size, size), size)
        r_ref[:, part] = r
        valid_ref[:, part] = valid
        return carry

    lax.fori_loop(0, nx * ny, body, 0, unroll=4)
    top_ref[...] = packed_ref[0:ny]
    bottom_ref[...] = packed_ref[(nx - 1) * ny : nx * ny]


def pack(nx, ny, counts, points, sides):
    leaves, _, size = sides.shape
    return pl.pallas_call(
        functools.partial(pack_kernel, nx, ny),
        out_shape=[
            jax.ShapeDtypeStruct((leaves, 8, size), F32),
            jax.ShapeDtypeStruct((ny, 8, size), F32),
            jax.ShapeDtypeStruct((ny, 8, size), F32),
            jax.ShapeDtypeStruct((4, leaves * size), F32),
            jax.ShapeDtypeStruct((1, leaves * size), F32),
        ],
        in_specs=[SM, VM, VM],
        out_specs=[VM] * 5,
        compiler_params=params(),
        name="pack",
    )(counts, points, sides)


def sides_kernel(nx, ny, own_ref, up_ref, down_ref, after_ref, left_ref, right_ref):
    for col, ref in ((0, left_ref), (ny - 1, right_ref)):
        ref[0] = up_ref[col]
        ref[nx + 1] = down_ref[col]
        for i in range(nx):
            ref[i + 1] = own_ref[i * ny + col]


def side_columns(nx, ny, own, up, down, after):
    out = jax.ShapeDtypeStruct((nx + 2,) + own.shape[1:], F32)
    return pl.pallas_call(
        functools.partial(sides_kernel, nx, ny),
        out_shape=[out, out],
        in_specs=[VM] * 3 + [ANY],
        out_specs=[VM] * 2,
        compiler_params=params(),
        name="side_columns",
    )(own, up, down, after)


def geometry_kernel(
    nx, ny, mask_ref, own_ref, up_ref, down_ref, left_ref, right_ref, target_ref, source_ref, c_ref, after_ref,
    s_ref, t_ref, v_ref, long_ref, short_ref, groups_ref, out_ref, count_ref,
):
    wide = ny + 2
    leaves = (nx + 2) * wide
    size = own_ref.shape[2]
    row = lax.broadcasted_iota(jnp.int32, (8, size), 0)
    refs = (own_ref, up_ref, down_ref, left_ref, right_ref)

    def read_count(e, ref, i):
        count_ref[e] = ref[i, 3, 0].astype(jnp.int32)

    each_leaf(nx, ny, refs, read_count)

    def features(e, ref, i):
        packed = ref[i]
        x = jnp.where(row < 3, packed, 0.0)
        first = rounded(x)
        second = rounded(x - first)
        held = first + second
        norm = jnp.sum(held * held, axis=0, keepdims=True)
        n1 = rounded(norm)
        n2 = rounded(norm - n1)
        n3 = rounded(norm - n1 - n2)
        last = jnp.where(row == 0, n1, jnp.where(row == 1, n2, jnp.where(row == 2, n3, jnp.where(row == 3, 1.0, 0.0))))
        f = jnp.concatenate([first, second, last], axis=0).astype(BF)
        t_ref[e] = dot(target_ref[...], f).astype(BF)
        s_ref[e] = lax.dot_general(
            f, source_ref[...], (((0,), (1,)), ((), ())), preferred_element_type=F32
        ).astype(BF)
        v_ref[e] = rows16(packed[4:8])

    def note(a, carry):
        features((a // ny + 1) * wide + a % ny + 1, own_ref, a)
        long_count, short_count = carry
        corner = (a // ny) * wide + a % ny
        for code in range(9):
            source = corner + code // 3 * wide + code % 3
            entry = (source * 16 + code) * 64 + a
            on = jnp.where(mask_ref[a // ny, a % ny, code] != 0, 1, 0)
            is_long = jnp.where(count_ref[source] > size - CHUNK, on, 0)
            long_ref[long_count] = entry
            short_ref[short_count] = entry
            long_count = long_count + is_long
            short_count = short_count + (on - is_long)
        return long_count, short_count

    long_count, short_count = lax.fori_loop(0, nx * ny, note, (0, 0), unroll=4)
    for j in range(GROUP):
        long_ref[long_count + j] = leaves * 1024
        short_ref[short_count + j] = leaves * 1024
    groups_ref[0] = (long_count + GROUP - 1) // GROUP
    groups_ref[1] = (short_count + GROUP - 1) // GROUP
    for ref, (count, place) in list(zip(refs, around(nx, ny)))[1:]:

        def step(i, carry, ref=ref, place=place):
            features(place(i), ref, i)
            return carry

        lax.fori_loop(0, count, step, 0, unroll=True)
    v_ref[leaves] = jnp.zeros((16, size), BF)
    for i in range(out_ref.shape[0]):
        out_ref[i] = c_ref[...]


def geometry(nx, ny, mask, parts, target_table, source_table, c, after, copies):
    leaves, size = (nx + 2) * (ny + 2), parts[0].shape[2]
    most = nx * ny * 9 + GROUP
    return pl.pallas_call(
        functools.partial(geometry_kernel, nx, ny),
        out_shape=[
            jax.ShapeDtypeStruct((leaves, size, 32), BF),
            jax.ShapeDtypeStruct((leaves, 32, size), BF),
            jax.ShapeDtypeStruct((leaves + 1, 16, size), BF),
            jax.ShapeDtypeStruct((most,), jnp.int32),
            jax.ShapeDtypeStruct((most,), jnp.int32),
            jax.ShapeDtypeStruct((2,), jnp.int32),
            jax.ShapeDtypeStruct((copies, 8, 128), F32),
        ],
        in_specs=[SM] + [VM] * 8 + [ANY],
        out_specs=[VM] * 3 + [SM] * 3 + [VM],
        scratch_shapes=[pltpu.SMEM((leaves,), jnp.int32)],
        compiler_params=params(),
        name="geometry",
    )(mask, *parts, jnp.asarray(target_table, BF), jnp.asarray(source_table, BF), c, after)


def block_copy(buffer, cache_ref, sems, slots, rows, inward):
    def copy(g):
        slot = g % slots
        here, there = buffer.at[slot], cache_ref.at[g]
        if rows < cache_ref.shape[3]:
            here, there = here.at[:, :, 0:rows], there.at[:, :, 0:rows]
        if inward:
            return pltpu.make_async_copy(there, here, sems.at[slot])
        return pltpu.make_async_copy(here, there, sems.at[slot])

    return copy


def build_kernel(
    nx, ny, long_ref, short_ref, groups_ref, v_ref, s_ref, t_ref, factor_ref, after_ref,
    o_ref, cache_ref, acc, buffer, sems,
):
    wide = ny + 2
    leaves = (nx + 2) * wide
    size = o_ref.shape[1] // (nx * ny)
    short = size - CHUNK
    acc[...] = jnp.zeros_like(acc)
    long_groups = groups_ref[0]
    groups = long_groups + groups_ref[1]
    out_long = block_copy(buffer, cache_ref, sems, BUILD_SLOTS, size, False)
    out_short = block_copy(buffer, cache_ref, sems, BUILD_SLOTS, short, False)

    def wait(g):
        @pl.when(g < long_groups)
        def _():
            out_long(g).wait()

        @pl.when(g >= long_groups)
        def _():
            out_short(g).wait()

    def run(first, last, rows, list_ref, start):
        def group(g, carry):
            slot = g % BUILD_SLOTS

            @pl.when(g >= BUILD_SLOTS)
            def _():
                wait(g - BUILD_SLOTS)

            done = []
            for j in range(GROUP):
                entry = list_ref[(g - first) * GROUP + j]
                a = entry & 63
                code = (entry >> 6) & 15
                source = entry >> 10
                t = t_ref[(a // ny + 1) * wide + a % ny + 1] * factor_ref[code]
                s = s_ref[jnp.minimum(source, leaves - 1)]
                v = v_ref[source]
                total = jnp.zeros((16, size), F32)
                for k in range(rows // CHUNK):
                    part = slice(k * CHUNK, (k + 1) * CHUNK)
                    squared = jnp.maximum(dot(s[part], t), 1e-30)
                    distance = squared * lax.rsqrt(squared)
                    value = (1.0 + NEAR_RATE * distance) * jnp.exp2((-NEAR_RATE * LOG2E) * distance)
                    high, low = split2(value)
                    buffer[slot, j, 0, part] = high
                    buffer[slot, j, 1, part] = low
                    total += dot(v[:, part], high) + dot(v[:, part], low)
                done.append((a, total))
            for a, total in done:
                acc[a] += total
            start(g).start()
            return carry

        lax.fori_loop(first, last, group, 0)

    run(0, long_groups, size, long_ref, out_long)
    run(long_groups, groups, short, short_ref, out_short)
    for back in range(BUILD_SLOTS):
        wait(groups - 1 - back)

    def finish(a, carry):
        o_ref[:, pl.ds(pl.multiple_of(a * size, size), size)] = join16(acc[a]) * (1.0 / size**0.5)
        return carry

    lax.fori_loop(0, nx * ny, finish, 0, unroll=4)


def near_build(nx, ny, lists, v, s, t, factor, after):
    size = v.shape[2]
    most = lists[0].shape[0] // GROUP + 1
    return pl.pallas_call(
        functools.partial(build_kernel, nx, ny),
        out_shape=[
            jax.ShapeDtypeStruct((4, nx * ny * size), F32),
            jax.ShapeDtypeStruct((most, GROUP, 2, size, size), BF),
        ],
        in_specs=[SM] * 3 + [VM] * 4 + [ANY],
        out_specs=[VM, ANY],
        scratch_shapes=[
            pltpu.VMEM((nx * ny, 16, size), F32),
            pltpu.VMEM((BUILD_SLOTS, GROUP, 2, size, size), BF),
            pltpu.SemaphoreType.DMA((BUILD_SLOTS,)),
        ],
        compiler_params=params(),
        name="near_build",
    )(*lists, v, s, t, factor, after)


def reuse_kernel(
    nx, ny, long_ref, short_ref, groups_ref, own_ref, up_ref, down_ref, left_ref, right_ref, c_ref, cache_ref,
    o_ref, out_ref, v16, acc, buffer, sems,
):
    wide = ny + 2
    leaves = (nx + 2) * wide
    size = own_ref.shape[2]
    short = size - CHUNK
    long_groups = groups_ref[0]
    groups = long_groups + groups_ref[1]
    in_long = block_copy(buffer, cache_ref, sems, READ_SLOTS, size, True)
    in_short = block_copy(buffer, cache_ref, sems, READ_SLOTS, short, True)

    def fetch(g):
        @pl.when(g < long_groups)
        def _():
            in_long(g).start()

        @pl.when(jnp.logical_and(g >= long_groups, g < groups))
        def _():
            in_short(g).start()

    for g in range(READ_SLOTS - 1):
        fetch(g)

    def split_leaf(e, ref, i):
        v16[e] = rows16(ref[i])

    each_leaf(nx, ny, (own_ref, up_ref, down_ref, left_ref, right_ref), split_leaf)
    v16[leaves] = jnp.zeros((16, size), BF)
    acc[...] = jnp.zeros_like(acc)

    def run(first, last, rows, list_ref, copy):
        def group(g, carry):
            slot = g % READ_SLOTS
            copy(g).wait()
            fetch(g + READ_SLOTS - 1)
            done = []
            for j in range(GROUP):
                entry = list_ref[(g - first) * GROUP + j]
                v = v16[entry >> 10][:, 0:rows]
                done.append((entry & 63, dot(v, buffer[slot, j, 0, 0:rows]) + dot(v, buffer[slot, j, 1, 0:rows])))
            for a, total in done:
                acc[a] += total
            return carry

        lax.fori_loop(first, last, group, 0)

    run(0, long_groups, size, long_ref, in_long)
    run(long_groups, groups, short, short_ref, in_short)

    def finish(a, sums):
        near = join16(acc[a]) * (1.0 / size**0.5)
        o_ref[:, pl.ds(pl.multiple_of(a * size, size), size)] = near
        v = own_ref[a]
        return tuple(sums[s] + v * near[s : s + 1] for s in range(4))

    sums = lax.fori_loop(0, nx * ny, finish, tuple(jnp.zeros((4, size), F32) for _ in range(4)), unroll=4)
    columns = [jnp.sum(x, axis=1, keepdims=True) for x in sums]
    block = jnp.concatenate([jnp.zeros((4, 12), F32)] + columns + [jnp.zeros((4, 112), F32)], axis=1)
    total = c_ref[...] + jnp.concatenate([jnp.zeros((4, 128), F32), block], axis=0)
    for i in range(out_ref.shape[0]):
        out_ref[i] = total


def near_reuse(nx, ny, lists, parts, c, cache, copies):
    size = parts[0].shape[2]
    leaves = (nx + 2) * (ny + 2)
    return pl.pallas_call(
        functools.partial(reuse_kernel, nx, ny),
        out_shape=[jax.ShapeDtypeStruct((4, nx * ny * size), F32), jax.ShapeDtypeStruct((copies, 8, 128), F32)],
        in_specs=[SM] * 3 + [VM] * 6 + [ANY],
        out_specs=[VM] * 2,
        scratch_shapes=[
            pltpu.VMEM((leaves + 1, 16, size), BF),
            pltpu.VMEM((nx * ny, 16, size), F32),
            pltpu.VMEM((READ_SLOTS,) + cache.shape[1:], BF),
            pltpu.SemaphoreType.DMA((READ_SLOTS,)),
        ],
        compiler_params=params(),
        name="near_reuse",
    )(*lists, *parts, c, cache)


def upward_kernel(r_ref, basis_ref, transfer_ref, joint_ref, c_ref):
    leaves, terms, size = basis_ref.shape

    def body(a, total):
        part = pl.ds(pl.multiple_of(a * size, size), size)
        v = rows16(r_ref[:, part])
        for term, piece in enumerate(split3(exact_dot(transfer_ref[a], basis_ref[a]))):
            joint_ref[term, :, part] = piece
            total = total + dot_nt(v, piece)
        return total

    total = lax.fori_loop(0, leaves, body, jnp.zeros((16, terms), F32), unroll=8)
    total = jnp.concatenate([join16(total), jnp.zeros((4, 128 - terms), F32)], axis=1)
    c_ref[...] = jnp.concatenate([total, jnp.zeros((4, 128), F32)], axis=0)


def upward(r, basis, transfer):
    leaves, terms, size = basis.shape
    return pl.pallas_call(
        upward_kernel,
        out_shape=[
            jax.ShapeDtypeStruct((3, terms, leaves * size), BF),
            jax.ShapeDtypeStruct((8, 128), F32),
        ],
        in_specs=[VM] * 3,
        out_specs=[VM] * 2,
        compiler_params=params(),
        name="upward",
    )(r, basis, transfer)


def own_place(cols):
    return lax.axis_index("gx") * cols + lax.axis_index("gy")


def coupling_kernel(levels, cols, tile, upper_ref, row_ref, b_ref, g_ref, turned_ref):
    place = own_place(cols)
    col_values = jnp.concatenate([row_ref[...], jnp.zeros((5, 64), F32)], axis=0).T
    for k in range(2):
        turned_ref[k] = upper_ref[k].T
    down = None
    for level in range(levels):
        span = 2**level
        extent = (1, span) if span <= cols else (span // cols, cols)
        half = (0.5 * tile[0] * extent[0], 0.5 * tile[1] * extent[1], 0.5)
        apart = (0.0, 2.0 * span * tile[1]) if 2 * span < cols else (2.0 * span / cols * tile[0], 0.0)

        def matrix(sign):
            squared = jnp.zeros((64, 64), F32)
            for c in range(3):
                step = half[c] * (col_values[:, c : c + 1] - row_ref[c : c + 1, :])
                if c < 2:
                    step = step + sign * apart[c]
                squared = squared + step * step
            squared = jnp.maximum(squared, 1e-30)
            scaled = FAR_RATE * (squared * lax.rsqrt(squared))
            return COUPLING_SCALE * ((1.0 + scaled) * jnp.exp(-scaled))

        b_ref[level] = matrix(-1.0)
        upper = (place // (2 * span)) % 2
        own = matrix(jnp.where(upper == 1, -1.0, 1.0))
        g_ref[level] = own if down is None else exact_dot(own, down)
        if level + 1 < levels:
            bit = (place // span) % 2
            step_down = upper_ref[bit]
            down = step_down if down is None else exact_dot(step_down, down)


def couplings(levels, cols, tile, upper, nodes):
    out = jax.ShapeDtypeStruct((levels, 64, 64), F32)
    return pl.pallas_call(
        functools.partial(coupling_kernel, levels, cols, tile),
        out_shape=[out, out, jax.ShapeDtypeStruct(upper.shape, F32)],
        in_specs=[VM] * 2,
        out_specs=[VM] * 3,
        compiler_params=params(),
        name="couplings",
    )(upper, nodes)


def pair_energy(c, b, sums):
    count = c.shape[0]
    quads = c.reshape(count // 4, 4, 8, 64)
    low = quads[:, 0:2].reshape(count // 2 * 8, 64)
    high = quads[:, 2:4].reshape(count // 2, 8, 64)
    carried = exact_dot(low, b).reshape(count // 2, 8, 64)
    return [sums[s] + jnp.sum(carried * high[:, s : s + 1, :], axis=0) for s in range(4)]


def lift(c, upper_t):
    count = c.shape[0]
    paired = c.reshape(count // 2, 2, 8, 64)
    even = paired[:, 0].reshape(count // 2 * 8, 64)
    odd = paired[:, 1].reshape(count // 2 * 8, 64)
    return (exact_dot(even, upper_t[0]) + exact_dot(odd, upper_t[1])).reshape(count // 2, 8, 64)


def no_sums():
    return [jnp.zeros((8, 64), F32) for _ in range(4)]


def columns_of(sums):
    return jnp.concatenate([jnp.sum(x, axis=1, keepdims=True) for x in sums], axis=1)


def row_kernel(with_energy, c_ref, upper_ref, g_ref, b_ref, y_ref, out_ref, scratch):
    x = c_ref[...]
    c = x[:, :, 0:64]
    place = lax.axis_index("gy")
    y = jnp.zeros((8, 64), F32)
    sums = no_sums()
    level = 0
    while c.shape[0] > 2:
        scratch[0 : c.shape[0]] = c
        y = y + exact_dot(scratch[(place // 2**level) ^ 2], g_ref[level])
        if with_energy:
            sums = pair_energy(c, b_ref[level], sums)
        c = lift(c, upper_ref)
        level += 1
    y_ref[...] = y
    lower = jnp.zeros((4, 128), F32)
    if with_energy:
        lower = jnp.sum(x, axis=0)[4:8]
        lower = jnp.concatenate([lower[:, 0:16], columns_of(sums)[0:4], jnp.zeros((4, 108), F32)], axis=1)
    total = jnp.concatenate([jnp.concatenate([c[0, 0:4], c[1, 0:4]], axis=1), lower], axis=0)
    for i in range(out_ref.shape[0]):
        out_ref[i] = total


def row_tree(with_energy, c, upper_t, g, b):
    return pl.pallas_call(
        functools.partial(row_kernel, with_energy),
        out_shape=[jax.ShapeDtypeStruct((8, 64), F32), jax.ShapeDtypeStruct(c.shape, F32)],
        in_specs=[VM] * 4,
        out_specs=[VM] * 2,
        scratch_shapes=[pltpu.VMEM((c.shape[0], 8, 64), F32)],
        compiler_params=params(),
        name="row_tree",
    )(c, upper_t, g, b)


def upper_levels(cols, levels, x, y, upper_ref, g_ref, b_ref, scratch, with_energy):
    place = own_place(cols)
    level = cols.bit_length() - 2
    c = jnp.stack([x[:, :, 0:64], x[:, :, 64:128]], axis=1).reshape(2 * x.shape[0], 8, 64)
    sums = no_sums()
    while level < levels:
        scratch[0 : c.shape[0]] = c
        y = y + exact_dot(scratch[(place // 2**level) ^ 2], g_ref[level])
        if with_energy:
            sums = pair_energy(c, b_ref[level], sums)
        if level + 1 < levels:
            c = lift(c, upper_ref)
        level += 1
    return y[0:4], sums


SPLITS = 4


def far_of(y, joint_ref, part):
    return join16(dot(y, joint_ref[0, :, part]) + (dot(y, joint_ref[1, :, part]) + dot(y, joint_ref[2, :, part])))


def middle_kernel(
    cols, levels, x_ref, y_ref, upper_ref, g_ref, joint_ref, r_ref, n_ref, valid_ref,
    e_ref, leaf_ref, top_ref, bottom_ref, out_ref, scratch, both,
):
    leaves, _, size = leaf_ref.shape
    own, _ = upper_levels(cols, levels, x_ref[...], y_ref[...], upper_ref, g_ref, None, scratch, False)
    y = rows16(own)
    width = leaves * size // SPLITS
    for k in range(SPLITS):
        part = slice(k * width, (k + 1) * width)
        far = far_of(y, joint_ref, part)
        e = valid_ref[:, part] * (n_ref[:, part] + far)
        e_ref[:, part] = e
        both[0:16, part] = rows16(r_ref[:, part])
        both[16:32, part] = rows16(e)
        for i in range(leaves // SPLITS):
            leaf_ref[k * (leaves // SPLITS) + i] = e[:, i * size : (i + 1) * size]
    edge = top_ref.shape[0]
    top_ref[...] = leaf_ref[0:edge]
    bottom_ref[...] = leaf_ref[leaves - edge : leaves]
    e16 = both[16:32, :]
    c = join16(dot_nt(e16, joint_ref[0]) + (dot_nt(e16, joint_ref[1]) + dot_nt(e16, joint_ref[2])))
    square = dot_nt(both[...], both[...])

    def block(i, j):
        part = join16(square[16 * i : 16 * i + 16, 16 * j : 16 * j + 16])
        return part[:, 0:4] + part[:, 4:8] + part[:, 8:12]

    moments = jnp.concatenate([block(0, 0), block(0, 1), block(1, 1), jnp.zeros((4, 116), F32)], axis=1)
    out_ref[...] = jnp.concatenate([jnp.concatenate([c, jnp.zeros((4, 64), F32)], axis=1), moments], axis=0)


def middle(cols, levels, leaves, edge, x, y, upper_t, g, joint, r, n, valid):
    size = r.shape[1] // leaves
    return pl.pallas_call(
        functools.partial(middle_kernel, cols, levels),
        out_shape=[
            jax.ShapeDtypeStruct(r.shape, F32),
            jax.ShapeDtypeStruct((leaves, 4, size), F32),
            jax.ShapeDtypeStruct((edge, 4, size), F32),
            jax.ShapeDtypeStruct((edge, 4, size), F32),
            jax.ShapeDtypeStruct((8, 128), F32),
        ],
        in_specs=[VM] * 8,
        out_specs=[VM] * 5,
        scratch_shapes=[pltpu.VMEM((2 * x.shape[0], 8, 64), F32), pltpu.VMEM((32, r.shape[1]), BF)],
        compiler_params=params(),
        name="middle",
    )(x, y, upper_t, g, joint, r, n, valid)


def mat_mul(a, b):
    return [[sum(a[i][k] * b[k][j] for k in range(4)) for j in range(4)] for i in range(4)]


def mat_add(a, b):
    return [[a[i][j] + b[i][j] for j in range(4)] for i in range(4)]


def mat_sub(a, b):
    return [[a[i][j] - b[i][j] for j in range(4)] for i in range(4)]


def mat_t(a):
    return [[a[j][i] for j in range(4)] for i in range(4)]


def mat_solve(a, b):
    a = [list(row) for row in a]
    b = [list(row) for row in b]
    width = len(b[0])
    inverse = []
    for col in range(4):
        inverse.append(1.0 / a[col][col])
        for row in range(col + 1, 4):
            factor = a[row][col] * inverse[col]
            for k in range(col + 1, 4):
                a[row][k] = a[row][k] - factor * a[col][k]
            for k in range(width):
                b[row][k] = b[row][k] - factor * b[col][k]
    result = [None] * 4
    for col in reversed(range(4)):
        row = list(b[col])
        for later in range(col + 1, 4):
            row = [row[k] - a[col][later] * result[later][k] for k in range(width)]
        result[col] = [value * inverse[col] for value in row]
    return result


def weights(gram, cross, square, cubic):
    curvature = mat_add(gram, cross)
    both = mat_solve(curvature, [gram[i] + cross[i] for i in range(4)])
    step = [row[0:4] for row in both]
    rest = [row[4:8] for row in both]
    mixed = mat_mul(mat_t(rest), mat_mul(cross, step))
    gram_next = mat_sub(
        mat_add(mat_mul(mat_t(rest), mat_mul(gram, rest)), mat_mul(mat_t(step), mat_mul(square, step))),
        mat_add(mixed, mat_t(mixed)),
    )
    mix = mat_solve(gram, gram_next)
    lead = mat_add(rest, mix)
    second = mat_sub(lead, step)
    with_r = mat_sub(mat_add(mat_mul(gram, lead), mat_mul(cross, second)), mat_mul(square, step))
    with_e = mat_sub(mat_add(mat_mul(mat_t(cross), lead), mat_mul(square, second)), mat_mul(cubic, step))
    curvature_next = mat_sub(mat_mul(mat_t(lead), with_r), mat_mul(mat_t(step), with_e))
    step_next = mat_solve(curvature_next, gram_next)
    lead_step = mat_mul(lead, step_next)
    step_step = mat_mul(step, step_next)
    second_step = mat_sub(lead_step, step_step)
    solution = (mat_add(step, lead_step), [[-v for v in row] for row in step_step], None)
    residual = (mat_sub(rest, lead_step), [[-(step[i][j] + second_step[i][j]) for j in range(4)] for i in range(4)], step_step)
    return solution, residual


def final_kernel(
    cols, levels, c_ref, y_ref, upper_ref, g_ref, b_ref, joint_ref, r_ref, e_ref, n_ref, valid_ref,
    x_ref, out_ref, scratch,
):
    leaves, _, size = x_ref.shape
    c = c_ref[...]
    own, sums = upper_levels(cols, levels, c, y_ref[...], upper_ref, g_ref, b_ref, scratch, True)
    y = rows16(own)
    moments = jnp.sum(c, axis=0)[4:8]
    half = columns_of(sums)

    def matrix(x, at):
        return [[jnp.broadcast_to(x[i : i + 1, at + j : at + j + 1], (1, 128)) for j in range(4)] for i in range(4)]

    half = mat_add(matrix(moments, 16), matrix(half, 0))
    cubic = mat_add(matrix(moments, 12), mat_add(half, mat_t(half)))
    solution, residual = weights(matrix(moments, 0), matrix(moments, 4), matrix(moments, 8), cubic)
    row = lax.broadcasted_iota(jnp.int32, (8, 128), 0)
    col = lax.broadcasted_iota(jnp.int32, (8, 128), 1)
    table = jnp.zeros((8, 128), F32)
    for first, parts in ((0, solution), (4, residual)):
        for k, part in enumerate(parts):
            if part is None:
                continue
            for i in range(4):
                line = jnp.zeros((8, 128), F32)
                for j in range(4):
                    line = jnp.where(row == first + j, part[i][j], line)
                table = jnp.where(col == 4 * k + i, line + table, table)
    table = table[:, 0:16]
    width = leaves * size // SPLITS
    for k in range(SPLITS):
        part = slice(k * width, (k + 1) * width)
        far = far_of(y, joint_ref, part)
        f = valid_ref[:, part] * (n_ref[:, part] + far)
        stacked = jnp.concatenate([r_ref[:, part], e_ref[:, part], f, jnp.zeros_like(f)], axis=0)
        both = jnp.dot(table, stacked, precision=lax.Precision.HIGHEST, preferred_element_type=F32)
        for i in range(leaves // SPLITS):
            x_ref[k * (leaves // SPLITS) + i] = both[0:4, i * size : (i + 1) * size]
            out_ref[k * (leaves // SPLITS) + i] = both[4:8, i * size : (i + 1) * size]


def final(cols, levels, leaves, c, y, upper_t, g, b, joint, r, e, n, valid):
    out = jax.ShapeDtypeStruct((leaves, 4, r.shape[1] // leaves), F32)
    return pl.pallas_call(
        functools.partial(final_kernel, cols, levels),
        out_shape=[out, out],
        in_specs=[VM] * 10,
        out_specs=[VM] * 2,
        scratch_shapes=[pltpu.VMEM((2 * c.shape[0], 8, 64), F32)],
        compiler_params=params(),
        name="final",
    )(c, y, upper_t, g, b, joint, r, e, n, valid)


def swap(axis, first, last):
    count = lax.axis_size(axis)
    up = [(i, (i + 1) % count) for i in range(count)]
    down = [(j, i) for i, j in up]
    return lax.ppermute(last, axis, up), lax.ppermute(first, axis, down)


def edges(nx, ny, own, top, bottom, after):
    up, down = swap("gx", top, bottom)
    left, right = swap("gy", *side_columns(nx, ny, own, up, down, after))
    return own, up, down, left, right


def exchange(x, axis):
    return lax.all_to_all(x, axis, 0, 0, tiled=True)


def on_device(points, right_sides, leaf_counts, near_mask, leaf_basis, leaf_transfer, upper_transfer, proxy_nodes):
    nx, ny, _, size = points.shape
    leaves = nx * ny
    rows, cols = lax.axis_size("gx"), lax.axis_size("gy")
    levels = (rows * cols).bit_length() - 2
    target_table, source_table, factor = feature_tables()
    factor = jnp.asarray(np.broadcast_to(factor[:, :, None], (9, 32, size)), BF)

    def flat(x):
        return x.reshape((leaves,) + x.shape[2:])

    packed, top, bottom, r, valid = pack(nx, ny, leaf_counts, jnp.swapaxes(points, 1, 2), flat(right_sides))
    joint, c = upward(r, flat(leaf_basis), flat(leaf_transfer))
    parts = edges(nx, ny, packed, top, bottom, c)
    b, g, upper_t = couplings(levels, cols, (nx, ny), upper_transfer, proxy_nodes)
    s, t, v, *lists, c = geometry(nx, ny, near_mask, parts, target_table, source_table, c, b, cols)
    y, c = row_tree(False, exchange(c, "gy"), upper_t, g, b)
    c = exchange(c, "gx")
    n, cache = near_build(nx, ny, lists, v, s, t, factor, c)
    e, e_leaves, top, bottom, c = middle(cols, levels, leaves, ny, c, y, upper_t, g, joint, r, n, valid)
    n, c = near_reuse(nx, ny, lists, edges(nx, ny, e_leaves, top, bottom, c), c, cache, cols)
    y, c = row_tree(True, exchange(c, "gy"), upper_t, g, b)
    x, out = final(cols, levels, leaves, exchange(c, "gx"), y, upper_t, g, b, joint, r, e, n, valid)
    shape = (nx, ny, 4, size)
    return x.reshape(shape), out.reshape(shape)


def solution(mesh):
    return jax.shard_map(
        on_device,
        mesh=mesh,
        in_specs=(
            P("gx", "gy", None, None),
            P("gx", "gy", None, None),
            P("gx", "gy"),
            P("gx", "gy", None),
            P("gx", "gy", None, None),
            P("gx", "gy", None, None),
            P(),
            P(),
        ),
        out_specs=(P("gx", "gy", None, None), P("gx", "gy", None, None)),
        check_vma=False,
    )
```

```python
import functools

import jax
import jax.numpy as jnp
import numpy as np
from jax import lax
from jax.experimental import pallas as pl
from jax.experimental.pallas import tpu as pltpu
from jax.sharding import PartitionSpec as P

F32 = jnp.float32
BF = jnp.bfloat16
NEAR_LENGTH = 0.5
FAR_LENGTH = 16.0
NEAR_RATE = 3.0**0.5 / NEAR_LENGTH
FAR_RATE = 3.0**0.5 / FAR_LENGTH
LOG2E = 1.4426950408889634
COUPLING_SCALE = 1.0 / 128.0
GROUP = 8
CHUNK = 64
BUILD_SLOTS = 2
READ_SLOTS = 6
VMEM_LIMIT = 20 * 2**20
VM = pl.BlockSpec(memory_space=pltpu.VMEM)
ANY = pl.BlockSpec(memory_space=pl.ANY)
SM = pl.BlockSpec(memory_space=pltpu.SMEM)


def rounded(x):
    return x.astype(BF).astype(F32)


def split2(x):
    high = x.astype(BF)
    return high, (x - high.astype(F32)).astype(BF)


def rows16(x):
    first = rounded(x)
    second = rounded(x - first)
    third = rounded(x - first - second)
    return jnp.concatenate([first, second, third, jnp.zeros_like(x)], axis=0).astype(BF)


def join16(y):
    return y[0:4] + y[4:8] + y[8:12]


def dot(a, b):
    return jnp.dot(a, b, preferred_element_type=F32)


def dot_nt(a, b):
    return lax.dot_general(a, b, (((1,), (1,)), ((), ())), preferred_element_type=F32)


def split3(x):
    first = x.astype(BF)
    rest = x - first.astype(F32)
    second = rest.astype(BF)
    return first, second, (rest - second.astype(F32)).astype(BF)


def exact_dot(a, b):
    return jnp.dot(a, b, precision=lax.Precision.HIGHEST, preferred_element_type=F32)


def feature_tables():
    target = np.zeros((32, 24), np.float32)
    source = np.zeros((32, 24), np.float32)
    factor = np.ones((9, 32), np.float32)
    one = 19
    for c in range(3):
        target[2 * c, c] = target[2 * c + 1, c] = -2
        source[2 * c, c] = source[2 * c + 1, 8 + c] = 1
        target[6 + 2 * c, 8 + c] = target[7 + 2 * c, 8 + c] = -2
        source[6 + 2 * c, c] = source[7 + 2 * c, 8 + c] = 1
    for k in range(3):
        target[12 + k, one] = source[12 + k, 16 + k] = 1
        target[15 + k, 16 + k] = source[15 + k, one] = 1
    for c in range(2):
        target[18 + 2 * c, c] = target[19 + 2 * c, 8 + c] = 1
        source[18 + 2 * c, one] = source[19 + 2 * c, one] = 1
        target[22 + 2 * c, one] = target[23 + 2 * c, one] = 1
        source[22 + 2 * c, c] = source[23 + 2 * c, 8 + c] = 1
    target[26, one] = source[26, one] = 1
    for code in range(9):
        off = (code // 3 - 1, code % 3 - 1)
        for c in range(2):
            factor[code, 18 + 2 * c : 20 + 2 * c] = -2 * off[c]
            factor[code, 22 + 2 * c : 24 + 2 * c] = 2 * off[c]
        factor[code, 26] = off[0] ** 2 + off[1] ** 2
    return target, source, factor


def params():
    return pltpu.CompilerParams(vmem_limit_bytes=VMEM_LIMIT)


def around(nx, ny):
    wide = ny + 2
    return (
        (nx * ny, lambda i: (i // ny + 1) * wide + i % ny + 1),
        (ny, lambda i: i + 1),
        (ny, lambda i: (nx + 1) * wide + i + 1),
        (nx + 2, lambda i: i * wide),
        (nx + 2, lambda i: i * wide + wide - 1),
    )


def each_leaf(nx, ny, refs, body, unroll=4):
    for ref, (count, place) in zip(refs, around(nx, ny)):

        def step(i, carry, ref=ref, place=place):
            body(place(i), ref, i)
            return carry

        lax.fori_loop(0, count, step, 0, unroll=unroll if count % unroll == 0 else 2)


def pack_kernel(nx, ny, count_ref, points_ref, sides_ref, packed_ref, top_ref, bottom_ref, r_ref, valid_ref):
    size = points_ref.shape[3]
    lane = lax.broadcasted_iota(jnp.int32, (1, size), 1)

    def body(a, carry):
        first = (lax.axis_index("gx") * nx + a // ny).astype(F32) + 0.5
        second = (lax.axis_index("gy") * ny + a % ny).astype(F32) + 0.5
        for c, centre in enumerate((first, second, 0.5)):
            packed_ref[a, c : c + 1] = points_ref[a // ny, c, pl.ds(a % ny, 1)] - centre
        count = count_ref[a // ny, a % ny]
        packed_ref[a, 3:4] = jnp.full((1, size), count.astype(F32))
        valid = jnp.where(lane < count, 1.0, 0.0)
        r = jnp.where(valid > 0.0, sides_ref[a], 0.0)
        packed_ref[a, 4:8] = r
        part = pl.ds(pl.multiple_of(a * size, size), size)
        r_ref[:, part] = r
        valid_ref[:, part] = valid
        return carry

    lax.fori_loop(0, nx * ny, body, 0, unroll=4)
    top_ref[...] = packed_ref[0:ny]
    bottom_ref[...] = packed_ref[(nx - 1) * ny : nx * ny]


def pack(nx, ny, counts, points, sides):
    leaves, _, size = sides.shape
    return pl.pallas_call(
        functools.partial(pack_kernel, nx, ny),
        out_shape=[
            jax.ShapeDtypeStruct((leaves, 8, size), F32),
            jax.ShapeDtypeStruct((ny, 8, size), F32),
            jax.ShapeDtypeStruct((ny, 8, size), F32),
            jax.ShapeDtypeStruct((4, leaves * size), F32),
            jax.ShapeDtypeStruct((1, leaves * size), F32),
        ],
        in_specs=[SM, VM, VM],
        out_specs=[VM] * 5,
        compiler_params=params(),
        name="pack",
    )(counts, points, sides)


def sides_kernel(nx, ny, own_ref, up_ref, down_ref, after_ref, left_ref, right_ref):
    for col, ref in ((0, left_ref), (ny - 1, right_ref)):
        ref[0] = up_ref[col]
        ref[nx + 1] = down_ref[col]
        for i in range(nx):
            ref[i + 1] = own_ref[i * ny + col]


def side_columns(nx, ny, own, up, down, after):
    out = jax.ShapeDtypeStruct((nx + 2,) + own.shape[1:], F32)
    return pl.pallas_call(
        functools.partial(sides_kernel, nx, ny),
        out_shape=[out, out],
        in_specs=[VM] * 3 + [ANY],
        out_specs=[VM] * 2,
        compiler_params=params(),
        name="side_columns",
    )(own, up, down, after)


def geometry_kernel(
    nx, ny, mask_ref, own_ref, up_ref, down_ref, left_ref, right_ref, target_ref, source_ref, c_ref, after_ref,
    s_ref, t_ref, v_ref, long_ref, short_ref, groups_ref, out_ref, count_ref,
):
    wide = ny + 2
    leaves = (nx + 2) * wide
    size = own_ref.shape[2]
    row = lax.broadcasted_iota(jnp.int32, (8, size), 0)
    refs = (own_ref, up_ref, down_ref, left_ref, right_ref)

    def read_count(e, ref, i):
        count_ref[e] = ref[i, 3, 0].astype(jnp.int32)

    each_leaf(nx, ny, refs, read_count)

    def features(e, ref, i):
        packed = ref[i]
        x = jnp.where(row < 3, packed, 0.0)
        first = rounded(x)
        second = rounded(x - first)
        held = first + second
        norm = jnp.sum(held * held, axis=0, keepdims=True)
        n1 = rounded(norm)
        n2 = rounded(norm - n1)
        n3 = rounded(norm - n1 - n2)
        last = jnp.where(row == 0, n1, jnp.where(row == 1, n2, jnp.where(row == 2, n3, jnp.where(row == 3, 1.0, 0.0))))
        f = jnp.concatenate([first, second, last], axis=0).astype(BF)
        t_ref[e] = dot(target_ref[...], f).astype(BF)
        s_ref[e] = lax.dot_general(
            f, source_ref[...], (((0,), (1,)), ((), ())), preferred_element_type=F32
        ).astype(BF)
        v_ref[e] = rows16(packed[4:8])

    def note(a, carry):
        features((a // ny + 1) * wide + a % ny + 1, own_ref, a)
        long_count, short_count = carry
        corner = (a // ny) * wide + a % ny
        for code in range(9):
            source = corner + code // 3 * wide + code % 3
            entry = (source * 16 + code) * 64 + a
            on = jnp.where(mask_ref[a // ny, a % ny, code] != 0, 1, 0)
            is_long = jnp.where(count_ref[source] > size - CHUNK, on, 0)
            long_ref[long_count] = entry
            short_ref[short_count] = entry
            long_count = long_count + is_long
            short_count = short_count + (on - is_long)
        return long_count, short_count

    long_count, short_count = lax.fori_loop(0, nx * ny, note, (0, 0), unroll=8)
    for j in range(GROUP):
        long_ref[long_count + j] = leaves * 1024
        short_ref[short_count + j] = leaves * 1024
    groups_ref[0] = (long_count + GROUP - 1) // GROUP
    groups_ref[1] = (short_count + GROUP - 1) // GROUP
    for ref, (count, place) in list(zip(refs, around(nx, ny)))[1:]:

        def step(i, carry, ref=ref, place=place):
            features(place(i), ref, i)
            return carry

        lax.fori_loop(0, count, step, 0, unroll=True)
    v_ref[leaves] = jnp.zeros((16, size), BF)
    for i in range(out_ref.shape[0]):
        out_ref[i] = c_ref[...]


def geometry(nx, ny, mask, parts, target_table, source_table, c, after, copies):
    leaves, size = (nx + 2) * (ny + 2), parts[0].shape[2]
    most = nx * ny * 9 + GROUP
    return pl.pallas_call(
        functools.partial(geometry_kernel, nx, ny),
        out_shape=[
            jax.ShapeDtypeStruct((leaves, size, 32), BF),
            jax.ShapeDtypeStruct((leaves, 32, size), BF),
            jax.ShapeDtypeStruct((leaves + 1, 16, size), BF),
            jax.ShapeDtypeStruct((most,), jnp.int32),
            jax.ShapeDtypeStruct((most,), jnp.int32),
            jax.ShapeDtypeStruct((2,), jnp.int32),
            jax.ShapeDtypeStruct((copies, 8, 128), F32),
        ],
        in_specs=[SM] + [VM] * 8 + [ANY],
        out_specs=[VM] * 3 + [SM] * 3 + [VM],
        scratch_shapes=[pltpu.SMEM((leaves,), jnp.int32)],
        compiler_params=params(),
        name="geometry",
    )(mask, *parts, jnp.asarray(target_table, BF), jnp.asarray(source_table, BF), c, after)


def block_copy(buffer, cache_ref, sems, slots, rows, inward):
    def copy(g):
        slot = g % slots
        here, there = buffer.at[slot], cache_ref.at[g]
        if rows < cache_ref.shape[3]:
            here, there = here.at[:, :, 0:rows], there.at[:, :, 0:rows]
        if inward:
            return pltpu.make_async_copy(there, here, sems.at[slot])
        return pltpu.make_async_copy(here, there, sems.at[slot])

    return copy


def build_kernel(
    nx, ny, long_ref, short_ref, groups_ref, v_ref, s_ref, t_ref, factor_ref, after_ref,
    o_ref, cache_ref, acc, buffer, sems,
):
    wide = ny + 2
    leaves = (nx + 2) * wide
    size = o_ref.shape[1] // (nx * ny)
    short = size - CHUNK
    acc[...] = jnp.zeros_like(acc)
    long_groups = groups_ref[0]
    groups = long_groups + groups_ref[1]
    out_long = block_copy(buffer, cache_ref, sems, BUILD_SLOTS, size, False)
    out_short = block_copy(buffer, cache_ref, sems, BUILD_SLOTS, short, False)

    def wait(g):
        @pl.when(g < long_groups)
        def _():
            out_long(g).wait()

        @pl.when(g >= long_groups)
        def _():
            out_short(g).wait()

    def run(first, last, rows, list_ref, start):
        def group(g, carry):
            slot = g % BUILD_SLOTS

            @pl.when(g >= BUILD_SLOTS)
            def _():
                wait(g - BUILD_SLOTS)

            done = []
            for j in range(GROUP):
                entry = list_ref[(g - first) * GROUP + j]
                a = entry & 63
                code = (entry >> 6) & 15
                source = entry >> 10
                t = t_ref[(a // ny + 1) * wide + a % ny + 1] * factor_ref[code]
                s = s_ref[jnp.minimum(source, leaves - 1)]
                v = v_ref[source]
                total = jnp.zeros((16, size), F32)
                for k in range(rows // CHUNK):
                    part = slice(k * CHUNK, (k + 1) * CHUNK)
                    squared = jnp.maximum(dot(s[part], t), 1e-30)
                    distance = squared * lax.rsqrt(squared)
                    value = (1.0 + NEAR_RATE * distance) * jnp.exp2((-NEAR_RATE * LOG2E) * distance)
                    high, low = split2(value)
                    buffer[slot, j, 0, part] = high
                    buffer[slot, j, 1, part] = low
                    total += dot(v[:, part], high) + dot(v[:, part], low)
                done.append((a, total))
            for a, total in done:
                acc[a] += total
            start(g).start()
            return carry

        lax.fori_loop(first, last, group, 0)

    run(0, long_groups, size, long_ref, out_long)
    run(long_groups, groups, short, short_ref, out_short)
    for back in range(BUILD_SLOTS):
        wait(groups - 1 - back)

    def finish(a, carry):
        o_ref[:, pl.ds(pl.multiple_of(a * size, size), size)] = join16(acc[a]) * (1.0 / size**0.5)
        return carry

    lax.fori_loop(0, nx * ny, finish, 0, unroll=4)


def near_build(nx, ny, lists, v, s, t, factor, after):
    size = v.shape[2]
    most = lists[0].shape[0] // GROUP + 1
    return pl.pallas_call(
        functools.partial(build_kernel, nx, ny),
        out_shape=[
            jax.ShapeDtypeStruct((4, nx * ny * size), F32),
            jax.ShapeDtypeStruct((most, GROUP, 2, size, size), BF),
        ],
        in_specs=[SM] * 3 + [VM] * 4 + [ANY],
        out_specs=[VM, ANY],
        scratch_shapes=[
            pltpu.VMEM((nx * ny, 16, size), F32),
            pltpu.VMEM((BUILD_SLOTS, GROUP, 2, size, size), BF),
            pltpu.SemaphoreType.DMA((BUILD_SLOTS,)),
        ],
        compiler_params=params(),
        name="near_build",
    )(*lists, v, s, t, factor, after)


def reuse_kernel(
    nx, ny, long_ref, short_ref, groups_ref, own_ref, up_ref, down_ref, left_ref, right_ref, c_ref, cache_ref,
    o_ref, out_ref, v16, acc, buffer, sems,
):
    wide = ny + 2
    leaves = (nx + 2) * wide
    size = own_ref.shape[2]
    short = size - CHUNK
    long_groups = groups_ref[0]
    groups = long_groups + groups_ref[1]
    in_long = block_copy(buffer, cache_ref, sems, READ_SLOTS, size, True)
    in_short = block_copy(buffer, cache_ref, sems, READ_SLOTS, short, True)

    def fetch(g):
        @pl.when(g < long_groups)
        def _():
            in_long(g).start()

        @pl.when(jnp.logical_and(g >= long_groups, g < groups))
        def _():
            in_short(g).start()

    for g in range(READ_SLOTS - 1):
        fetch(g)

    def split_leaf(e, ref, i):
        v16[e] = rows16(ref[i])

    each_leaf(nx, ny, (own_ref, up_ref, down_ref, left_ref, right_ref), split_leaf)
    v16[leaves] = jnp.zeros((16, size), BF)
    acc[...] = jnp.zeros_like(acc)

    def run(first, last, rows, list_ref, copy):
        def group(g, carry):
            slot = g % READ_SLOTS
            copy(g).wait()
            fetch(g + READ_SLOTS - 1)
            done = []
            for j in range(GROUP):
                entry = list_ref[(g - first) * GROUP + j]
                v = v16[entry >> 10][:, 0:rows]
                done.append((entry & 63, dot(v, buffer[slot, j, 0, 0:rows]) + dot(v, buffer[slot, j, 1, 0:rows])))
            for a, total in done:
                acc[a] += total
            return carry

        lax.fori_loop(first, last, group, 0)

    run(0, long_groups, size, long_ref, in_long)
    run(long_groups, groups, short, short_ref, in_short)

    def finish(a, sums):
        near = join16(acc[a]) * (1.0 / size**0.5)
        o_ref[:, pl.ds(pl.multiple_of(a * size, size), size)] = near
        v = own_ref[a]
        return tuple(sums[s] + v * near[s : s + 1] for s in range(4))

    sums = lax.fori_loop(0, nx * ny, finish, tuple(jnp.zeros((4, size), F32) for _ in range(4)), unroll=4)
    columns = [jnp.sum(x, axis=1, keepdims=True) for x in sums]
    block = jnp.concatenate([jnp.zeros((4, 12), F32)] + columns + [jnp.zeros((4, 112), F32)], axis=1)
    total = c_ref[...] + jnp.concatenate([jnp.zeros((4, 128), F32), block], axis=0)
    for i in range(out_ref.shape[0]):
        out_ref[i] = total


def near_reuse(nx, ny, lists, parts, c, cache, copies):
    size = parts[0].shape[2]
    leaves = (nx + 2) * (ny + 2)
    return pl.pallas_call(
        functools.partial(reuse_kernel, nx, ny),
        out_shape=[jax.ShapeDtypeStruct((4, nx * ny * size), F32), jax.ShapeDtypeStruct((copies, 8, 128), F32)],
        in_specs=[SM] * 3 + [VM] * 6 + [ANY],
        out_specs=[VM] * 2,
        scratch_shapes=[
            pltpu.VMEM((leaves + 1, 16, size), BF),
            pltpu.VMEM((nx * ny, 16, size), F32),
            pltpu.VMEM((READ_SLOTS,) + cache.shape[1:], BF),
            pltpu.SemaphoreType.DMA((READ_SLOTS,)),
        ],
        compiler_params=params(),
        name="near_reuse",
    )(*lists, *parts, c, cache)


def upward_kernel(r_ref, basis_ref, transfer_ref, joint_ref, c_ref):
    leaves, terms, size = basis_ref.shape

    def body(a, total):
        part = pl.ds(pl.multiple_of(a * size, size), size)
        v = rows16(r_ref[:, part])
        for term, piece in enumerate(split3(exact_dot(transfer_ref[a], basis_ref[a]))):
            joint_ref[term, :, part] = piece
            total = total + dot_nt(v, piece)
        return total

    total = lax.fori_loop(0, leaves, body, jnp.zeros((16, terms), F32), unroll=16)
    total = jnp.concatenate([join16(total), jnp.zeros((4, 128 - terms), F32)], axis=1)
    c_ref[...] = jnp.concatenate([total, jnp.zeros((4, 128), F32)], axis=0)


def upward(r, basis, transfer):
    leaves, terms, size = basis.shape
    return pl.pallas_call(
        upward_kernel,
        out_shape=[
            jax.ShapeDtypeStruct((3, terms, leaves * size), BF),
            jax.ShapeDtypeStruct((8, 128), F32),
        ],
        in_specs=[VM] * 3,
        out_specs=[VM] * 2,
        compiler_params=params(),
        name="upward",
    )(r, basis, transfer)


def own_place(cols):
    return lax.axis_index("gx") * cols + lax.axis_index("gy")


def coupling_kernel(levels, cols, tile, upper_ref, row_ref, b_ref, g_ref, turned_ref):
    place = own_place(cols)
    col_values = jnp.concatenate([row_ref[...], jnp.zeros((5, 64), F32)], axis=0).T
    for k in range(2):
        turned_ref[k] = upper_ref[k].T
    down = None
    for level in range(levels):
        span = 2**level
        extent = (1, span) if span <= cols else (span // cols, cols)
        half = (0.5 * tile[0] * extent[0], 0.5 * tile[1] * extent[1], 0.5)
        apart = (0.0, 2.0 * span * tile[1]) if 2 * span < cols else (2.0 * span / cols * tile[0], 0.0)

        def matrix(sign):
            squared = jnp.zeros((64, 64), F32)
            for c in range(3):
                step = half[c] * (col_values[:, c : c + 1] - row_ref[c : c + 1, :])
                if c < 2:
                    step = step + sign * apart[c]
                squared = squared + step * step
            squared = jnp.maximum(squared, 1e-30)
            scaled = FAR_RATE * (squared * lax.rsqrt(squared))
            return COUPLING_SCALE * ((1.0 + scaled) * jnp.exp(-scaled))

        b_ref[level] = matrix(-1.0)
        upper = (place // (2 * span)) % 2
        own = matrix(jnp.where(upper == 1, -1.0, 1.0))
        g_ref[level] = own if down is None else exact_dot(own, down)
        if level + 1 < levels:
            bit = (place // span) % 2
            step_down = upper_ref[bit]
            down = step_down if down is None else exact_dot(step_down, down)


def couplings(levels, cols, tile, upper, nodes):
    out = jax.ShapeDtypeStruct((levels, 64, 64), F32)
    return pl.pallas_call(
        functools.partial(coupling_kernel, levels, cols, tile),
        out_shape=[out, out, jax.ShapeDtypeStruct(upper.shape, F32)],
        in_specs=[VM] * 2,
        out_specs=[VM] * 3,
        compiler_params=params(),
        name="couplings",
    )(upper, nodes)


def pair_energy(c, b, sums):
    count = c.shape[0]
    quads = c.reshape(count // 4, 4, 8, 64)
    low = quads[:, 0:2].reshape(count // 2 * 8, 64)
    high = quads[:, 2:4].reshape(count // 2, 8, 64)
    carried = exact_dot(low, b).reshape(count // 2, 8, 64)
    return [sums[s] + jnp.sum(carried * high[:, s : s + 1, :], axis=0) for s in range(4)]


def lift(c, upper_t):
    count = c.shape[0]
    paired = c.reshape(count // 2, 2, 8, 64)
    even = paired[:, 0].reshape(count // 2 * 8, 64)
    odd = paired[:, 1].reshape(count // 2 * 8, 64)
    return (exact_dot(even, upper_t[0]) + exact_dot(odd, upper_t[1])).reshape(count // 2, 8, 64)


def no_sums():
    return [jnp.zeros((8, 64), F32) for _ in range(4)]


def columns_of(sums):
    return jnp.concatenate([jnp.sum(x, axis=1, keepdims=True) for x in sums], axis=1)


def row_kernel(with_energy, c_ref, upper_ref, g_ref, b_ref, y_ref, out_ref, scratch):
    x = c_ref[...]
    c = x[:, :, 0:64]
    place = lax.axis_index("gy")
    y = jnp.zeros((8, 64), F32)
    sums = no_sums()
    level = 0
    while c.shape[0] > 2:
        scratch[0 : c.shape[0]] = c
        y = y + exact_dot(scratch[(place // 2**level) ^ 2], g_ref[level])
        if with_energy:
            sums = pair_energy(c, b_ref[level], sums)
        c = lift(c, upper_ref)
        level += 1
    y_ref[...] = y
    if not with_energy:
        lower = jnp.max(jnp.max(jnp.abs(x), axis=0), axis=1, keepdims=True)
        lower = jnp.broadcast_to(jnp.max(lower, axis=0, keepdims=True), (4, 128))
    else:
        lower = jnp.sum(x, axis=0)[4:8]
        lower = jnp.concatenate([lower[:, 0:16], columns_of(sums)[0:4], jnp.zeros((4, 108), F32)], axis=1)
    total = jnp.concatenate([jnp.concatenate([c[0, 0:4], c[1, 0:4]], axis=1), lower], axis=0)
    for i in range(out_ref.shape[0]):
        out_ref[i] = total


def row_tree(with_energy, c, upper_t, g, b):
    return pl.pallas_call(
        functools.partial(row_kernel, with_energy),
        out_shape=[jax.ShapeDtypeStruct((8, 64), F32), jax.ShapeDtypeStruct(c.shape, F32)],
        in_specs=[VM] * 4,
        out_specs=[VM] * 2,
        scratch_shapes=[pltpu.VMEM((c.shape[0], 8, 64), F32)],
        compiler_params=params(),
        name="row_tree",
    )(c, upper_t, g, b)


def upper_levels(cols, levels, x, y, upper_ref, g_ref, b_ref, scratch, with_energy):
    place = own_place(cols)
    level = cols.bit_length() - 2
    c = jnp.stack([x[:, :, 0:64], x[:, :, 64:128]], axis=1).reshape(2 * x.shape[0], 8, 64)
    sums = no_sums()
    while level < levels:
        scratch[0 : c.shape[0]] = c
        y = y + exact_dot(scratch[(place // 2**level) ^ 2], g_ref[level])
        if with_energy:
            sums = pair_energy(c, b_ref[level], sums)
        if level + 1 < levels:
            c = lift(c, upper_ref)
        level += 1
    return y[0:4], sums


SPLITS = 4


def far_of(y, joint_ref, part):
    return join16(dot(y, joint_ref[0, :, part]) + (dot(y, joint_ref[1, :, part]) + dot(y, joint_ref[2, :, part])))


def scale_of(x, upper_ref, levels):
    largest = jnp.max(jnp.max(x[:, 4:8], axis=0), axis=0, keepdims=True)
    sizes = jnp.abs(upper_ref[...])
    up = jnp.max(jnp.sum(sizes[0] + sizes[1], axis=0, keepdims=True), axis=1, keepdims=True)
    down = jnp.max(jnp.max(jnp.sum(sizes, axis=2, keepdims=True), axis=0), axis=0, keepdims=True)
    growth = jnp.ones((1, 1), F32)
    for _ in range(levels - 1):
        growth = 1.0 + growth * (up * down)
    bound = 864.0 + 576.0 * (growth * largest)
    power = jnp.ones_like(bound)
    scale = jnp.full_like(bound, 2.0**48)
    inverse = jnp.full_like(bound, 2.0**-48)
    for k in (64, 32, 16, 8, 4, 2):
        fits = bound >= power * 2.0**k
        power = jnp.where(fits, power * 2.0**k, power)
        scale = jnp.where(fits, scale * 2.0 ** (-1.5 * k), scale)
        inverse = jnp.where(fits, inverse * 2.0 ** (1.5 * k), inverse)
    return jnp.minimum(scale, 1.0), jnp.maximum(inverse, 1.0)


def middle_kernel(
    cols, levels, x_ref, y_ref, upper_ref, g_ref, joint_ref, r_ref, n_ref, valid_ref,
    e_ref, leaf_ref, top_ref, bottom_ref, out_ref, scale_ref, scratch, both,
):
    leaves, _, size = leaf_ref.shape
    own, _ = upper_levels(cols, levels, x_ref[...], y_ref[...], upper_ref, g_ref, None, scratch, False)
    y = rows16(own)
    scale, inverse = scale_of(x_ref[...], upper_ref, levels)
    scale_ref[0:1] = scale
    scale_ref[1:2] = inverse
    scale = jnp.concatenate([scale] * (size // 128), axis=1)
    width = leaves * size // SPLITS
    scale = jnp.concatenate([scale] * (width // size), axis=1)
    for k in range(SPLITS):
        part = slice(k * width, (k + 1) * width)
        far = far_of(y, joint_ref, part)
        e = valid_ref[:, part] * (scale * (n_ref[:, part] + far))
        e_ref[:, part] = e
        both[0:16, part] = rows16(r_ref[:, part])
        both[16:32, part] = rows16(e)
        for i in range(leaves // SPLITS):
            leaf_ref[k * (leaves // SPLITS) + i] = e[:, i * size : (i + 1) * size]
    edge = top_ref.shape[0]
    top_ref[...] = leaf_ref[0:edge]
    bottom_ref[...] = leaf_ref[leaves - edge : leaves]
    e16 = both[16:32, :]
    c = join16(dot_nt(e16, joint_ref[0]) + (dot_nt(e16, joint_ref[1]) + dot_nt(e16, joint_ref[2])))
    square = dot_nt(both[...], both[...])

    def block(i, j):
        part = join16(square[16 * i : 16 * i + 16, 16 * j : 16 * j + 16])
        return part[:, 0:4] + part[:, 4:8] + part[:, 8:12]

    moments = jnp.concatenate([block(0, 0), block(0, 1), block(1, 1), jnp.zeros((4, 116), F32)], axis=1)
    out_ref[...] = jnp.concatenate([jnp.concatenate([c, jnp.zeros((4, 64), F32)], axis=1), moments], axis=0)


def middle(cols, levels, leaves, edge, x, y, upper_t, g, joint, r, n, valid):
    size = r.shape[1] // leaves
    return pl.pallas_call(
        functools.partial(middle_kernel, cols, levels),
        out_shape=[
            jax.ShapeDtypeStruct(r.shape, F32),
            jax.ShapeDtypeStruct((leaves, 4, size), F32),
            jax.ShapeDtypeStruct((edge, 4, size), F32),
            jax.ShapeDtypeStruct((edge, 4, size), F32),
            jax.ShapeDtypeStruct((8, 128), F32),
            jax.ShapeDtypeStruct((2, 128), F32),
        ],
        in_specs=[VM] * 8,
        out_specs=[VM] * 6,
        scratch_shapes=[pltpu.VMEM((2 * x.shape[0], 8, 64), F32), pltpu.VMEM((32, r.shape[1]), BF)],
        compiler_params=params(),
        name="middle",
    )(x, y, upper_t, g, joint, r, n, valid)


def mat_mul(a, b):
    return [[sum(a[i][k] * b[k][j] for k in range(4)) for j in range(4)] for i in range(4)]


def mat_add(a, b):
    return [[a[i][j] + b[i][j] for j in range(4)] for i in range(4)]


def mat_sub(a, b):
    return [[a[i][j] - b[i][j] for j in range(4)] for i in range(4)]


def mat_t(a):
    return [[a[j][i] for j in range(4)] for i in range(4)]


def mat_solve(a, b):
    a = [list(row) for row in a]
    b = [list(row) for row in b]
    width = len(b[0])
    inverse = []
    for col in range(4):
        inverse.append(1.0 / a[col][col])
        for row in range(col + 1, 4):
            factor = a[row][col] * inverse[col]
            for k in range(col + 1, 4):
                a[row][k] = a[row][k] - factor * a[col][k]
            for k in range(width):
                b[row][k] = b[row][k] - factor * b[col][k]
    result = [None] * 4
    for col in reversed(range(4)):
        row = list(b[col])
        for later in range(col + 1, 4):
            row = [row[k] - a[col][later] * result[later][k] for k in range(width)]
        result[col] = [value * inverse[col] for value in row]
    return result


def mat_scale(a, factor):
    return [[value * factor for value in row] for row in a]


def weights(gram, cross, square, cubic, scale, inverse):
    curvature = mat_add(mat_scale(gram, scale), cross)
    both = mat_solve(curvature, [gram[i] + cross[i] for i in range(4)])
    step = [row[0:4] for row in both]
    rest = [row[4:8] for row in both]
    mixed = mat_mul(mat_t(rest), mat_mul(cross, step))
    gram_next = mat_sub(
        mat_add(mat_mul(mat_t(rest), mat_mul(gram, rest)), mat_mul(mat_t(step), mat_mul(square, step))),
        mat_add(mixed, mat_t(mixed)),
    )
    mix = mat_solve(gram, gram_next)
    lead = mat_add(rest, mix)
    second = mat_sub(mat_scale(lead, inverse), step)
    with_r = mat_sub(
        mat_add(mat_mul(gram, lead), mat_mul(cross, second)), mat_scale(mat_mul(square, step), inverse)
    )
    with_e = mat_sub(mat_add(mat_mul(mat_t(cross), lead), mat_mul(square, second)), mat_mul(cubic, step))
    curvature_next = mat_sub(mat_mul(mat_t(lead), with_r), mat_mul(mat_t(step), with_e))
    step_next = mat_solve(curvature_next, gram_next)
    lead_step = mat_mul(lead, step_next)
    step_step = mat_mul(step, step_next)
    second_step = mat_mul(second, step_next)
    solution = (mat_add(mat_scale(step, scale), lead_step), mat_scale(step_step, -1.0), None)
    residual = (mat_sub(rest, lead_step), mat_scale(mat_add(step, second_step), -1.0), step_step)
    return solution, residual


def final_kernel(
    cols, levels, c_ref, y_ref, upper_ref, g_ref, b_ref, joint_ref, r_ref, e_ref, n_ref, valid_ref, scale_ref,
    x_ref, out_ref, scratch,
):
    leaves, _, size = x_ref.shape
    c = c_ref[...]
    own, sums = upper_levels(cols, levels, c, y_ref[...], upper_ref, g_ref, b_ref, scratch, True)
    y = rows16(own)
    moments = jnp.sum(c, axis=0)[4:8]
    half = columns_of(sums)

    def matrix(x, at):
        return [[jnp.broadcast_to(x[i : i + 1, at + j : at + j + 1], (1, 128)) for j in range(4)] for i in range(4)]

    half = mat_add(matrix(moments, 16), matrix(half, 0))
    cubic = mat_add(matrix(moments, 12), mat_add(half, mat_t(half)))
    solution, residual = weights(
        matrix(moments, 0), matrix(moments, 4), matrix(moments, 8), cubic, scale_ref[0:1], scale_ref[1:2]
    )
    row = lax.broadcasted_iota(jnp.int32, (8, 128), 0)
    col = lax.broadcasted_iota(jnp.int32, (8, 128), 1)
    table = jnp.zeros((8, 128), F32)
    for first, parts in ((0, solution), (4, residual)):
        for k, part in enumerate(parts):
            if part is None:
                continue
            for i in range(4):
                line = jnp.zeros((8, 128), F32)
                for j in range(4):
                    line = jnp.where(row == first + j, part[i][j], line)
                table = jnp.where(col == 4 * k + i, line + table, table)
    table = table[:, 0:16]
    width = leaves * size // SPLITS
    for k in range(SPLITS):
        part = slice(k * width, (k + 1) * width)
        far = far_of(y, joint_ref, part)
        f = valid_ref[:, part] * (n_ref[:, part] + far)
        stacked = jnp.concatenate([r_ref[:, part], e_ref[:, part], f, jnp.zeros_like(f)], axis=0)
        both = jnp.dot(table, stacked, precision=lax.Precision.HIGHEST, preferred_element_type=F32)
        for i in range(leaves // SPLITS):
            x_ref[k * (leaves // SPLITS) + i] = both[0:4, i * size : (i + 1) * size]
            out_ref[k * (leaves // SPLITS) + i] = both[4:8, i * size : (i + 1) * size]


def final(cols, levels, leaves, c, y, upper_t, g, b, joint, r, e, n, valid, scale):
    out = jax.ShapeDtypeStruct((leaves, 4, r.shape[1] // leaves), F32)
    return pl.pallas_call(
        functools.partial(final_kernel, cols, levels),
        out_shape=[out, out],
        in_specs=[VM] * 11,
        out_specs=[VM] * 2,
        scratch_shapes=[pltpu.VMEM((2 * c.shape[0], 8, 64), F32)],
        compiler_params=params(),
        name="final",
    )(c, y, upper_t, g, b, joint, r, e, n, valid, scale)


def swap(axis, first, last):
    count = lax.axis_size(axis)
    up = [(i, (i + 1) % count) for i in range(count)]
    down = [(j, i) for i, j in up]
    return lax.ppermute(last, axis, up), lax.ppermute(first, axis, down)


def edges(nx, ny, own, top, bottom, after):
    up, down = swap("gx", top, bottom)
    left, right = swap("gy", *side_columns(nx, ny, own, up, down, after))
    return own, up, down, left, right


def exchange(x, axis):
    return lax.all_to_all(x, axis, 0, 0, tiled=True)


def on_device(points, right_sides, leaf_counts, near_mask, leaf_basis, leaf_transfer, upper_transfer, proxy_nodes):
    nx, ny, _, size = points.shape
    leaves = nx * ny
    rows, cols = lax.axis_size("gx"), lax.axis_size("gy")
    levels = (rows * cols).bit_length() - 2
    target_table, source_table, factor = feature_tables()
    factor = jnp.asarray(np.broadcast_to(factor[:, :, None], (9, 32, size)), BF)

    def flat(x):
        return x.reshape((leaves,) + x.shape[2:])

    packed, top, bottom, r, valid = pack(nx, ny, leaf_counts, jnp.swapaxes(points, 1, 2), flat(right_sides))
    joint, c = upward(r, flat(leaf_basis), flat(leaf_transfer))
    parts = edges(nx, ny, packed, top, bottom, c)
    b, g, upper_t = couplings(levels, cols, (nx, ny), upper_transfer, proxy_nodes)
    s, t, v, *lists, c = geometry(nx, ny, near_mask, parts, target_table, source_table, c, b, cols)
    y, c = row_tree(False, exchange(c, "gy"), upper_t, g, b)
    c = exchange(c, "gx")
    n, cache = near_build(nx, ny, lists, v, s, t, factor, c)
    e, e_leaves, top, bottom, c, scale = middle(cols, levels, leaves, ny, c, y, upper_t, g, joint, r, n, valid)
    n, c = near_reuse(nx, ny, lists, edges(nx, ny, e_leaves, top, bottom, c), c, cache, cols)
    y, c = row_tree(True, exchange(c, "gy"), upper_t, g, b)
    x, out = final(cols, levels, leaves, exchange(c, "gx"), y, upper_t, g, b, joint, r, e, n, valid, scale)
    shape = (nx, ny, 4, size)
    return x.reshape(shape), out.reshape(shape)


def solution(mesh):
    return jax.shard_map(
        on_device,
        mesh=mesh,
        in_specs=(
            P("gx", "gy", None, None),
            P("gx", "gy", None, None),
            P("gx", "gy"),
            P("gx", "gy", None),
            P("gx", "gy", None, None),
            P("gx", "gy", None, None),
            P(),
            P(),
        ),
        out_specs=(P("gx", "gy", None, None), P("gx", "gy", None, None)),
        check_vma=False,
    )
```

```python
import functools

import jax
import jax.numpy as jnp
import numpy as np
from jax import lax
from jax.experimental import pallas as pl
from jax.experimental.pallas import tpu as pltpu
from jax.sharding import PartitionSpec as P

F32 = jnp.float32
BF = jnp.bfloat16
NEAR_LENGTH = 0.5
FAR_LENGTH = 16.0
NEAR_RATE = 3.0**0.5 / NEAR_LENGTH
FAR_RATE = 3.0**0.5 / FAR_LENGTH
LOG2E = 1.4426950408889634
COUPLING_SCALE = 1.0 / 128.0
GROUP = 16
CHUNK = 64
BUILD_SLOTS = 2
READ_SLOTS = 5
VMEM_LIMIT = 28 * 2**20
VM = pl.BlockSpec(memory_space=pltpu.VMEM)
ANY = pl.BlockSpec(memory_space=pl.ANY)
SM = pl.BlockSpec(memory_space=pltpu.SMEM)


def rounded(x):
    return x.astype(BF).astype(F32)


def split2(x):
    high = x.astype(BF)
    return high, (x - high.astype(F32)).astype(BF)


def rows16(x):
    first = rounded(x)
    second = rounded(x - first)
    third = rounded(x - first - second)
    return jnp.concatenate([first, second, third, jnp.zeros_like(x)], axis=0).astype(BF)


def join16(y):
    return y[0:4] + y[4:8] + y[8:12]


def dot(a, b):
    return jnp.dot(a, b, preferred_element_type=F32)


def dot_nt(a, b):
    return lax.dot_general(a, b, (((1,), (1,)), ((), ())), preferred_element_type=F32)


def split3(x):
    first = x.astype(BF)
    rest = x - first.astype(F32)
    second = rest.astype(BF)
    return first, second, (rest - second.astype(F32)).astype(BF)


def exact_dot(a, b):
    return jnp.dot(a, b, precision=lax.Precision.HIGHEST, preferred_element_type=F32)


def feature_tables():
    target = np.zeros((32, 24), np.float32)
    source = np.zeros((32, 24), np.float32)
    factor = np.ones((9, 32), np.float32)
    one = 19
    for c in range(3):
        target[2 * c, c] = target[2 * c + 1, c] = -2
        source[2 * c, c] = source[2 * c + 1, 8 + c] = 1
        target[6 + 2 * c, 8 + c] = target[7 + 2 * c, 8 + c] = -2
        source[6 + 2 * c, c] = source[7 + 2 * c, 8 + c] = 1
    for k in range(3):
        target[12 + k, one] = source[12 + k, 16 + k] = 1
        target[15 + k, 16 + k] = source[15 + k, one] = 1
    for c in range(2):
        target[18 + 2 * c, c] = target[19 + 2 * c, 8 + c] = 1
        source[18 + 2 * c, one] = source[19 + 2 * c, one] = 1
        target[22 + 2 * c, one] = target[23 + 2 * c, one] = 1
        source[22 + 2 * c, c] = source[23 + 2 * c, 8 + c] = 1
    target[26, one] = source[26, one] = 1
    for code in range(9):
        off = (code // 3 - 1, code % 3 - 1)
        for c in range(2):
            factor[code, 18 + 2 * c : 20 + 2 * c] = -2 * off[c]
            factor[code, 22 + 2 * c : 24 + 2 * c] = 2 * off[c]
        factor[code, 26] = off[0] ** 2 + off[1] ** 2
    return target, source, factor


def params():
    return pltpu.CompilerParams(vmem_limit_bytes=VMEM_LIMIT)


def around(nx, ny):
    wide = ny + 2
    return (
        (nx * ny, lambda i: (i // ny + 1) * wide + i % ny + 1),
        (ny, lambda i: i + 1),
        (ny, lambda i: (nx + 1) * wide + i + 1),
        (nx + 2, lambda i: i * wide),
        (nx + 2, lambda i: i * wide + wide - 1),
    )


def each_leaf(nx, ny, refs, body, unroll=4):
    for ref, (count, place) in zip(refs, around(nx, ny)):

        def step(i, carry, ref=ref, place=place):
            body(place(i), ref, i)
            return carry

        lax.fori_loop(0, count, step, 0, unroll=unroll if count % unroll == 0 else 2)


def pack_kernel(nx, ny, count_ref, points_ref, sides_ref, packed_ref, top_ref, bottom_ref, r_ref, valid_ref):
    size = points_ref.shape[3]
    lane = lax.broadcasted_iota(jnp.int32, (1, size), 1)

    def body(a, carry):
        first = (lax.axis_index("gx") * nx + a // ny).astype(F32) + 0.5
        second = (lax.axis_index("gy") * ny + a % ny).astype(F32) + 0.5
        for c, centre in enumerate((first, second, 0.5)):
            packed_ref[a, c : c + 1] = points_ref[a // ny, c, pl.ds(a % ny, 1)] - centre
        count = count_ref[a // ny, a % ny]
        packed_ref[a, 3:4] = jnp.full((1, size), count.astype(F32))
        valid = jnp.where(lane < count, 1.0, 0.0)
        r = jnp.where(valid > 0.0, sides_ref[a], 0.0)
        packed_ref[a, 4:8] = r
        part = pl.ds(pl.multiple_of(a * size, size), size)
        r_ref[:, part] = r
        valid_ref[:, part] = valid
        return carry

    lax.fori_loop(0, nx * ny, body, 0, unroll=4)
    top_ref[...] = packed_ref[0:ny]
    bottom_ref[...] = packed_ref[(nx - 1) * ny : nx * ny]


def pack(nx, ny, counts, points, sides):
    leaves, _, size = sides.shape
    return pl.pallas_call(
        functools.partial(pack_kernel, nx, ny),
        out_shape=[
            jax.ShapeDtypeStruct((leaves, 8, size), F32),
            jax.ShapeDtypeStruct((ny, 8, size), F32),
            jax.ShapeDtypeStruct((ny, 8, size), F32),
            jax.ShapeDtypeStruct((4, leaves * size), F32),
            jax.ShapeDtypeStruct((1, leaves * size), F32),
        ],
        in_specs=[SM, VM, VM],
        out_specs=[VM] * 5,
        compiler_params=params(),
        name="pack",
    )(counts, points, sides)


def sides_kernel(nx, ny, own_ref, up_ref, down_ref, after_ref, left_ref, right_ref):
    for col, ref in ((0, left_ref), (ny - 1, right_ref)):
        ref[0] = up_ref[col]
        ref[nx + 1] = down_ref[col]
        for i in range(nx):
            ref[i + 1] = own_ref[i * ny + col]


def side_columns(nx, ny, own, up, down, after):
    out = jax.ShapeDtypeStruct((nx + 2,) + own.shape[1:], F32)
    return pl.pallas_call(
        functools.partial(sides_kernel, nx, ny),
        out_shape=[out, out],
        in_specs=[VM] * 3 + [ANY],
        out_specs=[VM] * 2,
        compiler_params=params(),
        name="side_columns",
    )(own, up, down, after)


def geometry_kernel(
    nx, ny, mask_ref, own_ref, up_ref, down_ref, left_ref, right_ref, target_ref, source_ref, c_ref, after_ref,
    s_ref, t_ref, v_ref, long_ref, short_ref, groups_ref, out_ref, count_ref,
):
    wide = ny + 2
    leaves = (nx + 2) * wide
    size = own_ref.shape[2]
    row = lax.broadcasted_iota(jnp.int32, (8, size), 0)
    refs = (own_ref, up_ref, down_ref, left_ref, right_ref)

    def read_count(e, ref, i):
        count_ref[e] = ref[i, 3, 0].astype(jnp.int32)

    each_leaf(nx, ny, refs, read_count)

    def features(e, ref, i):
        packed = ref[i]
        x = jnp.where(row < 3, packed, 0.0)
        first = rounded(x)
        second = rounded(x - first)
        held = first + second
        norm = jnp.sum(held * held, axis=0, keepdims=True)
        n1 = rounded(norm)
        n2 = rounded(norm - n1)
        n3 = rounded(norm - n1 - n2)
        last = jnp.where(row == 0, n1, jnp.where(row == 1, n2, jnp.where(row == 2, n3, jnp.where(row == 3, 1.0, 0.0))))
        f = jnp.concatenate([first, second, last], axis=0).astype(BF)
        t_ref[e] = dot(target_ref[...], f).astype(BF)
        s_ref[e] = lax.dot_general(
            f, source_ref[...], (((0,), (1,)), ((), ())), preferred_element_type=F32
        ).astype(BF)
        v_ref[e] = rows16(packed[4:8])

    def note(a, carry):
        features((a // ny + 1) * wide + a % ny + 1, own_ref, a)
        long_count, short_count = carry
        corner = (a // ny) * wide + a % ny
        for code in range(9):
            source = corner + code // 3 * wide + code % 3
            entry = (source * 16 + code) * 64 + a
            on = jnp.where(mask_ref[a // ny, a % ny, code] != 0, 1, 0)
            is_long = jnp.where(count_ref[source] > size - CHUNK, on, 0)
            long_ref[long_count] = entry
            short_ref[short_count] = entry
            long_count = long_count + is_long
            short_count = short_count + (on - is_long)
        return long_count, short_count

    long_count, short_count = lax.fori_loop(0, nx * ny, note, (0, 0), unroll=8)
    for j in range(GROUP):
        long_ref[long_count + j] = leaves * 1024
        short_ref[short_count + j] = leaves * 1024
    groups_ref[0] = (long_count + GROUP - 1) // GROUP
    groups_ref[1] = (short_count + GROUP - 1) // GROUP
    for ref, (count, place) in list(zip(refs, around(nx, ny)))[1:]:

        def step(i, carry, ref=ref, place=place):
            features(place(i), ref, i)
            return carry

        lax.fori_loop(0, count, step, 0, unroll=True)
    v_ref[leaves] = jnp.zeros((16, size), BF)
    for i in range(out_ref.shape[0]):
        out_ref[i] = c_ref[...]


def geometry(nx, ny, mask, parts, target_table, source_table, c, after, copies):
    leaves, size = (nx + 2) * (ny + 2), parts[0].shape[2]
    most = nx * ny * 9 + GROUP
    return pl.pallas_call(
        functools.partial(geometry_kernel, nx, ny),
        out_shape=[
            jax.ShapeDtypeStruct((leaves, size, 32), BF),
            jax.ShapeDtypeStruct((leaves, 32, size), BF),
            jax.ShapeDtypeStruct((leaves + 1, 16, size), BF),
            jax.ShapeDtypeStruct((most,), jnp.int32),
            jax.ShapeDtypeStruct((most,), jnp.int32),
            jax.ShapeDtypeStruct((2,), jnp.int32),
            jax.ShapeDtypeStruct((copies, 8, 128), F32),
        ],
        in_specs=[SM] + [VM] * 8 + [ANY],
        out_specs=[VM] * 3 + [SM] * 3 + [VM],
        scratch_shapes=[pltpu.SMEM((leaves,), jnp.int32)],
        compiler_params=params(),
        name="geometry",
    )(mask, *parts, jnp.asarray(target_table, BF), jnp.asarray(source_table, BF), c, after)


def block_copy(buffer, cache_ref, sems, slots, rows, inward):
    def copy(g):
        slot = g % slots
        here, there = buffer.at[slot], cache_ref.at[g]
        if rows < cache_ref.shape[3]:
            here, there = here.at[:, :, 0:rows], there.at[:, :, 0:rows]
        if inward:
            return pltpu.make_async_copy(there, here, sems.at[slot])
        return pltpu.make_async_copy(here, there, sems.at[slot])

    return copy


def build_kernel(
    nx, ny, long_ref, short_ref, groups_ref, v_ref, s_ref, t_ref, factor_ref, after_ref,
    o_ref, cache_ref, acc, buffer, sems,
):
    wide = ny + 2
    leaves = (nx + 2) * wide
    size = o_ref.shape[1] // (nx * ny)
    short = size - CHUNK
    acc[...] = jnp.zeros_like(acc)
    long_groups = groups_ref[0]
    groups = long_groups + groups_ref[1]
    out_long = block_copy(buffer, cache_ref, sems, BUILD_SLOTS, size, False)
    out_short = block_copy(buffer, cache_ref, sems, BUILD_SLOTS, short, False)

    def wait(g):
        @pl.when(g < long_groups)
        def _():
            out_long(g).wait()

        @pl.when(g >= long_groups)
        def _():
            out_short(g).wait()

    def run(first, last, rows, list_ref, start):
        def group(g, carry):
            slot = g % BUILD_SLOTS

            @pl.when(g >= BUILD_SLOTS)
            def _():
                wait(g - BUILD_SLOTS)

            done = []
            for j in range(GROUP):
                entry = list_ref[(g - first) * GROUP + j]
                a = entry & 63
                code = (entry >> 6) & 15
                source = entry >> 10
                t = t_ref[(a // ny + 1) * wide + a % ny + 1] * factor_ref[code]
                s = s_ref[jnp.minimum(source, leaves - 1)]
                v = v_ref[source]
                total = jnp.zeros((16, size), F32)
                for k in range(rows // CHUNK):
                    part = slice(k * CHUNK, (k + 1) * CHUNK)
                    squared = jnp.maximum(dot(s[part], t), 1e-30)
                    distance = squared * lax.rsqrt(squared)
                    value = (1.0 + NEAR_RATE * distance) * jnp.exp2((-NEAR_RATE * LOG2E) * distance)
                    high, low = split2(value)
                    buffer[slot, j, 0, part] = high
                    buffer[slot, j, 1, part] = low
                    total += dot(v[:, part], high) + dot(v[:, part], low)
                done.append((a, total))
            for a, total in done:
                acc[a] += total
            start(g).start()
            return carry

        lax.fori_loop(first, last, group, 0)

    run(0, long_groups, size, long_ref, out_long)
    run(long_groups, groups, short, short_ref, out_short)
    for back in range(BUILD_SLOTS):
        wait(groups - 1 - back)

    def finish(a, carry):
        o_ref[:, pl.ds(pl.multiple_of(a * size, size), size)] = join16(acc[a]) * (1.0 / size**0.5)
        return carry

    lax.fori_loop(0, nx * ny, finish, 0, unroll=4)


def near_build(nx, ny, lists, v, s, t, factor, after):
    size = v.shape[2]
    most = lists[0].shape[0] // GROUP + 1
    return pl.pallas_call(
        functools.partial(build_kernel, nx, ny),
        out_shape=[
            jax.ShapeDtypeStruct((4, nx * ny * size), F32),
            jax.ShapeDtypeStruct((most, GROUP, 2, size, size), BF),
        ],
        in_specs=[SM] * 3 + [VM] * 4 + [ANY],
        out_specs=[VM, ANY],
        scratch_shapes=[
            pltpu.VMEM((nx * ny, 16, size), F32),
            pltpu.VMEM((BUILD_SLOTS, GROUP, 2, size, size), BF),
            pltpu.SemaphoreType.DMA((BUILD_SLOTS,)),
        ],
        compiler_params=params(),
        name="near_build",
    )(*lists, v, s, t, factor, after)


def reuse_kernel(
    nx, ny, long_ref, short_ref, groups_ref, own_ref, up_ref, down_ref, left_ref, right_ref, c_ref, cache_ref,
    o_ref, out_ref, v16, acc, buffer, sems,
):
    wide = ny + 2
    leaves = (nx + 2) * wide
    size = own_ref.shape[2]
    short = size - CHUNK
    long_groups = groups_ref[0]
    groups = long_groups + groups_ref[1]
    in_long = block_copy(buffer, cache_ref, sems, READ_SLOTS, size, True)
    in_short = block_copy(buffer, cache_ref, sems, READ_SLOTS, short, True)

    def fetch(g):
        @pl.when(g < long_groups)
        def _():
            in_long(g).start()

        @pl.when(jnp.logical_and(g >= long_groups, g < groups))
        def _():
            in_short(g).start()

    for g in range(READ_SLOTS - 1):
        fetch(g)

    def split_leaf(e, ref, i):
        v16[e] = rows16(ref[i])

    each_leaf(nx, ny, (own_ref, up_ref, down_ref, left_ref, right_ref), split_leaf)
    v16[leaves] = jnp.zeros((16, size), BF)
    acc[...] = jnp.zeros_like(acc)

    def run(first, last, rows, list_ref, copy):
        def group(g, carry):
            slot = g % READ_SLOTS
            copy(g).wait()
            fetch(g + READ_SLOTS - 1)
            done = []
            for j in range(GROUP):
                entry = list_ref[(g - first) * GROUP + j]
                v = v16[entry >> 10][:, 0:rows]
                done.append((entry & 63, dot(v, buffer[slot, j, 0, 0:rows]) + dot(v, buffer[slot, j, 1, 0:rows])))
            for a, total in done:
                acc[a] += total
            return carry

        lax.fori_loop(first, last, group, 0)

    run(0, long_groups, size, long_ref, in_long)
    run(long_groups, groups, short, short_ref, in_short)

    def finish(a, sums):
        near = join16(acc[a]) * (1.0 / size**0.5)
        o_ref[:, pl.ds(pl.multiple_of(a * size, size), size)] = near
        v = own_ref[a]
        return tuple(sums[s] + v * near[s : s + 1] for s in range(4))

    sums = lax.fori_loop(0, nx * ny, finish, tuple(jnp.zeros((4, size), F32) for _ in range(4)), unroll=4)
    columns = [jnp.sum(x, axis=1, keepdims=True) for x in sums]
    block = jnp.concatenate([jnp.zeros((4, 12), F32)] + columns + [jnp.zeros((4, 112), F32)], axis=1)
    total = c_ref[...] + jnp.concatenate([jnp.zeros((4, 128), F32), block], axis=0)
    for i in range(out_ref.shape[0]):
        out_ref[i] = total


def near_reuse(nx, ny, lists, parts, c, cache, copies):
    size = parts[0].shape[2]
    leaves = (nx + 2) * (ny + 2)
    return pl.pallas_call(
        functools.partial(reuse_kernel, nx, ny),
        out_shape=[jax.ShapeDtypeStruct((4, nx * ny * size), F32), jax.ShapeDtypeStruct((copies, 8, 128), F32)],
        in_specs=[SM] * 3 + [VM] * 6 + [ANY],
        out_specs=[VM] * 2,
        scratch_shapes=[
            pltpu.VMEM((leaves + 1, 16, size), BF),
            pltpu.VMEM((nx * ny, 16, size), F32),
            pltpu.VMEM((READ_SLOTS,) + cache.shape[1:], BF),
            pltpu.SemaphoreType.DMA((READ_SLOTS,)),
        ],
        compiler_params=params(),
        name="near_reuse",
    )(*lists, *parts, c, cache)


def upward_kernel(r_ref, basis_ref, transfer_ref, joint_ref, c_ref):
    leaves, terms, size = basis_ref.shape

    def body(a, total):
        part = pl.ds(pl.multiple_of(a * size, size), size)
        v = rows16(r_ref[:, part])
        for term, piece in enumerate(split3(exact_dot(transfer_ref[a], basis_ref[a]))):
            joint_ref[term, :, part] = piece
            total = total + dot_nt(v, piece)
        return total

    total = lax.fori_loop(0, leaves, body, jnp.zeros((16, terms), F32), unroll=16)
    total = jnp.concatenate([join16(total), jnp.zeros((4, 128 - terms), F32)], axis=1)
    c_ref[...] = jnp.concatenate([total, jnp.zeros((4, 128), F32)], axis=0)


def upward(r, basis, transfer):
    leaves, terms, size = basis.shape
    return pl.pallas_call(
        upward_kernel,
        out_shape=[
            jax.ShapeDtypeStruct((3, terms, leaves * size), BF),
            jax.ShapeDtypeStruct((8, 128), F32),
        ],
        in_specs=[VM] * 3,
        out_specs=[VM] * 2,
        compiler_params=params(),
        name="upward",
    )(r, basis, transfer)


def own_place(cols):
    return lax.axis_index("gx") * cols + lax.axis_index("gy")


def coupling_kernel(levels, cols, tile, upper_ref, row_ref, b_ref, g_ref, turned_ref):
    place = own_place(cols)
    col_values = jnp.concatenate([row_ref[...], jnp.zeros((5, 64), F32)], axis=0).T
    for k in range(2):
        turned_ref[k] = upper_ref[k].T
    down = None
    for level in range(levels):
        span = 2**level
        extent = (1, span) if span <= cols else (span // cols, cols)
        half = (0.5 * tile[0] * extent[0], 0.5 * tile[1] * extent[1], 0.5)
        apart = (0.0, 2.0 * span * tile[1]) if 2 * span < cols else (2.0 * span / cols * tile[0], 0.0)

        def matrix(sign):
            squared = jnp.zeros((64, 64), F32)
            for c in range(3):
                step = half[c] * (col_values[:, c : c + 1] - row_ref[c : c + 1, :])
                if c < 2:
                    step = step + sign * apart[c]
                squared = squared + step * step
            squared = jnp.maximum(squared, 1e-30)
            scaled = FAR_RATE * (squared * lax.rsqrt(squared))
            return COUPLING_SCALE * ((1.0 + scaled) * jnp.exp(-scaled))

        b_ref[level] = matrix(-1.0)
        upper = (place // (2 * span)) % 2
        own = matrix(jnp.where(upper == 1, -1.0, 1.0))
        g_ref[level] = own if down is None else exact_dot(own, down)
        if level + 1 < levels:
            bit = (place // span) % 2
            step_down = upper_ref[bit]
            down = step_down if down is None else exact_dot(step_down, down)


def couplings(levels, cols, tile, upper, nodes):
    out = jax.ShapeDtypeStruct((levels, 64, 64), F32)
    return pl.pallas_call(
        functools.partial(coupling_kernel, levels, cols, tile),
        out_shape=[out, out, jax.ShapeDtypeStruct(upper.shape, F32)],
        in_specs=[VM] * 2,
        out_specs=[VM] * 3,
        compiler_params=params(),
        name="couplings",
    )(upper, nodes)


def pair_energy(c, b, sums):
    count = c.shape[0]
    quads = c.reshape(count // 4, 4, 8, 64)
    low = quads[:, 0:2].reshape(count // 2 * 8, 64)
    high = quads[:, 2:4].reshape(count // 2, 8, 64)
    carried = exact_dot(low, b).reshape(count // 2, 8, 64)
    return [sums[s] + jnp.sum(carried * high[:, s : s + 1, :], axis=0) for s in range(4)]


def lift(c, upper_t):
    count = c.shape[0]
    paired = c.reshape(count // 2, 2, 8, 64)
    even = paired[:, 0].reshape(count // 2 * 8, 64)
    odd = paired[:, 1].reshape(count // 2 * 8, 64)
    return (exact_dot(even, upper_t[0]) + exact_dot(odd, upper_t[1])).reshape(count // 2, 8, 64)


def no_sums():
    return [jnp.zeros((8, 64), F32) for _ in range(4)]


def columns_of(sums):
    return jnp.concatenate([jnp.sum(x, axis=1, keepdims=True) for x in sums], axis=1)


def row_kernel(with_energy, c_ref, upper_ref, g_ref, b_ref, y_ref, out_ref, scratch):
    x = c_ref[...]
    c = x[:, :, 0:64]
    place = lax.axis_index("gy")
    y = jnp.zeros((8, 64), F32)
    sums = no_sums()
    level = 0
    while c.shape[0] > 2:
        scratch[0 : c.shape[0]] = c
        y = y + exact_dot(scratch[(place // 2**level) ^ 2], g_ref[level])
        if with_energy:
            sums = pair_energy(c, b_ref[level], sums)
        c = lift(c, upper_ref)
        level += 1
    y_ref[...] = y
    if not with_energy:
        lower = jnp.max(jnp.max(jnp.abs(x), axis=0), axis=1, keepdims=True)
        lower = jnp.broadcast_to(jnp.max(lower, axis=0, keepdims=True), (4, 128))
    else:
        lower = jnp.sum(x, axis=0)[4:8]
        lower = jnp.concatenate([lower[:, 0:16], columns_of(sums)[0:4], jnp.zeros((4, 108), F32)], axis=1)
    total = jnp.concatenate([jnp.concatenate([c[0, 0:4], c[1, 0:4]], axis=1), lower], axis=0)
    for i in range(out_ref.shape[0]):
        out_ref[i] = total


def row_tree(with_energy, c, upper_t, g, b):
    return pl.pallas_call(
        functools.partial(row_kernel, with_energy),
        out_shape=[jax.ShapeDtypeStruct((8, 64), F32), jax.ShapeDtypeStruct(c.shape, F32)],
        in_specs=[VM] * 4,
        out_specs=[VM] * 2,
        scratch_shapes=[pltpu.VMEM((c.shape[0], 8, 64), F32)],
        compiler_params=params(),
        name="row_tree",
    )(c, upper_t, g, b)


def upper_levels(cols, levels, x, y, upper_ref, g_ref, b_ref, scratch, with_energy):
    place = own_place(cols)
    level = cols.bit_length() - 2
    c = jnp.stack([x[:, :, 0:64], x[:, :, 64:128]], axis=1).reshape(2 * x.shape[0], 8, 64)
    sums = no_sums()
    while level < levels:
        scratch[0 : c.shape[0]] = c
        y = y + exact_dot(scratch[(place // 2**level) ^ 2], g_ref[level])
        if with_energy:
            sums = pair_energy(c, b_ref[level], sums)
        if level + 1 < levels:
            c = lift(c, upper_ref)
        level += 1
    return y[0:4], sums


SPLITS = 4


def far_of(y, joint_ref, part):
    return join16(dot(y, joint_ref[0, :, part]) + (dot(y, joint_ref[1, :, part]) + dot(y, joint_ref[2, :, part])))


def scale_of(x, upper_ref, levels):
    largest = jnp.max(jnp.max(x[:, 4:8], axis=0), axis=0, keepdims=True)
    sizes = jnp.abs(upper_ref[...])
    up = jnp.max(jnp.sum(sizes[0] + sizes[1], axis=0, keepdims=True), axis=1, keepdims=True)
    down = jnp.max(jnp.max(jnp.sum(sizes, axis=2, keepdims=True), axis=0), axis=0, keepdims=True)
    growth = jnp.ones((1, 1), F32)
    for _ in range(levels - 1):
        growth = 1.0 + growth * (up * down)
    bound = 864.0 + 576.0 * (growth * largest)
    power = jnp.ones_like(bound)
    scale = jnp.full_like(bound, 2.0**48)
    inverse = jnp.full_like(bound, 2.0**-48)
    for k in (64, 32, 16, 8, 4, 2):
        fits = bound >= power * 2.0**k
        power = jnp.where(fits, power * 2.0**k, power)
        scale = jnp.where(fits, scale * 2.0 ** (-1.5 * k), scale)
        inverse = jnp.where(fits, inverse * 2.0 ** (1.5 * k), inverse)
    return jnp.minimum(scale, 1.0), jnp.maximum(inverse, 1.0)


def middle_kernel(
    cols, levels, x_ref, y_ref, upper_ref, g_ref, joint_ref, r_ref, n_ref, valid_ref,
    e_ref, leaf_ref, top_ref, bottom_ref, out_ref, scale_ref, scratch, both,
):
    leaves, _, size = leaf_ref.shape
    own, _ = upper_levels(cols, levels, x_ref[...], y_ref[...], upper_ref, g_ref, None, scratch, False)
    y = rows16(own)
    scale, inverse = scale_of(x_ref[...], upper_ref, levels)
    scale_ref[0:1] = scale
    scale_ref[1:2] = inverse
    scale = jnp.concatenate([scale] * (size // 128), axis=1)
    width = leaves * size // SPLITS
    scale = jnp.concatenate([scale] * (width // size), axis=1)
    for k in range(SPLITS):
        part = slice(k * width, (k + 1) * width)
        far = far_of(y, joint_ref, part)
        e = valid_ref[:, part] * (scale * (n_ref[:, part] + far))
        e_ref[:, part] = e
        both[0:16, part] = rows16(r_ref[:, part])
        both[16:32, part] = rows16(e)
        for i in range(leaves // SPLITS):
            leaf_ref[k * (leaves // SPLITS) + i] = e[:, i * size : (i + 1) * size]
    edge = top_ref.shape[0]
    top_ref[...] = leaf_ref[0:edge]
    bottom_ref[...] = leaf_ref[leaves - edge : leaves]
    e16 = both[16:32, :]
    c = join16(dot_nt(e16, joint_ref[0]) + (dot_nt(e16, joint_ref[1]) + dot_nt(e16, joint_ref[2])))
    square = dot_nt(both[...], both[...])

    def block(i, j):
        part = join16(square[16 * i : 16 * i + 16, 16 * j : 16 * j + 16])
        return part[:, 0:4] + part[:, 4:8] + part[:, 8:12]

    moments = jnp.concatenate([block(0, 0), block(0, 1), block(1, 1), jnp.zeros((4, 116), F32)], axis=1)
    out_ref[...] = jnp.concatenate([jnp.concatenate([c, jnp.zeros((4, 64), F32)], axis=1), moments], axis=0)


def middle(cols, levels, leaves, edge, x, y, upper_t, g, joint, r, n, valid):
    size = r.shape[1] // leaves
    return pl.pallas_call(
        functools.partial(middle_kernel, cols, levels),
        out_shape=[
            jax.ShapeDtypeStruct(r.shape, F32),
            jax.ShapeDtypeStruct((leaves, 4, size), F32),
            jax.ShapeDtypeStruct((edge, 4, size), F32),
            jax.ShapeDtypeStruct((edge, 4, size), F32),
            jax.ShapeDtypeStruct((8, 128), F32),
            jax.ShapeDtypeStruct((2, 128), F32),
        ],
        in_specs=[VM] * 8,
        out_specs=[VM] * 6,
        scratch_shapes=[pltpu.VMEM((2 * x.shape[0], 8, 64), F32), pltpu.VMEM((32, r.shape[1]), BF)],
        compiler_params=params(),
        name="middle",
    )(x, y, upper_t, g, joint, r, n, valid)


def mat_mul(a, b):
    return [[sum(a[i][k] * b[k][j] for k in range(4)) for j in range(4)] for i in range(4)]


def mat_add(a, b):
    return [[a[i][j] + b[i][j] for j in range(4)] for i in range(4)]


def mat_sub(a, b):
    return [[a[i][j] - b[i][j] for j in range(4)] for i in range(4)]


def mat_t(a):
    return [[a[j][i] for j in range(4)] for i in range(4)]


def mat_solve(a, b):
    a = [list(row) for row in a]
    b = [list(row) for row in b]
    width = len(b[0])
    inverse = []
    for col in range(4):
        inverse.append(1.0 / a[col][col])
        for row in range(col + 1, 4):
            factor = a[row][col] * inverse[col]
            for k in range(col + 1, 4):
                a[row][k] = a[row][k] - factor * a[col][k]
            for k in range(width):
                b[row][k] = b[row][k] - factor * b[col][k]
    result = [None] * 4
    for col in reversed(range(4)):
        row = list(b[col])
        for later in range(col + 1, 4):
            row = [row[k] - a[col][later] * result[later][k] for k in range(width)]
        result[col] = [value * inverse[col] for value in row]
    return result


def mat_scale(a, factor):
    return [[value * factor for value in row] for row in a]


def weights(gram, cross, square, cubic, scale, inverse):
    curvature = mat_add(mat_scale(gram, scale), cross)
    both = mat_solve(curvature, [gram[i] + cross[i] for i in range(4)])
    step = [row[0:4] for row in both]
    rest = [row[4:8] for row in both]
    mixed = mat_mul(mat_t(rest), mat_mul(cross, step))
    gram_next = mat_sub(
        mat_add(mat_mul(mat_t(rest), mat_mul(gram, rest)), mat_mul(mat_t(step), mat_mul(square, step))),
        mat_add(mixed, mat_t(mixed)),
    )
    mix = mat_solve(gram, gram_next)
    lead = mat_add(rest, mix)
    second = mat_sub(mat_scale(lead, inverse), step)
    with_r = mat_sub(
        mat_add(mat_mul(gram, lead), mat_mul(cross, second)), mat_scale(mat_mul(square, step), inverse)
    )
    with_e = mat_sub(mat_add(mat_mul(mat_t(cross), lead), mat_mul(square, second)), mat_mul(cubic, step))
    curvature_next = mat_sub(mat_mul(mat_t(lead), with_r), mat_mul(mat_t(step), with_e))
    step_next = mat_solve(curvature_next, gram_next)
    lead_step = mat_mul(lead, step_next)
    step_step = mat_mul(step, step_next)
    second_step = mat_mul(second, step_next)
    solution = (mat_add(mat_scale(step, scale), lead_step), mat_scale(step_step, -1.0), None)
    residual = (mat_sub(rest, lead_step), mat_scale(mat_add(step, second_step), -1.0), step_step)
    return solution, residual


def final_kernel(
    cols, levels, c_ref, y_ref, upper_ref, g_ref, b_ref, joint_ref, r_ref, e_ref, n_ref, valid_ref, scale_ref,
    x_ref, out_ref, scratch,
):
    leaves, _, size = x_ref.shape
    c = c_ref[...]
    own, sums = upper_levels(cols, levels, c, y_ref[...], upper_ref, g_ref, b_ref, scratch, True)
    y = rows16(own)
    moments = jnp.sum(c, axis=0)[4:8]
    half = columns_of(sums)

    def matrix(x, at):
        return [[jnp.broadcast_to(x[i : i + 1, at + j : at + j + 1], (1, 128)) for j in range(4)] for i in range(4)]

    half = mat_add(matrix(moments, 16), matrix(half, 0))
    cubic = mat_add(matrix(moments, 12), mat_add(half, mat_t(half)))
    solution, residual = weights(
        matrix(moments, 0), matrix(moments, 4), matrix(moments, 8), cubic, scale_ref[0:1], scale_ref[1:2]
    )
    row = lax.broadcasted_iota(jnp.int32, (8, 128), 0)
    col = lax.broadcasted_iota(jnp.int32, (8, 128), 1)
    table = jnp.zeros((8, 128), F32)
    for first, parts in ((0, solution), (4, residual)):
        for k, part in enumerate(parts):
            if part is None:
                continue
            for i in range(4):
                line = jnp.zeros((8, 128), F32)
                for j in range(4):
                    line = jnp.where(row == first + j, part[i][j], line)
                table = jnp.where(col == 4 * k + i, line + table, table)
    table = table[:, 0:16]
    width = leaves * size // SPLITS
    for k in range(SPLITS):
        part = slice(k * width, (k + 1) * width)
        far = far_of(y, joint_ref, part)
        f = valid_ref[:, part] * (n_ref[:, part] + far)
        stacked = jnp.concatenate([r_ref[:, part], e_ref[:, part], f, jnp.zeros_like(f)], axis=0)
        both = jnp.dot(table, stacked, precision=lax.Precision.HIGHEST, preferred_element_type=F32)
        for i in range(leaves // SPLITS):
            x_ref[k * (leaves // SPLITS) + i] = both[0:4, i * size : (i + 1) * size]
            out_ref[k * (leaves // SPLITS) + i] = both[4:8, i * size : (i + 1) * size]


def final(cols, levels, leaves, c, y, upper_t, g, b, joint, r, e, n, valid, scale):
    out = jax.ShapeDtypeStruct((leaves, 4, r.shape[1] // leaves), F32)
    return pl.pallas_call(
        functools.partial(final_kernel, cols, levels),
        out_shape=[out, out],
        in_specs=[VM] * 11,
        out_specs=[VM] * 2,
        scratch_shapes=[pltpu.VMEM((2 * c.shape[0], 8, 64), F32)],
        compiler_params=params(),
        name="final",
    )(c, y, upper_t, g, b, joint, r, e, n, valid, scale)


def swap(axis, first, last):
    count = lax.axis_size(axis)
    up = [(i, (i + 1) % count) for i in range(count)]
    down = [(j, i) for i, j in up]
    return lax.ppermute(last, axis, up), lax.ppermute(first, axis, down)


def edges(nx, ny, own, top, bottom, after):
    up, down = swap("gx", top, bottom)
    left, right = swap("gy", *side_columns(nx, ny, own, up, down, after))
    return own, up, down, left, right


def exchange(x, axis):
    return lax.all_to_all(x, axis, 0, 0, tiled=True)


def on_device(points, right_sides, leaf_counts, near_mask, leaf_basis, leaf_transfer, upper_transfer, proxy_nodes):
    nx, ny, _, size = points.shape
    leaves = nx * ny
    rows, cols = lax.axis_size("gx"), lax.axis_size("gy")
    levels = (rows * cols).bit_length() - 2
    target_table, source_table, factor = feature_tables()
    factor = jnp.asarray(np.broadcast_to(factor[:, :, None], (9, 32, size)), BF)

    def flat(x):
        return x.reshape((leaves,) + x.shape[2:])

    packed, top, bottom, r, valid = pack(nx, ny, leaf_counts, jnp.swapaxes(points, 1, 2), flat(right_sides))
    joint, c = upward(r, flat(leaf_basis), flat(leaf_transfer))
    parts = edges(nx, ny, packed, top, bottom, c)
    b, g, upper_t = couplings(levels, cols, (nx, ny), upper_transfer, proxy_nodes)
    s, t, v, *lists, c = geometry(nx, ny, near_mask, parts, target_table, source_table, c, b, cols)
    y, c = row_tree(False, exchange(c, "gy"), upper_t, g, b)
    c = exchange(c, "gx")
    n, cache = near_build(nx, ny, lists, v, s, t, factor, c)
    e, e_leaves, top, bottom, c, scale = middle(cols, levels, leaves, ny, c, y, upper_t, g, joint, r, n, valid)
    n, c = near_reuse(nx, ny, lists, edges(nx, ny, e_leaves, top, bottom, c), c, cache, cols)
    y, c = row_tree(True, exchange(c, "gy"), upper_t, g, b)
    x, out = final(cols, levels, leaves, exchange(c, "gx"), y, upper_t, g, b, joint, r, e, n, valid, scale)
    shape = (nx, ny, 4, size)
    return x.reshape(shape), out.reshape(shape)


def solution(mesh):
    return jax.shard_map(
        on_device,
        mesh=mesh,
        in_specs=(
            P("gx", "gy", None, None),
            P("gx", "gy", None, None),
            P("gx", "gy"),
            P("gx", "gy", None),
            P("gx", "gy", None, None),
            P("gx", "gy", None, None),
            P(),
            P(),
        ),
        out_specs=(P("gx", "gy", None, None), P("gx", "gy", None, None)),
        check_vma=False,
    )
```
